512 devices in a mesh: grp: 16 (over y_hi, x, core), seq: 32 (over y_lo, z).
Axes of the slice: x: 4, y: 4 (y_hi: 2, y_lo: 2; y = y_hi * 2 + y_lo), z: 16, core: 2. Of those that a mesh axis runs over, the one named last changes fastest.
Arguments:
- inputs: bfloat16 [16, 4096, 1024], P('grp', 'seq'), may hold values from -6 to 6
- q_heads: bfloat16 [16, 4096, 512], P('grp', 'seq'), may hold values from -5.2 to 5.2
- k_heads: bfloat16 [16, 4096, 512], P('grp', 'seq'), may hold values from -5.2 to 5.2
- v_heads: bfloat16 [16, 4096, 512], P('grp', 'seq'), may hold values from -6 to 6
- w_out: bfloat16 [512, 1024], replicated, may hold values from -0.25 to 0.25
- group_lens: int32 [16, 8], P('grp'), may hold values from 1 to 1024, 4096 in all within a row
- query_emb: bfloat16 [8192, 1024], P(('grp', 'seq')), may hold values from -6 to 6
- positive: int32 [8192], P(('grp', 'seq')), may hold values from 0 to 127
Outputs:
- mean_loss: float32 [], replicated
- grad_inputs: bfloat16 [16, 4096, 1024], P('grp', 'seq')
- grad_q: bfloat16 [16, 4096, 512], P('grp', 'seq')
- grad_k: bfloat16 [16, 4096, 512], P('grp', 'seq')
- grad_v: bfloat16 [16, 4096, 512], P('grp', 'seq')
- grad_w_out: float32 [512, 1024], replicated
The draws below stay inside these ranges and needn't reach their ends.
All inputs are finite; a program needn't handle non-finite values.
Results may differ from the reference program's by a relative error of at most 0.02.
Values may be sent and summed in bfloat16 or wider, within the bound.
No kernel may reach another device: no remote copies, remote signals or barrier semaphores. Data moves between devices by JAX's collectives and lax.ppermute only.
A program may use at most 64 MiB of HBM per device.

```python
import math
import jax
import jax.numpy as jnp
import numpy as np
from jax import lax

MODEL_DIM = 1024
HEAD_COUNT = 8
HEAD_DIM = 64
HEADS_WIDTH = 512
SEQ_LEN = 4096
DOCUMENTS = 16
GROUPS = 8
GROUP_MOST = 1024
ALL_GROUPS = 128
QUERIES = 8192


def draw_q_heads(key, part):
    key = jax.random.fold_in(key, 1)
    shape_full = (DOCUMENTS, SEQ_LEN, HEADS_WIDTH)
    values = jnp.clip(jax.random.normal(key, shape_full, jnp.float32), -5.2, 5.2)
    return values.astype(jnp.bfloat16)


def draw_k_heads(key, part):
    key = jax.random.fold_in(key, 2)
    shape_full = (DOCUMENTS, SEQ_LEN, HEADS_WIDTH)
    values = jnp.clip(jax.random.normal(key, shape_full, jnp.float32), -5.2, 5.2)
    return values.astype(jnp.bfloat16)


def plant(entries, own_key, smallest, largest):
    shape = entries.shape
    place = [jax.random.randint(jax.random.fold_in(own_key, axis), (), 0, shape[axis]) for axis in range(len(shape))]
    entries = entries.at[tuple(place)].set(smallest)
    longest = shape.index(max(shape))
    place[longest] = (place[longest] + 1) % shape[longest]
    return entries.at[tuple(place)].set(largest)


def block_levels(stream_key, dims, shards, least, largest):
    def one(dim, shards_of):
        draws = jax.random.uniform(jax.random.fold_in(jax.random.fold_in(stream_key, 6), dim), (shards_of,), jnp.float32, least / len(shards), largest / len(shards))
        return jnp.repeat(jnp.exp(draws), dims[dim] // shards_of).reshape((-1,) + (1,) * (len(dims) - dim - 1))

    gain = one(*shards[0])
    for cut in shards[1:]:
        gain = gain * one(*cut)
    return gain


def profile(amount, total, limit, lean):
    weights = [(1 << 20) // math.isqrt(grade ** lean) + 1 for grade in range(2, amount + 1)]
    rest, given = total - limit - (amount - 1), [1] * (amount - 1)
    while rest > 0:
        candidates = [i for i in range(amount - 1) if given[i] < limit]
        mass, remaining = sum([weights[i] for i in candidates]), rest
        for i in candidates:
            extra = min(limit - given[i], max(1, remaining * weights[i] // mass), rest)
            given[i] = given[i] + extra
            rest = rest - extra
    return np.array([limit] + given)


def ragged(stream_key, count, total, limit, slope):
    if count == 2:
        one = jax.random.randint(stream_key, (), max(1, total - limit), min(limit, total - 1) + 1)
        return jnp.stack([one, total - one])
    tallies = jnp.asarray(profile(count, total, limit, slope), jnp.int32)
    twos = (count - 1) // 2
    donor, sink = tallies[1:1 + 2 * twos:2], tallies[2:2 + 2 * twos:2]
    room = jnp.minimum(donor - 1, limit - sink)
    moved = jax.random.randint(jax.random.fold_in(stream_key, 1), (twos,), 0, 1 << 20) % (room + 1)
    tallies = tallies.at[1:1 + 2 * twos:2].set(donor - moved).at[2:2 + 2 * twos:2].set(sink + moved)
    return tallies[jax.random.permutation(jax.random.fold_in(stream_key, 2), count)]


def bell_draw(rng, extent, scale, most, split=(), kind=jnp.bfloat16):
    values = scale * jax.random.normal(rng, extent, jnp.float32)
    if split:
        values = values * block_levels(rng, extent, split, -0.22, 0.18)
    return jnp.clip(values, -most, most).astype(kind)


def setup_inputs(seed: int = 0) -> dict:
    splits = jax.random.split(jax.random.key(seed), 9)
    return {
        "inputs": bell_draw(splits[0], (DOCUMENTS, SEQ_LEN, MODEL_DIM), 1.0, 6.0, ((0, 16), (1, 32))),
        "q_heads": draw_q_heads(jax.random.fold_in(splits[8], 71), 0),
        "k_heads": draw_k_heads(jax.random.fold_in(splits[8], 71), 0),
        "v_heads": bell_draw(splits[3], (DOCUMENTS, SEQ_LEN, HEADS_WIDTH), 1.0, 6.0, ((0, 16), (1, 32))),
        "w_out": bell_draw(splits[4], (HEADS_WIDTH, MODEL_DIM), HEADS_WIDTH ** -0.5, 0.25),
        "group_lens": jax.vmap(lambda own: ragged(own, GROUPS, SEQ_LEN, GROUP_MOST, 2))(jax.random.split(splits[5], DOCUMENTS)).reshape((DOCUMENTS, GROUPS)).astype(jnp.int32),
        "query_emb": bell_draw(splits[6], (QUERIES, MODEL_DIM), 1.0, 6.0, ((0, 512),)),
        "positive": plant(jax.random.randint(splits[7], (QUERIES,), 0, ALL_GROUPS), jax.random.fold_in(splits[7], 1), 0, ALL_GROUPS - 1).astype(jnp.int32),
    }


RECIPROCAL_TEMP = 20.0
GRADIENT_FACTOR = 64.0
NORM_EPS = 1e-06
EXACT_MATMUL = lax.Precision.HIGHEST

def group_member(positions, lengths):
    group_ends = jnp.cumsum(lengths).astype(jnp.int32)
    starts = (group_ends - lengths).astype(jnp.int32)
    inside = (positions[:, None] >= starts[None, :]) & (positions[:, None] < group_ends[None, :])
    return inside.astype(jnp.float32)

def head_scores(query_rows, key_rows):
    return jnp.dot(query_rows, key_rows.T, preferred_element_type=jnp.float32) * HEAD_DIM ** (-0.5)

def head_forward(operand):
    query_rows, key_rows, value_rows = operand
    scores = head_scores(query_rows, key_rows)
    row_max = lax.optimization_barrier(jnp.max(scores, axis=1))
    log_total = row_max + jnp.log(lax.optimization_barrier(jnp.sum(jnp.exp(scores - row_max[:, None]), axis=1)))
    prob_bf16 = jnp.exp(scores - log_total[:, None]).astype(jnp.bfloat16)
    outputs = jnp.dot(prob_bf16, value_rows, preferred_element_type=jnp.float32).astype(jnp.bfloat16)
    return (outputs, log_total)

def head_backward(operand):
    query_rows, key_rows, value_rows, log_total, dattn, delta = operand
    prob_f32 = jnp.exp(head_scores(query_rows, key_rows) - log_total[:, None])
    prob_bf16 = prob_f32.astype(jnp.bfloat16)
    grad_values = jnp.dot(prob_bf16.T, dattn, preferred_element_type=jnp.float32)
    prob_grad = jnp.dot(dattn, value_rows.T, preferred_element_type=jnp.float32)
    score_grad = (prob_f32 * (prob_grad - delta[:, None])).astype(jnp.bfloat16)
    grad_queries = jnp.dot(score_grad, key_rows, preferred_element_type=jnp.float32) * HEAD_DIM ** (-0.5)
    grad_keys = jnp.dot(score_grad.T, query_rows, preferred_element_type=jnp.float32) * HEAD_DIM ** (-0.5)
    return (grad_queries.astype(jnp.bfloat16), grad_keys.astype(jnp.bfloat16), grad_values.astype(jnp.bfloat16))

def split_heads(array):
    return array.reshape(SEQ_LEN, HEAD_COUNT, HEAD_DIM).transpose(1, 0, 2)

def join_heads(array):
    return array.transpose(1, 0, 2).reshape(SEQ_LEN, HEAD_COUNT * HEAD_DIM)

def reference(inputs, q_heads, k_heads, v_heads, w_out, group_lens, query_emb, positive):

    def doc_forward(operand):
        outputs, log_total = lax.map(head_forward, tuple((split_heads(item) for item in operand)))
        return (join_heads(outputs), log_total)
    attention, log_total = lax.map(doc_forward, (q_heads, k_heads, v_heads))
    positions = jnp.arange(SEQ_LEN, dtype=jnp.int32)
    members = jax.vmap(lambda lengths: group_member(positions, lengths))(group_lens)
    length_f32 = group_lens.astype(jnp.float32)
    hidden = inputs.astype(jnp.float32) + jnp.einsum('bsk,kd->bsd', attention.astype(jnp.float32), w_out.astype(jnp.float32))
    pooled = jnp.einsum('bsc,bsd->bcd', members, hidden, precision=EXACT_MATMUL) / length_f32[:, :, None]
    pooled = pooled.reshape(ALL_GROUPS, MODEL_DIM)
    row_norms = jnp.sqrt(lax.optimization_barrier(jnp.sum(pooled * pooled, axis=1)) + NORM_EPS)
    group_embedding = pooled / row_norms[:, None]
    query_f32 = query_emb.astype(jnp.float32)
    query_normalized = query_f32 / jnp.sqrt(lax.optimization_barrier(jnp.sum(query_f32 * query_f32, axis=1)) + NORM_EPS)[:, None]
    similarity_logits = RECIPROCAL_TEMP * jnp.dot(query_normalized, group_embedding.T, precision=EXACT_MATMUL)
    exp_logits = jnp.exp(similarity_logits)
    totals = lax.optimization_barrier(jnp.sum(exp_logits, axis=1))
    target = (jnp.arange(ALL_GROUPS, dtype=jnp.int32)[None, :] == positive[:, None]).astype(jnp.float32)
    losses = jnp.log(totals) - lax.optimization_barrier(jnp.sum(target * similarity_logits, axis=1))
    mean_loss = jnp.mean(losses)
    softmax_weight = exp_logits / totals[:, None] - target
    embedding_gradient = GRADIENT_FACTOR * RECIPROCAL_TEMP * jnp.dot(softmax_weight.T, query_normalized, precision=EXACT_MATMUL)
    pooled_grad = (embedding_gradient - group_embedding * lax.optimization_barrier(jnp.sum(group_embedding * embedding_gradient, axis=1))[:, None]) / row_norms[:, None]
    group_grad = pooled_grad.reshape(DOCUMENTS, GROUPS, MODEL_DIM) / length_f32[:, :, None]
    grad_inputs = jnp.einsum('bsc,bcd->bsd', members, group_grad, precision=EXACT_MATMUL).astype(jnp.bfloat16)
    attn_sums = jnp.einsum('bsc,bsk->bck', members, attention.astype(jnp.float32), precision=EXACT_MATMUL)
    grad_w_out = jnp.einsum('bck,bcd->kd', attn_sums, group_grad, precision=EXACT_MATMUL)
    group_dattn = jnp.einsum('bcd,kd->bck', group_grad, w_out.astype(jnp.float32), precision=EXACT_MATMUL).astype(jnp.bfloat16)
    dattn = jnp.einsum('bsc,bck->bsk', members, group_dattn.astype(jnp.float32), precision=EXACT_MATMUL).astype(jnp.bfloat16)
    delta = lax.optimization_barrier(jnp.sum((dattn.astype(jnp.float32) * attention.astype(jnp.float32)).reshape(DOCUMENTS, SEQ_LEN, HEAD_COUNT, HEAD_DIM), axis=3))

    def doc_backward(operand):
        query_doc, key_doc, value_doc, total_doc, dattn_doc, delta_doc = operand
        grads = lax.map(head_backward, (split_heads(query_doc), split_heads(key_doc), split_heads(value_doc), total_doc, split_heads(dattn_doc), delta_doc.T))
        return tuple((join_heads(item) for item in grads))
    grad_q, grad_k, grad_v = lax.map(doc_backward, (q_heads, k_heads, v_heads, log_total, dattn, delta))
    return (mean_loss, grad_inputs, grad_q, grad_k, grad_v, grad_w_out)
```

```python
import functools

import jax
import jax.numpy as jnp
from jax import lax
from jax.experimental import pallas as pl
from jax.experimental.pallas import tpu as pltpu
from jax.sharding import Mesh, PartitionSpec as P

HEAD_COUNT = 8
HEAD_DIM = 64
GROUPS = 8
DOCS = 16
MODEL = 1024
WIDTH = 512
ROWS = 128
HALF = 64
QUARTER = 1024
PLANE = 16
SCALE = HEAD_DIM ** (-0.5)

RECIPROCAL_TEMP = 20.0
GRADIENT_FACTOR = 64.0
NORM_EPS = 1e-06
QUERY_COUNT = 8192
EXACT = lax.Precision.HIGHEST

BF16 = jnp.bfloat16
F32 = jnp.float32

GRP = ("yh", "xa", "xb", "co")
SEQ = ("yl", "za", "zb", "zc", "zd")
ZED = ("za", "zb", "zc", "zd")
SQUARE = ("yl", "zd")
NT = (((1,), (1,)), ((), ()))
TN = (((0,), (0,)), ((), ()))

VMEM_BYTES = 56 << 20


def params():
    return pltpu.CompilerParams(vmem_limit_bytes=VMEM_BYTES)


def cost(flops, moved, exps=0):
    return pl.CostEstimate(flops=int(flops), bytes_accessed=int(moved), transcendentals=int(exps))


def share(value, axes):
    count = 2 ** len(axes)
    return lax.all_to_all(
        jnp.broadcast_to(value[None], (count,) + value.shape), axes, split_axis=0, concat_axis=0
    )


def swap(value, axes, flip):
    count = 2 ** len(axes)
    return lax.ppermute(value, axes, [(i, i ^ flip) for i in range(count)])


def gather_grp(value):
    for axis in ("co", "xb", "xa", "yh"):
        other = swap(value, (axis,), 1)
        first = lax.axis_index(axis) == 0
        value = jnp.where(
            first,
            jnp.concatenate([value, other], axis=0),
            jnp.concatenate([other, value], axis=0),
        )
    return value


def three(value):
    high = value.astype(BF16)
    rest = value - high.astype(F32)
    middle = rest.astype(BF16)
    low = (rest - middle.astype(F32)).astype(BF16)
    return high, middle, low


def stacked(value):
    parts = [part.astype(F32) for part in three(value)]
    parts.append(jnp.zeros_like(value))
    return jnp.concatenate(parts, axis=0).astype(BF16)


def folded(product):
    return (product[16:24] + product[8:16]) + product[0:8]


def quarter_member(bounds_ref, plane, half):
    row = lax.broadcasted_iota(jnp.int32, (GROUPS, QUARTER), 1)
    position = plane * (PLANE * ROWS) + (row >> 6) * ROWS + half * HALF + (row & 63)
    inside = (position >= bounds_ref[0, :, 0:1]) & (position < bounds_ref[1, :, 0:1])
    return inside.astype(F32)


def local_member(bounds_ref, first):
    position = first + lax.broadcasted_iota(jnp.int32, (GROUPS, ROWS), 1)
    inside = (position >= bounds_ref[0, :, 0:1]) & (position < bounds_ref[1, :, 0:1])
    return inside.astype(F32)


def halves(packed):
    return jnp.concatenate([packed[:, :, 0:64], packed[:, :, 64:128]], axis=1)


def lanes(rows):
    return lax.broadcasted_iota(jnp.int32, (rows, 128), 1)


def pack_kernel(place_ref, q_ref, k_ref, v_ref, inputs_ref, bounds_ref, out_ref):
    mine = local_member(bounds_ref, place_ref[3]).astype(BF16)
    sums = jnp.dot(mine, inputs_ref[...], preferred_element_type=F32)
    high, middle, low = [part.astype(F32) for part in three(sums)]
    zero = jnp.zeros((GROUPS, HALF), F32)
    for head in range(HEAD_COUNT):
        cols = slice(head * HEAD_DIM, (head + 1) * HEAD_DIM)
        for half in range(2):
            rows = slice(half * HALF, (half + 1) * HALF)
            place = 2 * head + half
            out_ref[place, 0:64, :] = jnp.concatenate([k_ref[rows, cols], v_ref[rows, cols]], axis=1)
            query = q_ref[rows, cols] * jnp.asarray(SCALE, BF16)
            out_ref[place, 64:96, :] = jnp.concatenate([query[0:32], query[32:64]], axis=1)
            part = slice(place * HALF, (place + 1) * HALF)
            upper = jnp.concatenate([high[:, part], middle[:, part]], axis=1)
            lower = jnp.concatenate([low[:, part], zero], axis=1)
            out_ref[place, 96:112, :] = jnp.concatenate([upper, lower], axis=0).astype(BF16)


def unpack_kernel(in_ref, q_ref, k_ref, v_ref):
    for pair in range(HEAD_COUNT // 2):
        cols = slice(pair * 128, (pair + 1) * 128)
        for half in range(2):
            one, two = 4 * pair + half, 4 * pair + 2 + half
            rows = slice(half * HALF, (half + 1) * HALF)
            first, second = in_ref[one, 0:64, :], in_ref[two, 0:64, :]
            k_ref[rows, cols] = jnp.concatenate([first[:, 0:64], second[:, 0:64]], axis=1)
            v_ref[rows, cols] = jnp.concatenate([first[:, 64:128], second[:, 64:128]], axis=1)
            first, second = in_ref[one, 64:96, :], in_ref[two, 64:96, :]
            early = jnp.concatenate([first[:, 0:64], second[:, 0:64]], axis=1)
            late = jnp.concatenate([first[:, 64:128], second[:, 64:128]], axis=1)
            q_ref[rows, cols] = jnp.concatenate([early, late], axis=0)


BLOCK = 256
PARTS = BLOCK // 128


def forward_kernel(
    place_ref, own_ref, x_ref, bounds_ref, length_ref, y_ref, lse_ref, means_ref, q_s
):
    queries = halves(own_ref[:, 64:96, :]).reshape(QUARTER, HEAD_DIM)
    q_s[...] = jnp.concatenate([queries, jnp.zeros_like(queries)], axis=1)

    def block(i, carry):
        rows = pl.ds(pl.multiple_of(i * BLOCK, BLOCK), BLOCK)
        scores = lax.dot_general(q_s[rows, :], x_ref[...], NT, preferred_element_type=F32)
        top = jnp.max(scores, axis=1, keepdims=True)
        grown = jnp.exp(scores - top)
        total = jnp.sum(grown, axis=1, keepdims=True)
        prob = (grown * (1.0 / total)).astype(BF16)
        mixed = jnp.dot(prob, x_ref[...], preferred_element_type=F32).astype(BF16)
        y_ref[rows, :] = jnp.where(lanes(BLOCK) < 64, q_s[rows, :], mixed)
        log_total = top + jnp.log(total)
        for part in range(PARTS):
            square = jnp.broadcast_to(log_total[part * 128 : (part + 1) * 128], (128, 128))
            lse_ref[pl.ds(i * PARTS + part, 1), :] = jnp.transpose(square)[0:1, :]
        return carry

    lax.fori_loop(0, QUARTER // BLOCK, block, 0)
    y_ref[QUARTER : QUARTER + 32, :] = stacked(lse_ref[...])
    member = quarter_member(bounds_ref, place_ref[0], place_ref[1]).astype(BF16)
    attn_sums = jnp.dot(member, y_ref[0:QUARTER, :], preferred_element_type=F32)
    sums = jnp.sum(own_ref[:, 96:112, :].astype(F32), axis=0)
    input_sums = (sums[0:8] + pltpu.roll(sums[0:8], 64, 1)) + sums[8:16]
    means = jnp.where(lanes(GROUPS) < 64, input_sums, attn_sums) / length_ref[...]
    means_ref[...] = jnp.broadcast_to(means[None], (2 * PLANE, GROUPS, 128))


def pool_kernel(means_ref, w_ref, pooled_ref, means_out_ref):
    columns, heads = [], []
    for z in range(PLANE):
        both = means_ref[z] + means_ref[PLANE + z]
        columns.append(both[:, 0:64])
        if z % 2 == 0:
            heads.append(both[:, 64:128])
        else:
            heads[-1] = heads[-1] + both[:, 64:128]
    means = jnp.concatenate(heads, axis=1)
    projected = jnp.dot(stacked(means), w_ref[...], preferred_element_type=F32)
    pooled = jnp.concatenate(columns, axis=1) + folded(projected)
    pooled_ref[...] = jnp.broadcast_to(pooled[None], (DOCS, GROUPS, MODEL))
    means_out_ref[...] = means


def query_kernel(query_ref, out_ref):
    query = query_ref[:, :MODEL].astype(F32)
    squares = lax.dot_general(
        jnp.ones((8, MODEL), F32), query * query, NT, precision=EXACT, preferred_element_type=F32
    )
    out_ref[0:8, :] = jnp.sqrt(squares + NORM_EPS)
    out_ref[8:16, :] = lax.dot_general(
        jnp.ones((8, 128), BF16), query_ref[:, MODEL:], NT, preferred_element_type=F32
    )


def loss_kernel(doc_ref, pooled_ref, query_ref, row_ref, w_ref, out_ref, weight_s):
    pooled = pooled_ref[...]
    norms = jnp.sqrt(jnp.sum(pooled * pooled, axis=1, keepdims=True) + NORM_EPS)
    unit = pooled / norms
    query = query_ref[:, :MODEL]
    scale = RECIPROCAL_TEMP / row_ref[0:1, :]
    logits = jnp.zeros((DOCS * GROUPS, 256), F32)
    for part in three(unit)[::-1]:
        logits = logits + lax.dot_general(part, query, NT, preferred_element_type=F32)
    logits = logits * scale
    grown = jnp.exp(logits)
    total = jnp.sum(grown, axis=0, keepdims=True)
    group = lax.broadcasted_iota(jnp.int32, logits.shape, 0)
    target = (group == row_ref[8:9, :].astype(jnp.int32)).astype(F32)
    losses = jnp.log(total) - jnp.sum(target * logits, axis=0, keepdims=True)
    loss = jnp.sum(losses, axis=1, keepdims=True)
    weight_s[...] = (grown / total - target) * (GRADIENT_FACTOR * scale)
    mine = pl.ds(pl.multiple_of(doc_ref[0] * GROUPS, GROUPS), GROUPS)
    grad = folded(jnp.dot(stacked(weight_s[mine, :]), query, preferred_element_type=F32))
    own = pooled_ref[mine, :]
    own_unit = own / jnp.sqrt(jnp.sum(own * own, axis=1, keepdims=True) + NORM_EPS)
    along = jnp.sum(own_unit * grad, axis=1, keepdims=True)
    spread = folded(
        lax.dot_general(stacked(grad), w_ref[...], NT, preferred_element_type=F32)
    )
    extra = jnp.where(lanes(GROUPS) < 64, along, loss)
    for z in range(PLANE):
        head = z // 2
        chunk = jnp.concatenate(
            [
                spread[:, head * HEAD_DIM : (head + 1) * HEAD_DIM],
                grad[:, z * HALF : (z + 1) * HALF],
            ],
            axis=1,
        )
        for plane in range(2):
            out_ref[plane * PLANE + z, 0:8, :] = chunk
            out_ref[plane * PLANE + z, 8:16, :] = extra


def group_kernel(place_ref, terms_ref, pooled_ref, w_ref, length_ref, dattn_ref, grad_ref, loss_ref):
    head = place_ref[2]
    z = 2 * head + place_ref[1]
    sums = terms_ref[0]
    for n in range(1, 2 * PLANE):
        sums = sums + terms_ref[n]
    along = sums[8:16, 0:1]
    loss_ref[...] = sums[8:16, :] / QUERY_COUNT
    pooled = pooled_ref[...]
    norms = jnp.sqrt(jnp.sum(pooled * pooled, axis=1, keepdims=True) + NORM_EPS)
    unit = pooled / norms
    w_head = w_ref[pl.ds(pl.multiple_of(head * HEAD_DIM, HEAD_DIM), HEAD_DIM), :]
    w_twice = jnp.concatenate([w_head, w_head], axis=0)
    shade = folded(lax.dot_general(stacked(unit), w_twice, NT, preferred_element_type=F32))
    raw = jnp.concatenate([sums[0:8, 0:64], sums[0:8, 0:64]], axis=1)
    dattn_ref[...] = (raw - shade * along) / norms / length_ref[...]
    part = jnp.zeros((GROUPS, HALF), F32)
    for n in range(PLANE):
        part = jnp.where(z == n, unit[:, n * HALF : (n + 1) * HALF], part)
    grad = (sums[0:8, 64:128] - part * along) / norms
    wide = jnp.concatenate([grad, grad], axis=1)
    grad_ref[...] = jnp.broadcast_to(wide[None], (PLANE, GROUPS, 128))


def inputs_kernel(place_ref, parts_ref, means_ref, bounds_ref, length_ref, grad_inputs_ref, out_ref):
    grad = jnp.concatenate([parts_ref[z][:, 0:64] for z in range(PLANE)], axis=1)
    mine = local_member(bounds_ref, place_ref[3])
    members = jnp.concatenate([mine, mine, mine, mine], axis=0).astype(BF16)
    grad_inputs_ref[...] = lax.dot_general(
        members, stacked(grad / length_ref[:, 0:1]), TN, preferred_element_type=F32
    ).astype(BF16)
    both = jnp.concatenate([grad, means_ref[...]], axis=1)
    out_ref[...] = jnp.broadcast_to(both[None], (DOCS, GROUPS, MODEL + WIDTH))


def weight_kernel(in_ref, out_ref):
    grads = three(in_ref[:, :MODEL])
    means = three(in_ref[:, MODEL:])
    out_ref[...] = lax.dot_general(
        jnp.concatenate([means[1], means[0], means[0]], axis=0),
        jnp.concatenate([grads[0], grads[1], grads[0]], axis=0),
        TN,
        preferred_element_type=F32,
    )


def row_kernel(place_ref, y_ref, lse_ref, x_ref, dattn_ref, bounds_ref, out_ref, q_s, d_s, delta_s):
    lane = lanes(QUARTER)
    member = quarter_member(bounds_ref, place_ref[0], place_ref[1]).astype(BF16)
    spread = lax.dot_general(
        member, dattn_ref[...].astype(BF16), TN, preferred_element_type=F32
    )
    spread = jnp.where(lane < 64, 0.0, spread)
    mine = y_ref[0:QUARTER, :]
    q_s[...] = jnp.where(lane < 64, mine, jnp.zeros_like(mine))
    d_s[...] = spread.astype(BF16)
    delta_s[...] = jnp.broadcast_to(
        jnp.sum(spread * mine.astype(F32), axis=1, keepdims=True), (QUARTER, 128)
    )

    def block(i, carry):
        rows = pl.ds(pl.multiple_of(i * BLOCK, BLOCK), BLOCK)
        columns = []
        for part in range(PARTS):
            line = lse_ref[pl.ds(i * PARTS + part, 1), :]
            columns.append(jnp.transpose(jnp.broadcast_to(line, (128, 128))))
        log_total = jnp.concatenate(columns, axis=0)[:, 0:1]
        scores = lax.dot_general(q_s[rows, :], x_ref[...], NT, preferred_element_type=F32)
        prob = jnp.exp(scores - log_total)
        prob_grad = lax.dot_general(d_s[rows, :], x_ref[...], NT, preferred_element_type=F32)
        score_grad = (prob * (prob_grad - delta_s[rows, 0:1])).astype(BF16)
        for_query = jnp.dot(score_grad, x_ref[...], preferred_element_type=F32) * SCALE
        count = BLOCK // HALF
        value = for_query[:, 0:64].astype(BF16).reshape(count, HALF, HEAD_DIM)
        out_ref[pl.ds(i * count, count), :, :] = jnp.concatenate(
            [value[:, 0:32], value[:, 32:64]], axis=2
        )
        return carry

    lax.fori_loop(0, QUARTER // BLOCK, block, 0)


def column_kernel(own_ref, y_ref, dattn_ref, bounds_ref, grad_q_ref, out_ref, y_s, k_s, v_s, delta_s, lse_s):
    lane = lanes(QUARTER)
    mine = own_ref[:, 0:64, :].reshape(QUARTER, 128)
    zero = jnp.zeros_like(mine)
    k_s[...] = jnp.where(lane < 64, mine, zero)
    v_s[...] = jnp.where(lane < 64, zero, mine)
    dattn = dattn_ref[...].astype(BF16)
    ones = jnp.ones((8, 128), F32)
    for n in range(4):
        rows = slice(n * QUARTER, (n + 1) * QUARTER)
        member = quarter_member(bounds_ref, n // 2, n % 2).astype(BF16)
        spread = lax.dot_general(member, dattn, TN, preferred_element_type=F32)
        spread = jnp.where(lane < 64, 0.0, spread)
        other = y_ref[n, 0:QUARTER, :]
        y_s[rows, :] = jnp.where(lane < 64, other, spread.astype(BF16))
        delta_s[:, rows] = lax.dot_general(
            ones, spread * other.astype(F32), NT, precision=EXACT, preferred_element_type=F32
        )
        lse = y_ref[n, QUARTER : QUARTER + 32, :].astype(F32)
        lse = (lse[16:24] + lse[8:16]) + lse[0:8]
        for part in range(8):
            lse_s[:, n * QUARTER + part * 128 : n * QUARTER + (part + 1) * 128] = jnp.broadcast_to(
                lse[part : part + 1, :], (8, 128)
            )

    def block(i, carry):
        rows = pl.ds(pl.multiple_of(i * BLOCK, BLOCK), BLOCK)
        scores = lax.dot_general(k_s[rows, :], y_s[...], NT, preferred_element_type=F32)
        prob = jnp.exp(scores - lse_s[0:1, :])
        prob_grad = lax.dot_general(v_s[rows, :], y_s[...], NT, preferred_element_type=F32)
        score_grad = (prob * (prob_grad - delta_s[0:1, :])).astype(BF16)
        for_key = jnp.dot(score_grad, y_s[...], preferred_element_type=F32)
        for_value = jnp.dot(prob.astype(BF16), y_s[...], preferred_element_type=F32)
        both = jnp.where(lanes(BLOCK) < 64, for_key, for_value).astype(BF16)
        count = BLOCK // HALF
        out_ref[pl.ds(i * count, count), 0:64, :] = both.reshape(count, HALF, 128)
        return carry

    lax.fori_loop(0, QUARTER // BLOCK, block, 0)
    out_ref[:, 64:96, :] = grad_q_ref[...]


SMEM = pl.BlockSpec(memory_space=pltpu.SMEM)
VMEM = pl.BlockSpec(memory_space=pltpu.VMEM)


def call(kernel, outs, scalars, arrays, scratch, estimate, name):
    return pl.pallas_call(
        kernel,
        out_shape=outs,
        in_specs=[SMEM] * len(scalars) + [VMEM] * len(arrays),
        out_specs=jax.tree.map(lambda _: VMEM, outs),
        scratch_shapes=scratch,
        compiler_params=params(),
        cost_estimate=estimate,
        name=name,
    )(*scalars, *arrays)


def shape(dims, dtype):
    return jax.ShapeDtypeStruct(dims, dtype)


def body(inputs, q_heads, k_heads, v_heads, w_out, group_lens, query_emb, positive):
    plane = lax.axis_index("yl")
    half = lax.axis_index("zd")
    head = lax.axis_index(("za", "zb", "zc"))
    first = lax.axis_index(SEQ) * ROWS
    doc = lax.axis_index(GRP).reshape(1).astype(jnp.int32)
    place = jnp.stack([plane, half, head, first]).astype(jnp.int32)
    lengths = group_lens[0]
    ends = jnp.cumsum(lengths)
    bounds = jnp.broadcast_to(jnp.stack([ends - lengths, ends])[:, :, None], (2, GROUPS, 128))
    length = jnp.broadcast_to(lengths.astype(F32)[:, None], (GROUPS, 128))

    packed = call(
        pack_kernel, shape((PLANE, 112, 128), BF16), (place,),
        (q_heads[0], k_heads[0], v_heads[0], inputs[0], bounds), (), cost(0, 1000000), "pack",
    )
    own = lax.all_to_all(packed, ZED, split_axis=0, concat_axis=0)
    keys = share(own[:, 0:64, :], SQUARE).reshape(4 * QUARTER, 128)

    tagged = jnp.concatenate(
        [query_emb, jnp.pad(positive.astype(BF16)[:, None], ((0, 0), (0, 127)))], axis=1
    )
    queries = gather_grp(tagged)
    query_rows = call(
        query_kernel, shape((16, 256), F32), (), (queries,), (), cost(6 * 2 * 8 * 256 * 1024, 600000),
        "queries",
    )

    pairs = QUARTER * 4 * QUARTER
    mine, lse, means = call(
        forward_kernel,
        (
            shape((QUARTER + 32, 128), BF16),
            shape((8, 128), F32),
            shape((2 * PLANE, GROUPS, 128), F32),
        ),
        (place,), (own, keys, bounds, length), [pltpu.VMEM((QUARTER, 128), BF16)],
        cost(pairs * 256 * 4, 3000000, pairs), "forward",
    )
    means = lax.all_to_all(means, SEQ, split_axis=0, concat_axis=0)
    others = share(mine, SQUARE)

    pooled, doc_means = call(
        pool_kernel,
        (shape((DOCS, GROUPS, MODEL), F32), shape((GROUPS, WIDTH), F32)),
        (), (means, w_out), (), cost(2 * 32 * 512 * 1024, 1200000), "pool",
    )
    pooled_own = pooled[0]
    pooled_all = lax.all_to_all(pooled, GRP, split_axis=0, concat_axis=0)
    pooled_all = pooled_all.reshape(DOCS * GROUPS, MODEL)
    pooled_all, others = lax.optimization_barrier((pooled_all, others))
    terms = call(
        loss_kernel, shape((2 * PLANE, 16, 128), F32), (doc,),
        (pooled_all, queries, query_rows, w_out), [pltpu.VMEM((DOCS * GROUPS, 256), F32)],
        cost(3 * 2 * 128 * 256 * 1024, 2500000, 40000), "loss",
    )
    terms = lax.all_to_all(terms, SEQ, split_axis=0, concat_axis=0)

    dattn, grad_part, loss = call(
        group_kernel,
        (
            shape((GROUPS, 128), F32),
            shape((PLANE, GROUPS, 128), F32),
            shape((GROUPS, 128), F32),
        ),
        (place,), (terms, pooled_own, w_out, length),
        (), cost(2 * 32 * 128 * 1024, 1500000), "group",
    )
    mean_loss = loss[0, 64]
    grad_parts = lax.all_to_all(grad_part, ZED, split_axis=0, concat_axis=0)
    grad_rows = call(
        row_kernel, shape((PLANE, 32, 128), BF16), (place,),
        (mine, lse, keys, dattn, bounds),
        [
            pltpu.VMEM((QUARTER, 128), BF16),
            pltpu.VMEM((QUARTER, 128), BF16),
            pltpu.VMEM((QUARTER, 128), F32),
        ],
        cost(pairs * 256 * 6, 2000000, pairs), "rows",
    )
    grad_inputs, grads = call(
        inputs_kernel,
        (shape((ROWS, MODEL), BF16), shape((DOCS, GROUPS, MODEL + WIDTH), F32)),
        (place,), (grad_parts, doc_means, bounds, length), (), cost(2 * 32 * 128 * 1024, 1200000),
        "inputs",
    )
    grad_rows, grads = lax.optimization_barrier((grad_rows, grads))
    all_grads = lax.all_to_all(grads, GRP, split_axis=0, concat_axis=0)
    packed_grads = call(
        column_kernel, shape((PLANE, 96, 128), BF16), (), (own, others, dattn, bounds, grad_rows),
        [
            pltpu.VMEM((4 * QUARTER, 128), BF16),
            pltpu.VMEM((QUARTER, 128), BF16),
            pltpu.VMEM((QUARTER, 128), BF16),
            pltpu.VMEM((8, 4 * QUARTER), F32),
            pltpu.VMEM((8, 4 * QUARTER), F32),
        ],
        cost(pairs * 256 * 8, 2500000, pairs), "columns",
    )
    home = lax.all_to_all(packed_grads, ZED, split_axis=0, concat_axis=0)
    out = shape((ROWS, WIDTH), BF16)
    grad_q, grad_k, grad_v = call(
        unpack_kernel, (out, out, out), (), (home,), (), cost(0, 800000), "unpack"
    )
    grad_w_out = call(
        weight_kernel, shape((WIDTH, MODEL), F32), (),
        (all_grads.reshape(DOCS * GROUPS, MODEL + WIDTH),), (),
        cost(2 * 384 * 512 * 1024, 3000000), "weights",
    )
    return (mean_loss, grad_inputs[None], grad_q[None], grad_k[None], grad_v[None], grad_w_out)


def solution(mesh):
    fine = Mesh(mesh.devices.reshape((2,) * 9), GRP + SEQ)
    rows = P(GRP, SEQ, None)
    return jax.shard_map(
        body,
        mesh=fine,
        in_specs=(
            rows,
            rows,
            rows,
            rows,
            P(),
            P(GRP, None),
            P(GRP + SEQ, None),
            P(GRP + SEQ),
        ),
        out_specs=(P(), rows, rows, rows, rows, P()),
        check_vma=False,
    )
```

```python
import functools

import jax
import jax.numpy as jnp
from jax import lax
from jax.experimental import pallas as pl
from jax.experimental.pallas import tpu as pltpu
from jax.sharding import Mesh, PartitionSpec as P

HEAD_COUNT = 8
HEAD_DIM = 64
GROUPS = 8
DOCS = 16
MODEL = 1024
WIDTH = 512
ROWS = 128
HALF = 64
QUARTER = 1024
PLANE = 16
SCALE = HEAD_DIM ** (-0.5)

RECIPROCAL_TEMP = 20.0
GRADIENT_FACTOR = 64.0
NORM_EPS = 1e-06
QUERY_COUNT = 8192
EXACT = lax.Precision.HIGHEST

BF16 = jnp.bfloat16
F32 = jnp.float32

GRP = ("yh", "xa", "xb", "co")
SEQ = ("yl", "za", "zb", "zc", "zd")
ZED = ("za", "zb", "zc", "zd")
SQUARE = ("yl", "zd")
HEADS = ("za", "zb", "zc")
NT = (((1,), (1,)), ((), ()))
TN = (((0,), (0,)), ((), ()))

VMEM_BYTES = 56 << 20


def params():
    return pltpu.CompilerParams(vmem_limit_bytes=VMEM_BYTES)


def cost(flops, moved, exps=0):
    return pl.CostEstimate(flops=int(flops), bytes_accessed=int(moved), transcendentals=int(exps))


def share(value, axes):
    count = 2 ** len(axes)
    return lax.all_to_all(
        jnp.broadcast_to(value[None], (count,) + value.shape), axes, split_axis=0, concat_axis=0
    )


def swap(value, axes, flip):
    count = 2 ** len(axes)
    return lax.ppermute(value, axes, [(i, i ^ flip) for i in range(count)])


def gather_grp(value):
    for axis in ("co", "xb", "xa", "yh"):
        other = swap(value, (axis,), 1)
        first = lax.axis_index(axis) == 0
        value = jnp.where(
            first,
            jnp.concatenate([value, other], axis=0),
            jnp.concatenate([other, value], axis=0),
        )
    return value


def three(value):
    high = value.astype(BF16)
    rest = value - high.astype(F32)
    middle = rest.astype(BF16)
    low = (rest - middle.astype(F32)).astype(BF16)
    return high, middle, low


def stacked(value):
    parts = [part.astype(F32) for part in three(value)]
    parts.append(jnp.zeros_like(value))
    return jnp.concatenate(parts, axis=0).astype(BF16)


def folded(product):
    return (product[16:24] + product[8:16]) + product[0:8]


def column_of(values):
    row = lax.broadcasted_iota(jnp.int32, (GROUPS, 128), 0)
    out = jnp.full((GROUPS, 128), values[0])
    for n in range(1, GROUPS):
        out = jnp.where(row == n, values[n], out)
    return out


def member_of(position, lens_ref):
    ends = [lens_ref[0]]
    for n in range(1, GROUPS):
        ends.append(ends[-1] + lens_ref[n])
    last = column_of(ends)
    first = last - column_of([lens_ref[n] for n in range(GROUPS)])
    return ((position >= first[:, 0:1]) & (position < last[:, 0:1])).astype(F32)


def lengths_of(lens_ref):
    return column_of([lens_ref[n] for n in range(GROUPS)]).astype(F32)


def quarter_member(lens_ref, plane, half):
    row = lax.broadcasted_iota(jnp.int32, (GROUPS, QUARTER), 1)
    position = plane * (PLANE * ROWS) + (row >> 6) * ROWS + half * HALF + (row & 63)
    return member_of(position, lens_ref)


def local_member(lens_ref, first):
    return member_of(first + lax.broadcasted_iota(jnp.int32, (GROUPS, ROWS), 1), lens_ref)


def halves(packed):
    return jnp.concatenate([packed[:, :, 0:64], packed[:, :, 64:128]], axis=1)


def lanes(rows):
    return lax.broadcasted_iota(jnp.int32, (rows, 128), 1)


def pack_kernel(place_ref, lens_ref, q_ref, k_ref, v_ref, inputs_ref, out_ref):
    mine = local_member(lens_ref, place_ref[3]).astype(BF16)
    sums = jnp.dot(mine, inputs_ref[...], preferred_element_type=F32)
    high, middle, low = [part.astype(F32) for part in three(sums)]
    zero = jnp.zeros((GROUPS, HALF), F32)
    for head in range(HEAD_COUNT):
        cols = slice(head * HEAD_DIM, (head + 1) * HEAD_DIM)
        for half in range(2):
            rows = slice(half * HALF, (half + 1) * HALF)
            place = 2 * head + half
            out_ref[place, 0:64, :] = jnp.concatenate([k_ref[rows, cols], v_ref[rows, cols]], axis=1)
            query = q_ref[rows, cols] * jnp.asarray(SCALE, BF16)
            out_ref[place, 64:96, :] = jnp.concatenate([query[0:32], query[32:64]], axis=1)
            part = slice(place * HALF, (place + 1) * HALF)
            upper = jnp.concatenate([high[:, part], middle[:, part]], axis=1)
            lower = jnp.concatenate([low[:, part], zero], axis=1)
            out_ref[place, 96:112, :] = jnp.concatenate([upper, lower], axis=0).astype(BF16)


def unpack_pair_kernel(in_ref, k_ref, v_ref):
    for pair in range(HEAD_COUNT // 2):
        cols = slice(pair * 128, (pair + 1) * 128)
        for half in range(2):
            rows = slice(half * HALF, (half + 1) * HALF)
            first, second = in_ref[4 * pair + half], in_ref[4 * pair + 2 + half]
            k_ref[rows, cols] = jnp.concatenate([first[:, 0:64], second[:, 0:64]], axis=1)
            v_ref[rows, cols] = jnp.concatenate([first[:, 64:128], second[:, 64:128]], axis=1)


def unpack_query_kernel(in_ref, q_ref):
    for pair in range(HEAD_COUNT // 2):
        cols = slice(pair * 128, (pair + 1) * 128)
        for half in range(2):
            rows = slice(half * HALF, (half + 1) * HALF)
            first, second = in_ref[4 * pair + half], in_ref[4 * pair + 2 + half]
            early = jnp.concatenate([first[:, 0:64], second[:, 0:64]], axis=1)
            late = jnp.concatenate([first[:, 64:128], second[:, 64:128]], axis=1)
            q_ref[rows, cols] = jnp.concatenate([early, late], axis=0)


BLOCK = 256
PARTS = BLOCK // 128


def forward_kernel(
    place_ref, lens_ref, own_ref, x_ref, out_ref, lse_ref, means_ref, y_ref, q_s
):
    queries = halves(own_ref[:, 64:96, :]).reshape(QUARTER, HEAD_DIM)
    q_s[...] = jnp.concatenate([queries, jnp.zeros_like(queries)], axis=1)

    def block(i, carry):
        rows = pl.ds(pl.multiple_of(i * BLOCK, BLOCK), BLOCK)
        scores = lax.dot_general(q_s[rows, :], x_ref[...], NT, preferred_element_type=F32)
        top = jnp.max(scores, axis=1, keepdims=True)
        grown = jnp.exp(scores - top)
        total = jnp.sum(grown, axis=1, keepdims=True)
        prob = (grown * (1.0 / total)).astype(BF16)
        mixed = jnp.dot(prob, x_ref[...], preferred_element_type=F32).astype(BF16)
        y_ref[rows, :] = jnp.where(lanes(BLOCK) < 64, q_s[rows, :], mixed)
        log_total = top + jnp.log(total)
        for part in range(PARTS):
            square = jnp.broadcast_to(log_total[part * 128 : (part + 1) * 128], (128, 128))
            lse_ref[pl.ds(i * PARTS + part, 1), :] = jnp.transpose(square)[0:1, :]
        return carry

    lax.fori_loop(0, QUARTER // BLOCK, block, 0)
    y_ref[QUARTER : QUARTER + 32, :] = stacked(lse_ref[...])
    out_ref[...] = jnp.broadcast_to(y_ref[...][None], (4, QUARTER + 32, 128))
    member = quarter_member(lens_ref, place_ref[0], place_ref[1]).astype(BF16)
    attn_sums = jnp.dot(member, y_ref[0:QUARTER, :], preferred_element_type=F32)
    sums = jnp.sum(own_ref[:, 96:112, :].astype(F32), axis=0)
    input_sums = (sums[0:8] + pltpu.roll(sums[0:8], 64, 1)) + sums[8:16]
    means = jnp.where(lanes(GROUPS) < 64, input_sums, attn_sums) / lengths_of(lens_ref)
    means_ref[...] = jnp.broadcast_to(means[None], (4, GROUPS, 128))


def square_kernel(means_ref, out_ref):
    means = [means_ref[n] for n in range(4)]
    sums = jnp.concatenate(
        [(means[0] + means[2])[:, 0:64], (means[1] + means[3])[:, 0:64]], axis=1
    )
    attn = (means[0] + means[1]) + (means[2] + means[3])
    both = jnp.concatenate([sums, attn], axis=0)
    out_ref[...] = jnp.broadcast_to(both[None], (HEAD_COUNT, 16, 128))


def pool_kernel(means_ref, w_ref, pooled_ref, own_ref, means_out_ref):
    columns = [means_ref[h, 0:8, :] for h in range(HEAD_COUNT)]
    means = jnp.concatenate([means_ref[h, 8:16, 64:128] for h in range(HEAD_COUNT)], axis=1)
    projected = jnp.dot(stacked(means), w_ref[...], preferred_element_type=F32)
    pooled = jnp.concatenate(columns, axis=1) + folded(projected)
    pooled_ref[...] = jnp.broadcast_to(pooled[None], (DOCS, GROUPS, MODEL))
    own_ref[...] = pooled
    means_out_ref[...] = means


def prepare_kernel(place_ref, pooled_ref, w_ref, out_ref):
    head = place_ref[2]
    pooled = pooled_ref[...]
    norms = jnp.sqrt(jnp.sum(pooled * pooled, axis=1, keepdims=True) + NORM_EPS)
    unit = pooled / norms
    w_head = w_ref[pl.ds(pl.multiple_of(head * HEAD_DIM, HEAD_DIM), HEAD_DIM), :]
    w_twice = jnp.concatenate([w_head, w_head], axis=0)
    out_ref[0:8, :] = folded(
        lax.dot_general(stacked(unit), w_twice, NT, preferred_element_type=F32)
    )
    part = unit[:, 0:128]
    for n in range(1, HEAD_COUNT):
        part = jnp.where(head == n, unit[:, n * 128 : (n + 1) * 128], part)
    out_ref[8:16, :] = part
    out_ref[16:24, :] = jnp.broadcast_to(norms, (GROUPS, 128))


def query_kernel(query_ref, out_ref):
    query = query_ref[:, :MODEL].astype(F32)
    squares = lax.dot_general(
        jnp.ones((8, MODEL), F32), query * query, NT, precision=EXACT, preferred_element_type=F32
    )
    out_ref[0:8, :] = jnp.sqrt(squares + NORM_EPS)
    out_ref[8:16, :] = lax.dot_general(
        jnp.ones((8, 128), BF16), query_ref[:, MODEL:], NT, preferred_element_type=F32
    )


def loss_kernel(doc_ref, pooled_ref, query_ref, row_ref, w_ref, out_ref, weight_s):
    pooled = pooled_ref[...]
    norms = jnp.sqrt(jnp.sum(pooled * pooled, axis=1, keepdims=True) + NORM_EPS)
    unit = pooled / norms
    query = query_ref[:, :MODEL]
    scale = RECIPROCAL_TEMP / row_ref[0:1, :]
    logits = jnp.zeros((DOCS * GROUPS, 256), F32)
    for part in three(unit)[::-1]:
        logits = logits + lax.dot_general(part, query, NT, preferred_element_type=F32)
    logits = logits * scale
    grown = jnp.exp(logits)
    total = jnp.sum(grown, axis=0, keepdims=True)
    group = lax.broadcasted_iota(jnp.int32, logits.shape, 0)
    target = (group == row_ref[8:9, :].astype(jnp.int32)).astype(F32)
    losses = jnp.log(total) - jnp.sum(target * logits, axis=0, keepdims=True)
    loss = jnp.sum(losses, axis=1, keepdims=True)
    weight_s[...] = (grown / total - target) * (GRADIENT_FACTOR * scale)
    mine = pl.ds(pl.multiple_of(doc_ref[0] * GROUPS, GROUPS), GROUPS)
    grad = folded(jnp.dot(stacked(weight_s[mine, :]), query, preferred_element_type=F32))
    own = pooled_ref[mine, :]
    own_unit = own / jnp.sqrt(jnp.sum(own * own, axis=1, keepdims=True) + NORM_EPS)
    along = jnp.sum(own_unit * grad, axis=1, keepdims=True)
    spread = folded(
        lax.dot_general(stacked(grad), w_ref[...], NT, preferred_element_type=F32)
    )
    extra = jnp.where(lanes(GROUPS) < 64, along, loss)
    for head in range(HEAD_COUNT):
        part = spread[:, head * HEAD_DIM : (head + 1) * HEAD_DIM]
        out_ref[head, 0:8, :] = jnp.concatenate([part, part], axis=1)
        out_ref[head, 8:16, :] = grad[:, head * 128 : (head + 1) * 128]
        out_ref[head, 16:24, :] = extra


def fold_kernel(in_ref, out_ref):
    terms = [in_ref[n] for n in range(HEAD_COUNT)]
    while len(terms) > 1:
        terms = [terms[n] + terms[n + 1] for n in range(0, len(terms), 2)]
    out_ref[...] = jnp.broadcast_to(terms[0][None], (4, 24, 128))


def group_kernel(lens_ref, terms_ref, ready_ref, dattn_ref, grad_ref, loss_ref):
    sums = (terms_ref[0] + terms_ref[1]) + (terms_ref[2] + terms_ref[3])
    along = sums[16:24, 0:1]
    loss_ref[...] = sums[16:24, :] / QUERY_COUNT
    norms = ready_ref[16:24, :]
    dattn_ref[...] = (sums[0:8] - ready_ref[0:8, :] * along) / norms / lengths_of(lens_ref)
    grad = (sums[8:16] - ready_ref[8:16, :] * along) / norms
    grad_ref[...] = jnp.broadcast_to(grad[None], (HEAD_COUNT, GROUPS, 128))


def inputs_kernel(place_ref, lens_ref, parts_ref, means_ref, grad_inputs_ref, out_ref):
    grad = jnp.concatenate([parts_ref[n] for n in range(HEAD_COUNT)], axis=1)
    mine = local_member(lens_ref, place_ref[3])
    members = jnp.concatenate([mine, mine, mine, mine], axis=0).astype(BF16)
    grad_inputs_ref[...] = lax.dot_general(
        members, stacked(grad / lengths_of(lens_ref)[:, 0:1]), TN, preferred_element_type=F32
    ).astype(BF16)
    both = jnp.concatenate([grad, means_ref[...]], axis=1)
    out_ref[...] = jnp.broadcast_to(both[None], (DOCS, GROUPS, MODEL + WIDTH))


def weight_kernel(in_ref, out_ref):
    grads = three(in_ref[:, :MODEL])
    means = three(in_ref[:, MODEL:])
    out_ref[...] = lax.dot_general(
        jnp.concatenate([means[1], means[0], means[0]], axis=0),
        jnp.concatenate([grads[0], grads[1], grads[0]], axis=0),
        TN,
        preferred_element_type=F32,
    )


def row_kernel(place_ref, lens_ref, y_ref, lse_ref, x_ref, dattn_ref, out_ref, q_s, d_s, delta_s):
    lane = lanes(QUARTER)
    member = quarter_member(lens_ref, place_ref[0], place_ref[1]).astype(BF16)
    spread = lax.dot_general(
        member, dattn_ref[...].astype(BF16), TN, preferred_element_type=F32
    )
    spread = jnp.where(lane < 64, 0.0, spread)
    mine = y_ref[0:QUARTER, :]
    q_s[...] = jnp.where(lane < 64, mine, jnp.zeros_like(mine))
    d_s[...] = spread.astype(BF16)
    delta_s[...] = jnp.broadcast_to(
        jnp.sum(spread * mine.astype(F32), axis=1, keepdims=True), (QUARTER, 128)
    )

    def block(i, carry):
        rows = pl.ds(pl.multiple_of(i * BLOCK, BLOCK), BLOCK)
        columns = []
        for part in range(PARTS):
            line = lse_ref[pl.ds(i * PARTS + part, 1), :]
            columns.append(jnp.transpose(jnp.broadcast_to(line, (128, 128))))
        log_total = jnp.concatenate(columns, axis=0)[:, 0:1]
        scores = lax.dot_general(q_s[rows, :], x_ref[...], NT, preferred_element_type=F32)
        prob = jnp.exp(scores - log_total)
        prob_grad = lax.dot_general(d_s[rows, :], x_ref[...], NT, preferred_element_type=F32)
        score_grad = (prob * (prob_grad - delta_s[rows, 0:1])).astype(BF16)
        for_query = jnp.dot(score_grad, x_ref[...], preferred_element_type=F32) * SCALE
        count = BLOCK // HALF
        value = for_query[:, 0:64].astype(BF16).reshape(count, HALF, HEAD_DIM)
        out_ref[pl.ds(i * count, count), :, :] = jnp.concatenate(
            [value[:, 0:32], value[:, 32:64]], axis=2
        )
        return carry

    lax.fori_loop(0, QUARTER // BLOCK, block, 0)


def column_kernel(lens_ref, own_ref, y_ref, dattn_ref, out_ref, y_s, k_s, v_s, delta_s, lse_s):
    lane = lanes(QUARTER)
    mine = own_ref[:, 0:64, :].reshape(QUARTER, 128)
    zero = jnp.zeros_like(mine)
    k_s[...] = jnp.where(lane < 64, mine, zero)
    v_s[...] = jnp.where(lane < 64, zero, mine)
    dattn = dattn_ref[...].astype(BF16)
    ones = jnp.ones((8, 128), F32)
    for n in range(4):
        rows = slice(n * QUARTER, (n + 1) * QUARTER)
        member = quarter_member(lens_ref, n // 2, n % 2).astype(BF16)
        spread = lax.dot_general(member, dattn, TN, preferred_element_type=F32)
        spread = jnp.where(lane < 64, 0.0, spread)
        other = y_ref[n, 0:QUARTER, :]
        y_s[rows, :] = jnp.where(lane < 64, other, spread.astype(BF16))
        delta_s[:, rows] = lax.dot_general(
            ones, spread * other.astype(F32), NT, precision=EXACT, preferred_element_type=F32
        )
        lse = y_ref[n, QUARTER : QUARTER + 32, :].astype(F32)
        lse = (lse[16:24] + lse[8:16]) + lse[0:8]
        for part in range(8):
            lse_s[:, n * QUARTER + part * 128 : n * QUARTER + (part + 1) * 128] = jnp.broadcast_to(
                lse[part : part + 1, :], (8, 128)
            )

    def block(i, carry):
        rows = pl.ds(pl.multiple_of(i * BLOCK, BLOCK), BLOCK)
        scores = lax.dot_general(k_s[rows, :], y_s[...], NT, preferred_element_type=F32)
        prob = jnp.exp(scores - lse_s[0:1, :])
        prob_grad = lax.dot_general(v_s[rows, :], y_s[...], NT, preferred_element_type=F32)
        score_grad = (prob * (prob_grad - delta_s[0:1, :])).astype(BF16)
        for_key = jnp.dot(score_grad, y_s[...], preferred_element_type=F32)
        for_value = jnp.dot(prob.astype(BF16), y_s[...], preferred_element_type=F32)
        both = jnp.where(lanes(BLOCK) < 64, for_key, for_value).astype(BF16)
        count = BLOCK // HALF
        out_ref[pl.ds(i * count, count), :, :] = both.reshape(count, HALF, 128)
        return carry

    lax.fori_loop(0, QUARTER // BLOCK, block, 0)


SMEM = pl.BlockSpec(memory_space=pltpu.SMEM)
VMEM = pl.BlockSpec(memory_space=pltpu.VMEM)


def call(kernel, outs, scalars, arrays, scratch, estimate, name):
    return pl.pallas_call(
        kernel,
        out_shape=outs,
        in_specs=[SMEM] * len(scalars) + [VMEM] * len(arrays),
        out_specs=jax.tree.map(lambda _: VMEM, outs),
        scratch_shapes=scratch,
        compiler_params=params(),
        cost_estimate=estimate,
        name=name,
    )(*scalars, *arrays)


def shape(dims, dtype):
    return jax.ShapeDtypeStruct(dims, dtype)


def body(inputs, q_heads, k_heads, v_heads, w_out, group_lens, query_emb, positive):
    plane = lax.axis_index("yl")
    half = lax.axis_index("zd")
    head = lax.axis_index(HEADS)
    first = lax.axis_index(SEQ) * ROWS
    doc = lax.axis_index(GRP).reshape(1).astype(jnp.int32)
    place = jnp.stack([plane, half, head, first]).astype(jnp.int32)
    lengths = group_lens[0]
    exchange = functools.partial(lax.all_to_all, split_axis=0, concat_axis=0)

    packed = call(
        pack_kernel, shape((PLANE, 112, 128), BF16), (place, lengths),
        (q_heads[0], k_heads[0], v_heads[0], inputs[0]), (), cost(0, 1000000), "pack",
    )
    tagged = jnp.concatenate(
        [query_emb, jnp.pad(positive.astype(BF16)[:, None], ((0, 0), (0, 127)))], axis=1
    )
    packed, tagged = lax.optimization_barrier((packed, tagged))
    own = exchange(packed, ZED)
    queries = gather_grp(tagged)
    query_rows = call(
        query_kernel, shape((16, 256), F32), (), (queries,), (), cost(6 * 2 * 8 * 256 * 1024, 600000),
        "queries",
    )
    own, queries, query_rows = lax.optimization_barrier((own, queries, query_rows))
    keys = share(own[:, 0:64, :], SQUARE).reshape(4 * QUARTER, 128)

    pairs = QUARTER * 4 * QUARTER
    outgoing, lse, means, mine = call(
        forward_kernel,
        (
            shape((4, QUARTER + 32, 128), BF16),
            shape((8, 128), F32),
            shape((4, GROUPS, 128), F32),
            shape((QUARTER + 32, 128), BF16),
        ),
        (place, lengths), (own, keys), [pltpu.VMEM((QUARTER, 128), BF16)],
        cost(pairs * 256 * 4, 3000000, pairs), "forward",
    )
    means = exchange(means, SQUARE)
    means = call(
        square_kernel, shape((HEAD_COUNT, 16, 128), F32), (), (means,), (), cost(0, 100000), "square",
    )
    means = exchange(means, HEADS)
    pooled, pooled_own, doc_means = call(
        pool_kernel,
        (
            shape((DOCS, GROUPS, MODEL), F32),
            shape((GROUPS, MODEL), F32),
            shape((GROUPS, WIDTH), F32),
        ),
        (), (means, w_out), (), cost(2 * 32 * 512 * 1024, 1200000), "pool",
    )
    pooled, pooled_own, outgoing = lax.optimization_barrier((pooled, pooled_own, outgoing))
    pooled_all = exchange(pooled, GRP).reshape(DOCS * GROUPS, MODEL)
    others = exchange(outgoing, SQUARE)
    ready = call(
        prepare_kernel, shape((24, 128), F32), (place,), (pooled_own, w_out), (),
        cost(2 * 32 * 128 * 1024, 1200000), "prepare",
    )
    pooled_all, others, ready = lax.optimization_barrier((pooled_all, others, ready))
    terms = call(
        loss_kernel, shape((HEAD_COUNT, 24, 128), F32), (doc,),
        (pooled_all, queries, query_rows, w_out), [pltpu.VMEM((DOCS * GROUPS, 256), F32)],
        cost(3 * 2 * 128 * 256 * 1024, 2500000, 40000), "loss",
    )
    terms = exchange(terms, HEADS)
    terms = call(
        fold_kernel, shape((4, 24, 128), F32), (), (terms,), (), cost(0, 150000), "fold",
    )
    terms = exchange(terms, SQUARE)

    dattn, grad_part, loss = call(
        group_kernel,
        (
            shape((GROUPS, 128), F32),
            shape((HEAD_COUNT, GROUPS, 128), F32),
            shape((GROUPS, 128), F32),
        ),
        (lengths,), (terms, ready), (), cost(0, 100000), "group",
    )
    mean_loss = loss[0, 64]
    grad_parts = exchange(grad_part, HEADS)
    packed_pair = call(
        column_kernel, shape((PLANE, HALF, 128), BF16), (lengths,), (own, others, dattn),
        [
            pltpu.VMEM((4 * QUARTER, 128), BF16),
            pltpu.VMEM((QUARTER, 128), BF16),
            pltpu.VMEM((QUARTER, 128), BF16),
            pltpu.VMEM((8, 4 * QUARTER), F32),
            pltpu.VMEM((8, 4 * QUARTER), F32),
        ],
        cost(pairs * 256 * 8, 2500000, pairs), "columns",
    )
    grad_inputs, grads = call(
        inputs_kernel,
        (shape((ROWS, MODEL), BF16), shape((DOCS, GROUPS, MODEL + WIDTH), F32)),
        (place, lengths), (grad_parts, doc_means), (), cost(2 * 32 * 128 * 1024, 1200000), "inputs",
    )
    packed_pair, grads, dattn = lax.optimization_barrier((packed_pair, grads, dattn))
    home_pair = exchange(packed_pair, ZED)
    all_grads = exchange(grads, GRP)
    packed_query = call(
        row_kernel, shape((PLANE, 32, 128), BF16), (place, lengths), (mine, lse, keys, dattn),
        [
            pltpu.VMEM((QUARTER, 128), BF16),
            pltpu.VMEM((QUARTER, 128), BF16),
            pltpu.VMEM((QUARTER, 128), F32),
        ],
        cost(pairs * 256 * 6, 2000000, pairs), "rows",
    )
    home_query = exchange(packed_query, ZED)
    out = shape((ROWS, WIDTH), BF16)
    grad_k, grad_v = call(
        unpack_pair_kernel, (out, out), (), (home_pair,), (), cost(0, 500000), "unpack_pair"
    )
    grad_w_out = call(
        weight_kernel, shape((WIDTH, MODEL), F32), (),
        (all_grads.reshape(DOCS * GROUPS, MODEL + WIDTH),), (),
        cost(2 * 384 * 512 * 1024, 3000000), "weights",
    )
    grad_q = call(
        unpack_query_kernel, out, (), (home_query,), (), cost(0, 300000), "unpack_query"
    )
    return (mean_loss, grad_inputs[None], grad_q[None], grad_k[None], grad_v[None], grad_w_out)


def solution(mesh):
    fine = Mesh(mesh.devices.reshape((2,) * 9), GRP + SEQ)
    rows = P(GRP, SEQ, None)
    return jax.shard_map(
        body,
        mesh=fine,
        in_specs=(
            rows,
            rows,
            rows,
            rows,
            P(),
            P(GRP, None),
            P(GRP + SEQ, None),
            P(GRP + SEQ),
        ),
        out_specs=(P(), rows, rows, rows, rows, P()),
        check_vma=False,
    )
```

```python
import functools

import jax
import jax.numpy as jnp
from jax import lax
from jax.experimental import pallas as pl
from jax.experimental.pallas import tpu as pltpu
from jax.sharding import Mesh, PartitionSpec as P

HEAD_COUNT = 8
HEAD_DIM = 64
GROUPS = 8
DOCS = 16
MODEL = 1024
WIDTH = 512
ROWS = 128
HALF = 64
QUARTER = 1024
PLANE = 16
SCALE = HEAD_DIM ** (-0.5)

RECIPROCAL_TEMP = 20.0
GRADIENT_FACTOR = 64.0
NORM_EPS = 1e-06
QUERY_COUNT = 8192
EXACT = lax.Precision.HIGHEST

BF16 = jnp.bfloat16
F32 = jnp.float32

GRP = ("yh", "xa", "xb", "co")
SEQ = ("yl", "za", "zb", "zc", "zd")
ZED = ("za", "zb", "zc", "zd")
SQUARE = ("yl", "zd")
HEADS = ("za", "zb", "zc")
NT = (((1,), (1,)), ((), ()))
TN = (((0,), (0,)), ((), ()))

VMEM_BYTES = 56 << 20


def params():
    return pltpu.CompilerParams(vmem_limit_bytes=VMEM_BYTES)


def cost(flops, moved, exps=0):
    return pl.CostEstimate(flops=int(flops), bytes_accessed=int(moved), transcendentals=int(exps))


def share(value, axes):
    count = 2 ** len(axes)
    return lax.all_to_all(
        jnp.broadcast_to(value[None], (count,) + value.shape), axes, split_axis=0, concat_axis=0
    )


def swap(value, axes, flip):
    count = 2 ** len(axes)
    return lax.ppermute(value, axes, [(i, i ^ flip) for i in range(count)])


def gather_step(value, axis):
    other = swap(value, (axis,), 1)
    first = lax.axis_index(axis) == 0
    return jnp.where(
        first,
        jnp.concatenate([value, other], axis=0),
        jnp.concatenate([other, value], axis=0),
    )


def three(value):
    high = value.astype(BF16)
    rest = value - high.astype(F32)
    middle = rest.astype(BF16)
    low = (rest - middle.astype(F32)).astype(BF16)
    return high, middle, low


def stacked(value):
    parts = [part.astype(F32) for part in three(value)]
    parts.append(jnp.zeros_like(value))
    return jnp.concatenate(parts, axis=0).astype(BF16)


def folded(product):
    return (product[16:24] + product[8:16]) + product[0:8]


def column_of(values):
    row = lax.broadcasted_iota(jnp.int32, (GROUPS, 128), 0)
    out = jnp.full((GROUPS, 128), values[0])
    for n in range(1, GROUPS):
        out = jnp.where(row == n, values[n], out)
    return out


def member_of(position, lens_ref):
    ends = [lens_ref[0]]
    for n in range(1, GROUPS):
        ends.append(ends[-1] + lens_ref[n])
    last = column_of(ends)
    first = last - column_of([lens_ref[n] for n in range(GROUPS)])
    return ((position >= first[:, 0:1]) & (position < last[:, 0:1])).astype(F32)


def lengths_of(lens_ref):
    return column_of([lens_ref[n] for n in range(GROUPS)]).astype(F32)


def quarter_member(lens_ref, plane, half):
    row = lax.broadcasted_iota(jnp.int32, (GROUPS, QUARTER), 1)
    position = plane * (PLANE * ROWS) + (row >> 6) * ROWS + half * HALF + (row & 63)
    return member_of(position, lens_ref)


def local_member(lens_ref, first):
    return member_of(first + lax.broadcasted_iota(jnp.int32, (GROUPS, ROWS), 1), lens_ref)


def halves(packed):
    return jnp.concatenate([packed[:, :, 0:64], packed[:, :, 64:128]], axis=1)


def lanes(rows):
    return lax.broadcasted_iota(jnp.int32, (rows, 128), 1)


def pack_kernel(place_ref, lens_ref, q_ref, k_ref, v_ref, inputs_ref, out_ref):
    mine = local_member(lens_ref, place_ref[3]).astype(BF16)
    sums = jnp.dot(mine, inputs_ref[...], preferred_element_type=F32)
    high, middle, low = [part.astype(F32) for part in three(sums)]
    zero = jnp.zeros((GROUPS, HALF), F32)
    for head in range(HEAD_COUNT):
        cols = slice(head * HEAD_DIM, (head + 1) * HEAD_DIM)
        for half in range(2):
            rows = slice(half * HALF, (half + 1) * HALF)
            place = 2 * head + half
            out_ref[place, 0:64, :] = jnp.concatenate([k_ref[rows, cols], v_ref[rows, cols]], axis=1)
            query = q_ref[rows, cols] * jnp.asarray(SCALE, BF16)
            out_ref[place, 64:96, :] = jnp.concatenate([query[0:32], query[32:64]], axis=1)
            part = slice(place * HALF, (place + 1) * HALF)
            upper = jnp.concatenate([high[:, part], middle[:, part]], axis=1)
            lower = jnp.concatenate([low[:, part], zero], axis=1)
            out_ref[place, 96:112, :] = jnp.concatenate([upper, lower], axis=0).astype(BF16)


def unpack_kernel(in_ref, q_ref, k_ref):
    for pair in range(HEAD_COUNT // 2):
        cols = slice(pair * 128, (pair + 1) * 128)
        for half in range(2):
            rows = slice(half * HALF, (half + 1) * HALF)
            first, second = in_ref[4 * pair + half], in_ref[4 * pair + 2 + half]
            k_ref[rows, cols] = jnp.concatenate([first[:, 0:64], second[:, 0:64]], axis=1)
            q_ref[rows, cols] = jnp.concatenate([first[:, 64:128], second[:, 64:128]], axis=1)


BLOCK = 256
PARTS = BLOCK // 128


STEPS = QUARTER // BLOCK
KEYS = 4 * QUARTER


def forward_kernel(
    place_ref, lens_ref, own_ref, x_ref, prob_ref, y_ref, lse_ref, means_ref, q_s
):
    i = pl.program_id(0)

    @pl.when(i == 0)
    def start():
        queries = halves(own_ref[:, 64:96, :]).reshape(QUARTER, HEAD_DIM)
        q_s[...] = jnp.concatenate([queries, jnp.zeros_like(queries)], axis=1)

    rows = pl.ds(pl.multiple_of(i * BLOCK, BLOCK), BLOCK)
    scores = lax.dot_general(q_s[rows, :], x_ref[...], NT, preferred_element_type=F32)
    top = jnp.max(scores, axis=1, keepdims=True)
    grown = jnp.exp(scores - top)
    total = jnp.sum(grown, axis=1, keepdims=True)
    prob_ref[...] = (grown * (1.0 / total)).astype(BF16)
    mixed = jnp.dot(prob_ref[...], x_ref[...], preferred_element_type=F32).astype(BF16)
    y_ref[rows, :] = jnp.where(lanes(BLOCK) < 64, q_s[rows, :], mixed)
    log_total = top + jnp.log(total)
    for part in range(PARTS):
        square = jnp.broadcast_to(log_total[part * 128 : (part + 1) * 128], (128, 128))
        lse_ref[pl.ds(i * PARTS + part, 1), :] = jnp.transpose(square)[0:1, :]

    @pl.when(i == STEPS - 1)
    def finish():
        y_ref[QUARTER : QUARTER + 32, :] = stacked(lse_ref[...])
        member = quarter_member(lens_ref, place_ref[0], place_ref[1]).astype(BF16)
        attn_sums = jnp.dot(member, y_ref[0:QUARTER, :], preferred_element_type=F32)
        sums = jnp.sum(own_ref[:, 96:112, :].astype(F32), axis=0)
        input_sums = (sums[0:8] + pltpu.roll(sums[0:8], 64, 1)) + sums[8:16]
        means = jnp.where(lanes(GROUPS) < 64, input_sums, attn_sums) / lengths_of(lens_ref)
        means_ref[...] = jnp.broadcast_to(means[None], (2 * PLANE, GROUPS, 128))


def pool_kernel(means_ref, w_ref, pooled_ref, own_ref, means_out_ref):
    columns, heads = [], []
    for z in range(PLANE):
        both = means_ref[z] + means_ref[PLANE + z]
        columns.append(both[:, 0:64])
        if z % 2 == 0:
            heads.append(both[:, 64:128])
        else:
            heads[-1] = heads[-1] + both[:, 64:128]
    means = jnp.concatenate(heads, axis=1)
    projected = jnp.dot(stacked(means), w_ref[...], preferred_element_type=F32)
    pooled = jnp.concatenate(columns, axis=1) + folded(projected)
    pooled_ref[...] = jnp.broadcast_to(pooled[None], (DOCS, GROUPS, MODEL))
    own_ref[...] = pooled
    means_out_ref[...] = means


def prepare_kernel(place_ref, pooled_ref, w_ref, out_ref):
    head = place_ref[2]
    pooled = pooled_ref[...]
    norms = jnp.sqrt(jnp.sum(pooled * pooled, axis=1, keepdims=True) + NORM_EPS)
    unit = pooled / norms
    w_head = w_ref[pl.ds(pl.multiple_of(head * HEAD_DIM, HEAD_DIM), HEAD_DIM), :]
    w_twice = jnp.concatenate([w_head, w_head], axis=0)
    out_ref[0:8, :] = folded(
        lax.dot_general(stacked(unit), w_twice, NT, preferred_element_type=F32)
    )
    z = 2 * head + place_ref[1]
    part = unit[:, 0:64]
    for n in range(1, PLANE):
        part = jnp.where(z == n, unit[:, n * HALF : (n + 1) * HALF], part)
    out_ref[8:16, :] = jnp.concatenate([part, part], axis=1)
    out_ref[16:24, :] = jnp.broadcast_to(norms, (GROUPS, 128))


def query_kernel(query_ref, out_ref):
    query = query_ref[:, :MODEL].astype(F32)
    squares = lax.dot_general(
        jnp.ones((8, MODEL), F32), query * query, NT, precision=EXACT, preferred_element_type=F32
    )
    out_ref[0:8, :] = jnp.sqrt(squares + NORM_EPS)
    out_ref[8:16, :] = lax.dot_general(
        jnp.ones((8, 128), BF16), query_ref[:, MODEL:], NT, preferred_element_type=F32
    )


def loss_kernel(doc_ref, pooled_ref, query_ref, row_ref, w_ref, out_ref, weight_s):
    pooled = pooled_ref[...]
    norms = jnp.sqrt(jnp.sum(pooled * pooled, axis=1, keepdims=True) + NORM_EPS)
    unit = pooled / norms
    query = query_ref[:, :MODEL]
    scale = RECIPROCAL_TEMP / row_ref[0:1, :]
    logits = jnp.zeros((DOCS * GROUPS, 256), F32)
    for part in three(unit)[::-1]:
        logits = logits + lax.dot_general(part, query, NT, preferred_element_type=F32)
    logits = logits * scale
    grown = jnp.exp(logits)
    total = jnp.sum(grown, axis=0, keepdims=True)
    group = lax.broadcasted_iota(jnp.int32, logits.shape, 0)
    target = (group == row_ref[8:9, :].astype(jnp.int32)).astype(F32)
    losses = jnp.log(total) - jnp.sum(target * logits, axis=0, keepdims=True)
    loss = jnp.sum(losses, axis=1, keepdims=True)
    weight_s[...] = (grown / total - target) * (GRADIENT_FACTOR * scale)
    mine = pl.ds(pl.multiple_of(doc_ref[0] * GROUPS, GROUPS), GROUPS)
    grad = folded(jnp.dot(stacked(weight_s[mine, :]), query, preferred_element_type=F32))
    own = pooled_ref[mine, :]
    own_unit = own / jnp.sqrt(jnp.sum(own * own, axis=1, keepdims=True) + NORM_EPS)
    along = jnp.sum(own_unit * grad, axis=1, keepdims=True)
    spread = folded(
        lax.dot_general(stacked(grad), w_ref[...], NT, preferred_element_type=F32)
    )
    extra = jnp.where(lanes(GROUPS) < 64, along, loss)
    for z in range(PLANE):
        head = z // 2
        chunk = jnp.concatenate(
            [
                spread[:, head * HEAD_DIM : (head + 1) * HEAD_DIM],
                grad[:, z * HALF : (z + 1) * HALF],
            ],
            axis=1,
        )
        for plane in range(2):
            out_ref[plane * PLANE + z, 0:8, :] = chunk
            out_ref[plane * PLANE + z, 8:16, :] = extra


def mass_kernel(lens_ref, own_ref, y_ref, prob_ref, mass_ref, k_s, lse_s, member_s):
    i = pl.program_id(0)

    @pl.when(i == 0)
    def start():
        mine = own_ref[:, 0:64, :].reshape(QUARTER, 128)
        k_s[...] = jnp.where(lanes(QUARTER) < 64, mine, jnp.zeros_like(mine))
        for n in range(4):
            lse = y_ref[n * (QUARTER + 32) + QUARTER : (n + 1) * (QUARTER + 32), :].astype(F32)
            lse = (lse[16:24] + lse[8:16]) + lse[0:8]
            for part in range(8):
                at = n * QUARTER + part * 128
                lse_s[:, at : at + 128] = jnp.broadcast_to(lse[part : part + 1, :], (8, 128))
            member = quarter_member(lens_ref, n // 2, n % 2)
            padded = jnp.concatenate([member, jnp.zeros((120, QUARTER), F32)], axis=0)
            member_s[:, n * QUARTER : (n + 1) * QUARTER] = padded.astype(BF16)

    rows = pl.ds(pl.multiple_of(i * BLOCK, BLOCK), BLOCK)
    sums = jnp.zeros((BLOCK, 128), F32)
    for n in range(4):
        cols = slice(n * QUARTER, (n + 1) * QUARTER)
        other = y_ref[n * (QUARTER + 32) : n * (QUARTER + 32) + QUARTER, :]
        scores = lax.dot_general(k_s[rows, :], other, NT, preferred_element_type=F32)
        prob_ref[:, cols] = jnp.exp(scores - lse_s[0:1, cols]).astype(BF16)
        sums = sums + lax.dot_general(
            prob_ref[:, cols], member_s[:, cols], NT, preferred_element_type=F32
        )
    for part in range(PARTS):
        mass_ref[i * PARTS + part] = jnp.transpose(sums[part * 128 : (part + 1) * 128])[0:8, :]


def group_kernel(lens_ref, terms_ref, ready_ref, mass_ref, dattn_ref, grad_ref, loss_ref):
    sums = terms_ref[0]
    for n in range(1, 2 * PLANE):
        sums = sums + terms_ref[n]
    along = sums[8:16, 0:1]
    loss_ref[...] = sums[8:16, :] / QUERY_COUNT
    norms = ready_ref[16:24, :]
    raw = jnp.concatenate([sums[0:8, 0:64], sums[0:8, 0:64]], axis=1)
    dattn_ref[...] = (raw - ready_ref[0:8, :] * along) / norms / lengths_of(lens_ref)
    grad = (sums[0:8, 64:128] - ready_ref[8:16, 0:64] * along) / norms[:, 0:64]
    for z in range(PLANE):
        half = (z % 2) * HALF
        grad_ref[z] = jnp.concatenate([grad, mass_ref[z // 2, :, half : half + HALF]], axis=1)


def inputs_kernel(place_ref, lens_ref, parts_ref, means_ref, grad_inputs_ref, out_ref):
    grad = jnp.concatenate([parts_ref[z, :, 0:64] for z in range(PLANE)], axis=1)
    mine = local_member(lens_ref, place_ref[3])
    members = jnp.concatenate([mine, mine, mine, mine], axis=0).astype(BF16)
    grad_inputs_ref[...] = lax.dot_general(
        members, stacked(grad / lengths_of(lens_ref)[:, 0:1]), TN, preferred_element_type=F32
    ).astype(BF16)
    both = jnp.concatenate([grad, means_ref[...]], axis=1)
    out_ref[...] = jnp.broadcast_to(both[None], (DOCS, GROUPS, MODEL + WIDTH))


def value_kernel(lens_ref, parts_ref, w_ref, grad_v_ref):
    grad = jnp.concatenate([parts_ref[z, :, 0:64] for z in range(PLANE)], axis=1)
    grad = grad / lengths_of(lens_ref)[:, 0:1]
    dattn = folded(lax.dot_general(stacked(grad), w_ref[...], NT, preferred_element_type=F32))
    dattn = dattn.astype(BF16).astype(F32)
    dattn = jnp.concatenate([dattn, dattn, dattn, jnp.zeros_like(dattn)], axis=0).astype(BF16)
    for pair in range(HEAD_COUNT // 2):
        cols = slice(pair * 128, (pair + 1) * 128)
        both = []
        for head in (2 * pair, 2 * pair + 1):
            mass = jnp.concatenate(
                [parts_ref[2 * head, :, 64:128], parts_ref[2 * head + 1, :, 64:128]], axis=1
            )
            both.append(
                lax.dot_general(stacked(mass), dattn[:, cols], TN, preferred_element_type=F32)
            )
        grad_v_ref[:, cols] = jnp.where(lanes(ROWS) < 64, both[0], both[1]).astype(BF16)


def weight_kernel(in_ref, out_ref):
    grads = three(in_ref[:, :MODEL])
    means = three(in_ref[:, MODEL:])
    out_ref[...] = lax.dot_general(
        jnp.concatenate([means[1], means[0], means[0]], axis=0),
        jnp.concatenate([grads[0], grads[1], grads[0]], axis=0),
        TN,
        preferred_element_type=F32,
    )


def row_kernel(place_ref, lens_ref, prob_ref, y_ref, x_ref, dattn_ref, out_ref, d_s, delta_s):
    i = pl.program_id(0)

    @pl.when(i == 0)
    def start():
        member = quarter_member(lens_ref, place_ref[0], place_ref[1]).astype(BF16)
        spread = lax.dot_general(
            member, dattn_ref[...].astype(BF16), TN, preferred_element_type=F32
        )
        spread = jnp.where(lanes(QUARTER) < 64, 0.0, spread)
        d_s[...] = spread.astype(BF16)
        delta_s[...] = jnp.broadcast_to(
            jnp.sum(spread * y_ref[0:QUARTER, :].astype(F32), axis=1, keepdims=True),
            (QUARTER, 128),
        )

    rows = pl.ds(pl.multiple_of(i * BLOCK, BLOCK), BLOCK)
    prob_grad = lax.dot_general(d_s[rows, :], x_ref[...], NT, preferred_element_type=F32)
    score_grad = (prob_ref[...].astype(F32) * (prob_grad - delta_s[rows, 0:1])).astype(BF16)
    for_query = jnp.dot(score_grad, x_ref[...], preferred_element_type=F32) * SCALE
    out_ref[rows, :] = jnp.concatenate([for_query[:, 0:64]] * 2, axis=1).astype(BF16)


def column_kernel(
    lens_ref, prob_ref, own_ref, y_ref, dattn_ref, grad_q_ref, out_ref, y_s, v_s, delta_s
):
    i = pl.program_id(0)

    @pl.when(i == 0)
    def start():
        lane = lanes(QUARTER)
        mine = own_ref[:, 0:64, :].reshape(QUARTER, 128)
        v_s[...] = jnp.where(lane < 64, jnp.zeros_like(mine), mine)
        dattn = dattn_ref[...].astype(BF16)
        ones = jnp.ones((8, 128), F32)
        for n in range(4):
            rows = slice(n * QUARTER, (n + 1) * QUARTER)
            member = quarter_member(lens_ref, n // 2, n % 2).astype(BF16)
            spread = lax.dot_general(member, dattn, TN, preferred_element_type=F32)
            spread = jnp.where(lane < 64, 0.0, spread)
            other = y_ref[n * (QUARTER + 32) : n * (QUARTER + 32) + QUARTER, :]
            y_s[rows, :] = jnp.where(lane < 64, other, spread.astype(BF16))
            delta_s[:, rows] = lax.dot_general(
                ones, spread * other.astype(F32), NT, precision=EXACT, preferred_element_type=F32
            )

    rows = pl.ds(pl.multiple_of(i * BLOCK, BLOCK), BLOCK)
    prob_grad = lax.dot_general(v_s[rows, :], y_s[...], NT, preferred_element_type=F32)
    score_grad = (prob_ref[...].astype(F32) * (prob_grad - delta_s[0:1, :])).astype(BF16)
    for_key = jnp.dot(score_grad, y_s[...], preferred_element_type=F32).astype(BF16)
    both = jnp.where(lanes(BLOCK) < 64, for_key, grad_q_ref[rows, :])
    count = BLOCK // HALF
    out_ref[pl.ds(i * count, count), :, :] = both.reshape(count, HALF, 128)


SMEM = pl.BlockSpec(memory_space=pltpu.SMEM)
VMEM = pl.BlockSpec(memory_space=pltpu.VMEM)


def call(kernel, outs, scalars, arrays, scratch, estimate, name):
    return pl.pallas_call(
        kernel,
        out_shape=outs,
        in_specs=[SMEM] * len(scalars) + [VMEM] * len(arrays),
        out_specs=jax.tree.map(lambda _: VMEM, outs),
        scratch_shapes=scratch,
        compiler_params=params(),
        cost_estimate=estimate,
        name=name,
    )(*scalars, *arrays)


def whole(array):
    rank = len(array.shape)
    return pl.BlockSpec(array.shape, lambda i: (0,) * rank)


PROB = pl.BlockSpec((BLOCK, KEYS), lambda i: (i, 0))


def sweep(kernel, outs, scalars, arrays, scratch, estimate, name):
    def spec(array):
        return PROB if array.shape == (QUARTER, KEYS) else whole(array)

    return pl.pallas_call(
        kernel,
        out_shape=outs,
        grid=(STEPS,),
        in_specs=[SMEM] * len(scalars) + [spec(array) for array in arrays],
        out_specs=jax.tree.map(spec, outs),
        scratch_shapes=scratch,
        compiler_params=params(),
        cost_estimate=estimate,
        name=name,
    )(*scalars, *arrays)


def shape(dims, dtype):
    return jax.ShapeDtypeStruct(dims, dtype)


def body(inputs, q_heads, k_heads, v_heads, w_out, group_lens, query_emb, positive):
    plane = lax.axis_index("yl")
    half = lax.axis_index("zd")
    head = lax.axis_index(HEADS)
    first = lax.axis_index(SEQ) * ROWS
    doc = lax.axis_index(GRP).reshape(1).astype(jnp.int32)
    place = jnp.stack([plane, half, head, first]).astype(jnp.int32)
    lengths = group_lens[0]
    exchange = functools.partial(lax.all_to_all, split_axis=0, concat_axis=0)
    barrier = lax.optimization_barrier
    pairs = QUARTER * KEYS

    packed = call(
        pack_kernel, shape((PLANE, 112, 128), BF16), (place, lengths),
        (q_heads[0], k_heads[0], v_heads[0], inputs[0]), (), cost(0, 1000000), "pack",
    )
    tagged = jnp.concatenate(
        [query_emb, jnp.pad(positive.astype(BF16)[:, None], ((0, 0), (0, 127)))], axis=1
    )
    packed, tagged = barrier((packed, tagged))
    own = exchange(packed, ZED)
    queries = gather_step(gather_step(gather_step(tagged, "co"), "xb"), "xa")
    own, queries = barrier((own, queries))
    keys = share(own[:, 0:64, :], SQUARE).reshape(KEYS, 128)

    prob, mine, lse, means = sweep(
        forward_kernel,
        (
            shape((QUARTER, KEYS), BF16),
            shape((QUARTER + 32, 128), BF16),
            shape((8, 128), F32),
            shape((2 * PLANE, GROUPS, 128), F32),
        ),
        (place, lengths), (own, keys), [pltpu.VMEM((QUARTER, 128), BF16)],
        cost(pairs * 256 * 4, 11000000, pairs), "forward",
    )
    mine, means, queries = barrier((mine, means, queries))
    means = exchange(means, SEQ)
    queries = gather_step(queries, "yh")
    around = [swap(mine, SQUARE, flip) for flip in (1, 2, 3)]
    means, queries, around = barrier((means, queries, around))
    pooled, pooled_own, doc_means = call(
        pool_kernel,
        (
            shape((DOCS, GROUPS, MODEL), F32),
            shape((GROUPS, MODEL), F32),
            shape((GROUPS, WIDTH), F32),
        ),
        (), (means, w_out), (), cost(2 * 32 * 512 * 1024, 1200000), "pool",
    )
    pooled_all = exchange(pooled, GRP).reshape(DOCS * GROUPS, MODEL)
    square = [mine] + around
    rotated = [jnp.where(half == 0, square[n], square[n ^ 1]) for n in range(4)]
    ordered = [jnp.where(plane == 0, rotated[n], rotated[n ^ 2]) for n in range(4)]
    others = jnp.concatenate(ordered, axis=0)
    query_rows = call(
        query_kernel, shape((16, 256), F32), (), (queries,), (), cost(6 * 2 * 8 * 256 * 1024, 600000),
        "queries",
    )
    ready = call(
        prepare_kernel, shape((24, 128), F32), (place,), (pooled_own, w_out), (),
        cost(2 * 32 * 128 * 1024, 1200000), "prepare",
    )
    pooled_all, others, ready, query_rows = barrier((pooled_all, others, ready, query_rows))
    terms = call(
        loss_kernel, shape((2 * PLANE, 16, 128), F32), (doc,),
        (pooled_all, queries, query_rows, w_out), [pltpu.VMEM((DOCS * GROUPS, 256), F32)],
        cost(3 * 2 * 128 * 256 * 1024, 2500000, 40000), "loss",
    )
    terms, own, others = barrier((terms, own, others))
    terms = exchange(terms, SEQ)
    turned, mass = sweep(
        mass_kernel,
        (shape((QUARTER, KEYS), BF16), shape((GROUPS, 8, 128), F32)),
        (lengths,), (own, others),
        [
            pltpu.VMEM((QUARTER, 128), BF16),
            pltpu.VMEM((8, KEYS), F32),
            pltpu.VMEM((128, KEYS), BF16),
        ],
        cost(pairs * 256 * 4, 11000000, pairs), "mass",
    )
    terms, turned, mass = barrier((terms, turned, mass))

    dattn, grad_part, loss = call(
        group_kernel,
        (
            shape((GROUPS, 128), F32),
            shape((PLANE, GROUPS, 128), F32),
            shape((GROUPS, 128), F32),
        ),
        (lengths,), (terms, ready, mass), (), cost(0, 100000), "group",
    )
    mean_loss = loss[0, 64]
    grad_parts = exchange(grad_part, ZED)
    grad_rows = sweep(
        row_kernel, shape((QUARTER, 128), BF16), (place, lengths), (prob, mine, keys, dattn),
        [pltpu.VMEM((QUARTER, 128), BF16), pltpu.VMEM((QUARTER, 128), F32)],
        cost(pairs * 256 * 4, 11000000), "rows",
    )
    grad_inputs, grads = call(
        inputs_kernel,
        (shape((ROWS, MODEL), BF16), shape((DOCS, GROUPS, MODEL + WIDTH), F32)),
        (place, lengths), (grad_parts, doc_means), (), cost(2 * 32 * 128 * 1024, 1200000), "inputs",
    )
    grad_rows, grads = barrier((grad_rows, grads))
    all_grads = exchange(grads, GRP)
    packed_grads = sweep(
        column_kernel, shape((PLANE, HALF, 128), BF16), (lengths,),
        (turned, own, others, dattn, grad_rows),
        [
            pltpu.VMEM((KEYS, 128), BF16),
            pltpu.VMEM((QUARTER, 128), BF16),
            pltpu.VMEM((8, KEYS), F32),
        ],
        cost(pairs * 256 * 4, 11000000), "columns",
    )
    packed_grads, grad_parts = barrier((packed_grads, grad_parts))
    home = exchange(packed_grads, ZED)
    out = shape((ROWS, WIDTH), BF16)
    grad_v = call(
        value_kernel, out, (lengths,), (grad_parts, w_out), (), cost(2 * 32 * 512 * 1024, 1300000),
        "values",
    )
    grad_w_out = call(
        weight_kernel, shape((WIDTH, MODEL), F32), (),
        (all_grads.reshape(DOCS * GROUPS, MODEL + WIDTH),), (),
        cost(2 * 384 * 512 * 1024, 3000000), "weights",
    )
    grad_q, grad_k = call(
        unpack_kernel, (out, out), (), (home,), (), cost(0, 500000), "unpack"
    )
    return (mean_loss, grad_inputs[None], grad_q[None], grad_k[None], grad_v[None], grad_w_out)


def solution(mesh):
    fine = Mesh(mesh.devices.reshape((2,) * 9), GRP + SEQ)
    rows = P(GRP, SEQ, None)
    return jax.shard_map(
        body,
        mesh=fine,
        in_specs=(
            rows,
            rows,
            rows,
            rows,
            P(),
            P(GRP, None),
            P(GRP + SEQ, None),
            P(GRP + SEQ),
        ),
        out_specs=(P(), rows, rows, rows, rows, P()),
        check_vma=False,
    )
```

```python
import functools

import jax
import jax.numpy as jnp
from jax import lax
from jax.experimental import pallas as pl
from jax.experimental.pallas import tpu as pltpu
from jax.sharding import Mesh, PartitionSpec as P

HEAD_COUNT = 8
HEAD_DIM = 64
GROUPS = 8
DOCS = 16
MODEL = 1024
WIDTH = 512
ROWS = 128
HALF = 64
QUARTER = 1024
PLANE = 16
SCALE = HEAD_DIM ** (-0.5)

RECIPROCAL_TEMP = 20.0
GRADIENT_FACTOR = 64.0
NORM_EPS = 1e-06
QUERY_COUNT = 8192
EXACT = lax.Precision.HIGHEST

BF16 = jnp.bfloat16
F32 = jnp.float32

GRP = ("yh", "xa", "xb", "co")
SEQ = ("yl", "za", "zb", "zc", "zd")
ZED = ("za", "zb", "zc", "zd")
SQUARE = ("yl", "zd")
HEADS = ("za", "zb", "zc")
NT = (((1,), (1,)), ((), ()))
TN = (((0,), (0,)), ((), ()))

VMEM_BYTES = 56 << 20


def params():
    return pltpu.CompilerParams(vmem_limit_bytes=VMEM_BYTES)


def cost(flops, moved, exps=0):
    return pl.CostEstimate(flops=int(flops), bytes_accessed=int(moved), transcendentals=int(exps))


def share(value, axes):
    count = 2 ** len(axes)
    return lax.all_to_all(
        jnp.broadcast_to(value[None], (count,) + value.shape), axes, split_axis=0, concat_axis=0
    )


def swap(value, axes, flip):
    count = 2 ** len(axes)
    return lax.ppermute(value, axes, [(i, i ^ flip) for i in range(count)])


def gather_grp(value):
    for axis in GRP:
        other = swap(value, (axis,), 1)
        first = lax.axis_index(axis) == 0
        value = jnp.where(
            first,
            jnp.concatenate([value, other], axis=0),
            jnp.concatenate([other, value], axis=0),
        )
    return value


def three(value):
    high = value.astype(BF16)
    rest = value - high.astype(F32)
    middle = rest.astype(BF16)
    low = (rest - middle.astype(F32)).astype(BF16)
    return high, middle, low


def stacked(value):
    parts = [part.astype(F32) for part in three(value)]
    parts.append(jnp.zeros_like(value))
    return jnp.concatenate(parts, axis=0).astype(BF16)


def folded(product):
    return (product[16:24] + product[8:16]) + product[0:8]


def column_of(values):
    row = lax.broadcasted_iota(jnp.int32, (GROUPS, 128), 0)
    out = jnp.full((GROUPS, 128), values[0])
    for n in range(1, GROUPS):
        out = jnp.where(row == n, values[n], out)
    return out


def member_of(position, lens_ref):
    ends = [lens_ref[0]]
    for n in range(1, GROUPS):
        ends.append(ends[-1] + lens_ref[n])
    last = column_of(ends)
    first = last - column_of([lens_ref[n] for n in range(GROUPS)])
    return ((position >= first[:, 0:1]) & (position < last[:, 0:1])).astype(F32)


def lengths_of(lens_ref):
    return column_of([lens_ref[n] for n in range(GROUPS)]).astype(F32)


def quarter_member(lens_ref, plane, half):
    row = lax.broadcasted_iota(jnp.int32, (GROUPS, QUARTER), 1)
    position = plane * (PLANE * ROWS) + (row >> 6) * ROWS + half * HALF + (row & 63)
    return member_of(position, lens_ref)


def local_member(lens_ref, first):
    return member_of(first + lax.broadcasted_iota(jnp.int32, (GROUPS, ROWS), 1), lens_ref)


def halves(packed):
    return jnp.concatenate([packed[:, :, 0:64], packed[:, :, 64:128]], axis=1)


def lanes(rows):
    return lax.broadcasted_iota(jnp.int32, (rows, 128), 1)


def pack_kernel(place_ref, lens_ref, q_ref, k_ref, v_ref, inputs_ref, out_ref):
    mine = local_member(lens_ref, place_ref[3]).astype(BF16)
    sums = jnp.dot(mine, inputs_ref[...], preferred_element_type=F32)
    high, middle, low = [part.astype(F32) for part in three(sums)]
    zero = jnp.zeros((GROUPS, HALF), F32)
    for head in range(HEAD_COUNT):
        cols = slice(head * HEAD_DIM, (head + 1) * HEAD_DIM)
        for half in range(2):
            rows = slice(half * HALF, (half + 1) * HALF)
            place = 2 * head + half
            out_ref[place, 0:64, :] = jnp.concatenate([k_ref[rows, cols], v_ref[rows, cols]], axis=1)
            query = q_ref[rows, cols] * jnp.asarray(SCALE, BF16)
            out_ref[place, 64:96, :] = jnp.concatenate([query[0:32], query[32:64]], axis=1)
            part = slice(place * HALF, (place + 1) * HALF)
            upper = jnp.concatenate([high[:, part], middle[:, part]], axis=1)
            lower = jnp.concatenate([low[:, part], zero], axis=1)
            out_ref[place, 96:112, :] = jnp.concatenate([upper, lower], axis=0).astype(BF16)


def unpack_kernel(in_ref, q_ref, k_ref):
    for pair in range(HEAD_COUNT // 2):
        cols = slice(pair * 128, (pair + 1) * 128)
        for half in range(2):
            rows = slice(half * HALF, (half + 1) * HALF)
            first, second = in_ref[4 * pair + half], in_ref[4 * pair + 2 + half]
            k_ref[rows, cols] = jnp.concatenate([first[:, 0:64], second[:, 0:64]], axis=1)
            q_ref[rows, cols] = jnp.concatenate([first[:, 64:128], second[:, 64:128]], axis=1)


BLOCK = 256
PARTS = BLOCK // 128


KEYS = 4 * QUARTER


def forward_kernel(
    place_ref, lens_ref, own_ref, x_ref, y_ref, lse_ref, means_ref, q_s
):
    queries = halves(own_ref[:, 64:96, :]).reshape(QUARTER, HEAD_DIM)
    q_s[...] = jnp.concatenate([queries, jnp.zeros_like(queries)], axis=1)

    def block(i, carry):
        rows = pl.ds(pl.multiple_of(i * BLOCK, BLOCK), BLOCK)
        scores = lax.dot_general(q_s[rows, :], x_ref[...], NT, preferred_element_type=F32)
        top = jnp.max(scores, axis=1, keepdims=True)
        grown = jnp.exp(scores - top)
        total = jnp.sum(grown, axis=1, keepdims=True)
        prob = (grown * (1.0 / total)).astype(BF16)
        mixed = jnp.dot(prob, x_ref[...], preferred_element_type=F32).astype(BF16)
        y_ref[rows, :] = jnp.where(lanes(BLOCK) < 64, q_s[rows, :], mixed)
        log_total = top + jnp.log(total)
        for part in range(PARTS):
            square = jnp.broadcast_to(log_total[part * 128 : (part + 1) * 128], (128, 128))
            lse_ref[pl.ds(i * PARTS + part, 1), :] = jnp.transpose(square)[0:1, :]
        return carry

    lax.fori_loop(0, QUARTER // BLOCK, block, 0)
    y_ref[QUARTER : QUARTER + 32, :] = stacked(lse_ref[...])
    member = quarter_member(lens_ref, place_ref[0], place_ref[1]).astype(BF16)
    attn_sums = jnp.dot(member, y_ref[0:QUARTER, :], preferred_element_type=F32)
    sums = jnp.sum(own_ref[:, 96:112, :].astype(F32), axis=0)
    input_sums = (sums[0:8] + pltpu.roll(sums[0:8], 64, 1)) + sums[8:16]
    means = jnp.where(lanes(GROUPS) < 64, input_sums, attn_sums) / lengths_of(lens_ref)
    means_ref[...] = jnp.broadcast_to(means[None], (2 * PLANE, GROUPS, 128))


def pool_kernel(doc_ref, means_ref, w_ref, query_ref, row_ref, own_ref, means_out_ref, logits_ref, out_ref):
    columns, heads = [], []
    for z in range(PLANE):
        both = means_ref[z] + means_ref[PLANE + z]
        columns.append(both[:, 0:64])
        if z % 2 == 0:
            heads.append(both[:, 64:128])
        else:
            heads[-1] = heads[-1] + both[:, 64:128]
    means = jnp.concatenate(heads, axis=1)
    projected = jnp.dot(stacked(means), w_ref[...], preferred_element_type=F32)
    pooled = jnp.concatenate(columns, axis=1) + folded(projected)
    own_ref[...] = pooled
    means_out_ref[...] = means
    unit = pooled / jnp.sqrt(jnp.sum(pooled * pooled, axis=1, keepdims=True) + NORM_EPS)
    logits = folded(
        lax.dot_general(stacked(unit), query_ref[:, :MODEL], NT, preferred_element_type=F32)
    )
    logits = logits * (RECIPROCAL_TEMP / row_ref[0:1, :])
    logits_ref[...] = logits
    group = doc_ref[0] * GROUPS + lax.broadcasted_iota(jnp.int32, logits.shape, 0)
    target = (group == row_ref[8:9, :].astype(jnp.int32)).astype(F32)
    total = jnp.sum(jnp.exp(logits), axis=0, keepdims=True)
    chosen = jnp.sum(target * logits, axis=0, keepdims=True)
    zero = jnp.zeros((4, 128), F32)
    sums = jnp.concatenate(
        [total[:, 0:128], total[:, 128:256], chosen[:, 0:128], chosen[:, 128:256], zero], axis=0
    )
    out_ref[...] = jnp.broadcast_to(sums[None], (DOCS, 8, 128))


def prepare_kernel(place_ref, pooled_ref, w_ref, out_ref):
    head = place_ref[2]
    pooled = pooled_ref[...]
    norms = jnp.sqrt(jnp.sum(pooled * pooled, axis=1, keepdims=True) + NORM_EPS)
    unit = pooled / norms
    w_head = w_ref[pl.ds(pl.multiple_of(head * HEAD_DIM, HEAD_DIM), HEAD_DIM), :]
    w_twice = jnp.concatenate([w_head, w_head], axis=0)
    out_ref[0:8, :] = folded(
        lax.dot_general(stacked(unit), w_twice, NT, preferred_element_type=F32)
    )
    z = 2 * head + place_ref[1]
    part = unit[:, 0:64]
    for n in range(1, PLANE):
        part = jnp.where(z == n, unit[:, n * HALF : (n + 1) * HALF], part)
    out_ref[8:16, :] = jnp.concatenate([part, part], axis=1)
    out_ref[16:24, :] = jnp.broadcast_to(norms, (GROUPS, 128))


def query_kernel(query_ref, out_ref):
    query = query_ref[:, :MODEL].astype(F32)
    squares = lax.dot_general(
        jnp.ones((8, MODEL), F32), query * query, NT, precision=EXACT, preferred_element_type=F32
    )
    out_ref[0:8, :] = jnp.sqrt(squares + NORM_EPS)
    out_ref[8:16, :] = lax.dot_general(
        jnp.ones((8, 128), BF16), query_ref[:, MODEL:], NT, preferred_element_type=F32
    )


def loss_kernel(doc_ref, sums_ref, logits_ref, own_ref, query_ref, row_ref, w_ref, out_ref):
    sums = sums_ref[0]
    for n in range(1, DOCS):
        sums = sums + sums_ref[n]
    total = jnp.concatenate([sums[0:1], sums[1:2]], axis=1)
    losses = jnp.log(sums[0:2]) - sums[2:4]
    loss = jnp.sum(jnp.sum(losses, axis=1, keepdims=True), axis=0, keepdims=True)
    query = query_ref[:, :MODEL]
    scale = RECIPROCAL_TEMP / row_ref[0:1, :]
    logits = logits_ref[...]
    group = doc_ref[0] * GROUPS + lax.broadcasted_iota(jnp.int32, logits.shape, 0)
    target = (group == row_ref[8:9, :].astype(jnp.int32)).astype(F32)
    weight = (jnp.exp(logits) / total - target) * (GRADIENT_FACTOR * scale)
    grad = folded(jnp.dot(stacked(weight), query, preferred_element_type=F32))
    own = own_ref[...]
    own_unit = own / jnp.sqrt(jnp.sum(own * own, axis=1, keepdims=True) + NORM_EPS)
    along = jnp.sum(own_unit * grad, axis=1, keepdims=True)
    spread = folded(
        lax.dot_general(stacked(grad), w_ref[...], NT, preferred_element_type=F32)
    )
    extra = jnp.where(lanes(GROUPS) < 64, along, loss)
    for z in range(PLANE):
        head = z // 2
        chunk = jnp.concatenate(
            [
                spread[:, head * HEAD_DIM : (head + 1) * HEAD_DIM],
                grad[:, z * HALF : (z + 1) * HALF],
            ],
            axis=1,
        )
        for plane in range(2):
            out_ref[plane * PLANE + z, 0:8, :] = chunk
            out_ref[plane * PLANE + z, 8:16, :] = extra


def mass_kernel(lens_ref, own_ref, y_ref, mass_ref, lse_ref, k_s, member_s):
    mine = own_ref[:, 0:64, :].reshape(QUARTER, 128)
    k_s[...] = jnp.where(lanes(QUARTER) < 64, mine, jnp.zeros_like(mine))
    for n in range(4):
        lse = y_ref[n * (QUARTER + 32) + QUARTER : (n + 1) * (QUARTER + 32), :].astype(F32)
        lse = (lse[16:24] + lse[8:16]) + lse[0:8]
        for part in range(8):
            at = n * QUARTER + part * 128
            lse_ref[:, at : at + 128] = jnp.broadcast_to(lse[part : part + 1, :], (8, 128))
        member = quarter_member(lens_ref, n // 2, n % 2)
        padded = jnp.concatenate([member, jnp.zeros((120, QUARTER), F32)], axis=0)
        member_s[:, n * QUARTER : (n + 1) * QUARTER] = padded.astype(BF16)

    def block(i, carry):
        rows = pl.ds(pl.multiple_of(i * BLOCK, BLOCK), BLOCK)
        sums = jnp.zeros((BLOCK, 128), F32)
        for n in range(4):
            cols = slice(n * QUARTER, (n + 1) * QUARTER)
            other = y_ref[n * (QUARTER + 32) : n * (QUARTER + 32) + QUARTER, :]
            scores = lax.dot_general(k_s[rows, :], other, NT, preferred_element_type=F32)
            prob = jnp.exp(scores - lse_ref[0:1, cols]).astype(BF16)
            sums = sums + lax.dot_general(
                prob, member_s[:, cols], NT, preferred_element_type=F32
            )
        for part in range(PARTS):
            mass_ref[i * PARTS + part] = jnp.transpose(sums[part * 128 : (part + 1) * 128])[0:8, :]
        return carry

    lax.fori_loop(0, QUARTER // BLOCK, block, 0)


def group_kernel(lens_ref, terms_ref, ready_ref, mass_ref, dattn_ref, grad_ref, loss_ref):
    sums = terms_ref[0]
    for n in range(1, 2 * PLANE):
        sums = sums + terms_ref[n]
    along = sums[8:16, 0:1]
    loss_ref[...] = sums[8:16, :] / QUERY_COUNT
    norms = ready_ref[16:24, :]
    raw = jnp.concatenate([sums[0:8, 0:64], sums[0:8, 0:64]], axis=1)
    dattn_ref[...] = (raw - ready_ref[0:8, :] * along) / norms / lengths_of(lens_ref)
    grad = (sums[0:8, 64:128] - ready_ref[8:16, 0:64] * along) / norms[:, 0:64]
    for z in range(PLANE):
        half = (z % 2) * HALF
        grad_ref[z] = jnp.concatenate([grad, mass_ref[z // 2, :, half : half + HALF]], axis=1)


def inputs_kernel(place_ref, lens_ref, parts_ref, means_ref, grad_inputs_ref, out_ref):
    grad = jnp.concatenate([parts_ref[z, :, 0:64] for z in range(PLANE)], axis=1)
    mine = local_member(lens_ref, place_ref[3])
    members = jnp.concatenate([mine, mine, mine, mine], axis=0).astype(BF16)
    grad_inputs_ref[...] = lax.dot_general(
        members, stacked(grad / lengths_of(lens_ref)[:, 0:1]), TN, preferred_element_type=F32
    ).astype(BF16)
    both = jnp.concatenate([grad, means_ref[...]], axis=1)
    out_ref[...] = jnp.concatenate([both, jnp.zeros_like(both)], axis=0).astype(BF16)


def value_kernel(lens_ref, parts_ref, w_ref, grad_v_ref):
    grad = jnp.concatenate([parts_ref[z, :, 0:64] for z in range(PLANE)], axis=1)
    grad = grad / lengths_of(lens_ref)[:, 0:1]
    dattn = folded(lax.dot_general(stacked(grad), w_ref[...], NT, preferred_element_type=F32))
    dattn = dattn.astype(BF16).astype(F32)
    dattn = jnp.concatenate([dattn, dattn, dattn, jnp.zeros_like(dattn)], axis=0).astype(BF16)
    for pair in range(HEAD_COUNT // 2):
        cols = slice(pair * 128, (pair + 1) * 128)
        both = []
        for head in (2 * pair, 2 * pair + 1):
            mass = jnp.concatenate(
                [parts_ref[2 * head, :, 64:128], parts_ref[2 * head + 1, :, 64:128]], axis=1
            )
            both.append(
                lax.dot_general(stacked(mass), dattn[:, cols], TN, preferred_element_type=F32)
            )
        grad_v_ref[:, cols] = jnp.where(lanes(ROWS) < 64, both[0], both[1]).astype(BF16)


def weight_kernel(in_ref, out_ref):
    out_ref[...] = lax.dot_general(
        in_ref[:, MODEL:], in_ref[:, :MODEL], TN, preferred_element_type=F32
    )


CHUNK = 512
TALL = 512


def row_kernel(place_ref, lens_ref, y_ref, lse_ref, x_ref, dattn_ref, out_ref, q_s, d_s, delta_s):
    lane = lanes(QUARTER)
    member = quarter_member(lens_ref, place_ref[0], place_ref[1]).astype(BF16)
    spread = lax.dot_general(
        member, dattn_ref[...].astype(BF16), TN, preferred_element_type=F32
    )
    spread = jnp.where(lane < 64, 0.0, spread)
    mine = y_ref[0:QUARTER, :]
    q_s[...] = jnp.where(lane < 64, mine, jnp.zeros_like(mine))
    d_s[...] = spread.astype(BF16)
    delta_s[...] = jnp.broadcast_to(
        jnp.sum(spread * mine.astype(F32), axis=1, keepdims=True), (QUARTER, 128)
    )

    def block(i, carry):
        rows = pl.ds(pl.multiple_of(i * TALL, TALL), TALL)
        columns = []
        for part in range(TALL // 128):
            line = lse_ref[pl.ds(i * (TALL // 128) + part, 1), :]
            columns.append(jnp.transpose(jnp.broadcast_to(line, (128, 128))))
        log_total = jnp.concatenate(columns, axis=0)[:, 0:1]
        delta = delta_s[rows, 0:1]
        total = jnp.zeros((TALL, 128), F32)
        for n in range(KEYS // CHUNK):
            part = x_ref[n * CHUNK : (n + 1) * CHUNK, :]
            scores = lax.dot_general(q_s[rows, :], part, NT, preferred_element_type=F32)
            prob_grad = lax.dot_general(d_s[rows, :], part, NT, preferred_element_type=F32)
            score_grad = (jnp.exp(scores - log_total) * (prob_grad - delta)).astype(BF16)
            total = total + jnp.dot(score_grad, part, preferred_element_type=F32)
        total = total * SCALE
        out_ref[rows, :] = jnp.concatenate([total[:, 0:64]] * 2, axis=1).astype(BF16)
        return carry

    lax.fori_loop(0, QUARTER // TALL, block, 0)


def column_kernel(
    lens_ref, own_ref, y_ref, lse_ref, dattn_ref, grad_q_ref, out_ref, y_s, k_s, v_s, delta_s
):
    lane = lanes(QUARTER)
    mine = own_ref[:, 0:64, :].reshape(QUARTER, 128)
    zero = jnp.zeros_like(mine)
    k_s[...] = jnp.where(lane < 64, mine, zero)
    v_s[...] = jnp.where(lane < 64, zero, mine)
    dattn = jnp.where(lanes(GROUPS) < 64, 0.0, dattn_ref[...]).astype(BF16)
    for n in range(4):
        rows = slice(n * QUARTER, (n + 1) * QUARTER)
        member = quarter_member(lens_ref, n // 2, n % 2)
        spread = lax.dot_general(member.astype(BF16), dattn, TN, preferred_element_type=F32)
        other = y_ref[n * (QUARTER + 32) : n * (QUARTER + 32) + QUARTER, :]
        y_s[rows, :] = jnp.where(lane < 64, other, spread.astype(BF16))
        products = lax.dot_general(dattn, other, NT, preferred_element_type=F32)
        delta_s[:, rows] = jnp.broadcast_to(
            jnp.sum(products * member, axis=0, keepdims=True), (8, QUARTER)
        )

    def block(i, carry):
        rows = pl.ds(pl.multiple_of(i * BLOCK, BLOCK), BLOCK)
        total = jnp.zeros((BLOCK, 128), F32)
        for n in range(KEYS // CHUNK):
            cols = slice(n * CHUNK, (n + 1) * CHUNK)
            part = y_s[cols, :]
            scores = lax.dot_general(k_s[rows, :], part, NT, preferred_element_type=F32)
            prob_grad = lax.dot_general(v_s[rows, :], part, NT, preferred_element_type=F32)
            score_grad = (
                jnp.exp(scores - lse_ref[0:1, cols]) * (prob_grad - delta_s[0:1, cols])
            ).astype(BF16)
            total = total + jnp.dot(score_grad, part, preferred_element_type=F32)
        both = jnp.where(lanes(BLOCK) < 64, total.astype(BF16), grad_q_ref[rows, :])
        count = BLOCK // HALF
        out_ref[pl.ds(i * count, count), :, :] = both.reshape(count, HALF, 128)
        return carry

    lax.fori_loop(0, QUARTER // BLOCK, block, 0)


SMEM = pl.BlockSpec(memory_space=pltpu.SMEM)
VMEM = pl.BlockSpec(memory_space=pltpu.VMEM)


def call(kernel, outs, scalars, arrays, scratch, estimate, name):
    return pl.pallas_call(
        kernel,
        out_shape=outs,
        in_specs=[SMEM] * len(scalars) + [VMEM] * len(arrays),
        out_specs=jax.tree.map(lambda _: VMEM, outs),
        scratch_shapes=scratch,
        compiler_params=params(),
        cost_estimate=estimate,
        name=name,
    )(*scalars, *arrays)


def shape(dims, dtype):
    return jax.ShapeDtypeStruct(dims, dtype)


def body(inputs, q_heads, k_heads, v_heads, w_out, group_lens, query_emb, positive):
    plane = lax.axis_index("yl")
    half = lax.axis_index("zd")
    head = lax.axis_index(HEADS)
    first = lax.axis_index(SEQ) * ROWS
    doc = lax.axis_index(GRP).reshape(1).astype(jnp.int32)
    place = jnp.stack([plane, half, head, first]).astype(jnp.int32)
    lengths = group_lens[0]
    exchange = functools.partial(lax.all_to_all, split_axis=0, concat_axis=0)
    barrier = lax.optimization_barrier
    pairs = QUARTER * KEYS

    packed = call(
        pack_kernel, shape((PLANE, 112, 128), BF16), (place, lengths),
        (q_heads[0], k_heads[0], v_heads[0], inputs[0]), (), cost(0, 1000000), "pack",
    )
    tagged = jnp.concatenate(
        [query_emb, jnp.pad(positive.astype(BF16)[:, None], ((0, 0), (0, 127)))], axis=1
    )
    packed, tagged = barrier((packed, tagged))
    own = exchange(packed, ZED)
    queries = gather_grp(tagged)
    own, queries = barrier((own, queries))
    keys = share(own[:, 0:64, :], SQUARE).reshape(KEYS, 128)

    mine, lse, means = call(
        forward_kernel,
        (
            shape((QUARTER + 32, 128), BF16),
            shape((8, 128), F32),
            shape((2 * PLANE, GROUPS, 128), F32),
        ),
        (place, lengths), (own, keys), [pltpu.VMEM((QUARTER, 128), BF16)],
        cost(pairs * 256 * 4, 3000000, pairs), "forward",
    )
    mine, means, queries = barrier((mine, means, queries))
    means = exchange(means, SEQ)
    around = [swap(mine, SQUARE, flip) for flip in (1, 2, 3)]
    query_rows = call(
        query_kernel, shape((16, 256), F32), (), (queries,), (), cost(6 * 2 * 8 * 256 * 1024, 600000),
        "queries",
    )
    means, query_rows, around = barrier((means, query_rows, around))
    pooled_own, doc_means, logits, sums = call(
        pool_kernel,
        (
            shape((GROUPS, MODEL), F32),
            shape((GROUPS, WIDTH), F32),
            shape((GROUPS, 256), F32),
            shape((DOCS, 8, 128), F32),
        ),
        (doc,), (means, w_out, queries, query_rows), (), cost(2 * 32 * 768 * 1024, 1800000), "pool",
    )
    sums = exchange(sums, GRP)
    square = [mine] + around
    rotated = [jnp.where(half == 0, square[n], square[n ^ 1]) for n in range(4)]
    ordered = [jnp.where(plane == 0, rotated[n], rotated[n ^ 2]) for n in range(4)]
    others = jnp.concatenate(ordered, axis=0)
    ready = call(
        prepare_kernel, shape((24, 128), F32), (place,), (pooled_own, w_out), (),
        cost(2 * 32 * 128 * 1024, 1200000), "prepare",
    )
    sums, others, ready = barrier((sums, others, ready))
    terms = call(
        loss_kernel, shape((2 * PLANE, 16, 128), F32), (doc,),
        (sums, logits, pooled_own, queries, query_rows, w_out), (),
        cost(2 * 32 * 768 * 1024, 1800000, 2000), "loss",
    )
    terms, own, others = barrier((terms, own, others))
    terms = exchange(terms, SEQ)
    mass, lse_rows = call(
        mass_kernel,
        (shape((GROUPS, 8, 128), F32), shape((8, KEYS), F32)),
        (lengths,), (own, others),
        [pltpu.VMEM((QUARTER, 128), BF16), pltpu.VMEM((128, KEYS), BF16)],
        cost(pairs * 256 * 4, 2500000, pairs), "mass",
    )
    terms, mass, lse_rows = barrier((terms, mass, lse_rows))

    dattn, grad_part, loss = call(
        group_kernel,
        (
            shape((GROUPS, 128), F32),
            shape((PLANE, GROUPS, 128), F32),
            shape((GROUPS, 128), F32),
        ),
        (lengths,), (terms, ready, mass), (), cost(0, 100000), "group",
    )
    mean_loss = loss[0, 64]
    grad_parts = exchange(grad_part, ZED)
    grad_rows = call(
        row_kernel, shape((QUARTER, 128), BF16), (place, lengths), (mine, lse, keys, dattn),
        [
            pltpu.VMEM((QUARTER, 128), BF16),
            pltpu.VMEM((QUARTER, 128), BF16),
            pltpu.VMEM((QUARTER, 128), F32),
        ],
        cost(pairs * 256 * 6, 2000000, pairs), "rows",
    )
    packed_grads = call(
        column_kernel, shape((PLANE, HALF, 128), BF16), (lengths,),
        (own, others, lse_rows, dattn, grad_rows),
        [
            pltpu.VMEM((KEYS, 128), BF16),
            pltpu.VMEM((QUARTER, 128), BF16),
            pltpu.VMEM((QUARTER, 128), BF16),
            pltpu.VMEM((8, KEYS), F32),
        ],
        cost(pairs * 256 * 6, 2500000, pairs), "columns",
    )
    packed_grads, grad_parts = barrier((packed_grads, grad_parts))
    grad_inputs, grads = call(
        inputs_kernel,
        (shape((ROWS, MODEL), BF16), shape((2 * GROUPS, MODEL + WIDTH), BF16)),
        (place, lengths), (grad_parts, doc_means), (), cost(2 * 32 * 128 * 1024, 1200000), "inputs",
    )
    home = exchange(packed_grads, ZED)
    all_grads = gather_grp(grads[0:GROUPS])
    out = shape((ROWS, WIDTH), BF16)
    grad_v = call(
        value_kernel, out, (lengths,), (grad_parts, w_out), (), cost(2 * 32 * 512 * 1024, 1300000),
        "values",
    )
    grad_w_out = call(
        weight_kernel, shape((WIDTH, MODEL), F32), (), (all_grads,), (),
        cost(2 * 128 * 512 * 1024, 2500000), "weights",
    )
    grad_q, grad_k = call(
        unpack_kernel, (out, out), (), (home,), (), cost(0, 500000), "unpack"
    )
    return (mean_loss, grad_inputs[None], grad_q[None], grad_k[None], grad_v[None], grad_w_out)


def solution(mesh):
    fine = Mesh(mesh.devices.reshape((2,) * 9), GRP + SEQ)
    rows = P(GRP, SEQ, None)
    return jax.shard_map(
        body,
        mesh=fine,
        in_specs=(
            rows,
            rows,
            rows,
            rows,
            P(),
            P(GRP, None),
            P(GRP + SEQ, None),
            P(GRP + SEQ),
        ),
        out_specs=(P(), rows, rows, rows, rows, P()),
        check_vma=False,
    )
```

```python
import functools

import jax
import jax.numpy as jnp
from jax import lax
from jax.experimental import pallas as pl
from jax.experimental.pallas import tpu as pltpu
from jax.sharding import Mesh, PartitionSpec as P

HEAD_COUNT = 8
HEAD_DIM = 64
GROUPS = 8
DOCS = 16
MODEL = 1024
WIDTH = 512
ROWS = 128
HALF = 64
QUARTER = 1024
PLANE = 16
SCALE = HEAD_DIM ** (-0.5)

RECIPROCAL_TEMP = 20.0
GRADIENT_FACTOR = 64.0
NORM_EPS = 1e-06
QUERY_COUNT = 8192
EXACT = lax.Precision.HIGHEST

BF16 = jnp.bfloat16
F32 = jnp.float32

GRP = ("yh", "xa", "xb", "co")
SEQ = ("yl", "za", "zb", "zc", "zd")
ZED = ("za", "zb", "zc", "zd")
SQUARE = ("yl", "zd")
HEADS = ("za", "zb", "zc")
NT = (((1,), (1,)), ((), ()))
TN = (((0,), (0,)), ((), ()))

HELD = 512


def params(large):
    return pltpu.CompilerParams(vmem_limit_bytes=(40 if large else 12) << 20)


def cost(flops, moved, exps=0):
    return pl.CostEstimate(flops=int(flops), bytes_accessed=int(moved), transcendentals=int(exps))


def share(value, axes):
    count = 2 ** len(axes)
    return lax.all_to_all(
        jnp.broadcast_to(value[None], (count,) + value.shape), axes, split_axis=0, concat_axis=0
    )


def swap(value, axes, flip):
    count = 2 ** len(axes)
    return lax.ppermute(value, axes, [(i, i ^ flip) for i in range(count)])


def gather(value, axes):
    for axis in axes:
        other = swap(value, (axis,), 1)
        first = lax.axis_index(axis) == 0
        value = jnp.where(
            first,
            jnp.concatenate([value, other], axis=0),
            jnp.concatenate([other, value], axis=0),
        )
    return value


def gather_pair(value, axes):
    square = [value] + [swap(value, axes, flip) for flip in (1, 2, 3)]
    low, high = lax.axis_index(axes[1]) == 0, lax.axis_index(axes[0]) == 0
    turned = [jnp.where(low, square[n], square[n ^ 1]) for n in range(4)]
    return jnp.concatenate([jnp.where(high, turned[n], turned[n ^ 2]) for n in range(4)], axis=0)


def three(value):
    high = value.astype(BF16)
    rest = value - high.astype(F32)
    middle = rest.astype(BF16)
    low = (rest - middle.astype(F32)).astype(BF16)
    return high, middle, low


def stacked(value):
    parts = [part.astype(F32) for part in three(value)]
    parts.append(jnp.zeros_like(value))
    return jnp.concatenate(parts, axis=0).astype(BF16)


def folded(product):
    return (product[16:24] + product[8:16]) + product[0:8]


def column_of(values):
    row = lax.broadcasted_iota(jnp.int32, (GROUPS, 128), 0)
    out = jnp.full((GROUPS, 128), values[0])
    for n in range(1, GROUPS):
        out = jnp.where(row == n, values[n], out)
    return out


def member_of(position, lens_ref):
    ends = [lens_ref[0]]
    for n in range(1, GROUPS):
        ends.append(ends[-1] + lens_ref[n])
    last = column_of(ends)
    first = last - column_of([lens_ref[n] for n in range(GROUPS)])
    return ((position >= first[:, 0:1]) & (position < last[:, 0:1])).astype(F32)


def lengths_of(lens_ref):
    return column_of([lens_ref[n] for n in range(GROUPS)]).astype(F32)


def quarter_member(lens_ref, plane, half):
    row = lax.broadcasted_iota(jnp.int32, (GROUPS, QUARTER), 1)
    position = plane * (PLANE * ROWS) + (row >> 6) * ROWS + half * HALF + (row & 63)
    return member_of(position, lens_ref)


def local_member(lens_ref, first):
    return member_of(first + lax.broadcasted_iota(jnp.int32, (GROUPS, ROWS), 1), lens_ref)


def halves(packed):
    return jnp.concatenate([packed[:, :, 0:64], packed[:, :, 64:128]], axis=1)


def lanes(rows):
    return lax.broadcasted_iota(jnp.int32, (rows, 128), 1)


def pack_kernel(place_ref, lens_ref, q_ref, k_ref, v_ref, inputs_ref, out_ref):
    mine = local_member(lens_ref, place_ref[3]).astype(BF16)
    sums = jnp.dot(mine, inputs_ref[...], preferred_element_type=F32)
    high, middle, low = [part.astype(F32) for part in three(sums)]
    zero = jnp.zeros((GROUPS, HALF), F32)
    for head in range(HEAD_COUNT):
        cols = slice(head * HEAD_DIM, (head + 1) * HEAD_DIM)
        for half in range(2):
            rows = slice(half * HALF, (half + 1) * HALF)
            place = 2 * head + half
            out_ref[place, 0:64, :] = jnp.concatenate([k_ref[rows, cols], v_ref[rows, cols]], axis=1)
            query = q_ref[rows, cols] * jnp.asarray(SCALE, BF16)
            out_ref[place, 64:96, :] = jnp.concatenate([query[0:32], query[32:64]], axis=1)
            part = slice(place * HALF, (place + 1) * HALF)
            upper = jnp.concatenate([high[:, part], middle[:, part]], axis=1)
            lower = jnp.concatenate([low[:, part], zero], axis=1)
            out_ref[place, 96:112, :] = jnp.concatenate([upper, lower], axis=0).astype(BF16)


def unpack_kernel(in_ref, q_ref, k_ref):
    for pair in range(HEAD_COUNT // 2):
        cols = slice(pair * 128, (pair + 1) * 128)
        for half in range(2):
            rows = slice(half * HALF, (half + 1) * HALF)
            first, second = in_ref[4 * pair + half], in_ref[4 * pair + 2 + half]
            k_ref[rows, cols] = jnp.concatenate([first[:, 0:64], second[:, 0:64]], axis=1)
            q_ref[rows, cols] = jnp.concatenate([first[:, 64:128], second[:, 64:128]], axis=1)


BLOCK = 256
PARTS = BLOCK // 128


KEYS = 4 * QUARTER


def forward_kernel(
    place_ref, lens_ref, own_ref, x_ref, y_ref, lse_ref, means_ref, q_s
):
    queries = halves(own_ref[:, 64:96, :]).reshape(QUARTER, HEAD_DIM)
    q_s[...] = jnp.concatenate([queries, jnp.zeros_like(queries)], axis=1)

    def block(i, carry):
        rows = pl.ds(pl.multiple_of(i * BLOCK, BLOCK), BLOCK)
        scores = lax.dot_general(q_s[rows, :], x_ref[...], NT, preferred_element_type=F32)
        top = jnp.max(scores, axis=1, keepdims=True)
        grown = jnp.exp(scores - top)
        total = jnp.sum(grown, axis=1, keepdims=True)
        prob = (grown * (1.0 / total)).astype(BF16)
        mixed = jnp.dot(prob, x_ref[...], preferred_element_type=F32).astype(BF16)
        y_ref[rows, :] = jnp.where(lanes(BLOCK) < 64, q_s[rows, :], mixed)
        log_total = top + jnp.log(total)
        for part in range(PARTS):
            square = jnp.broadcast_to(log_total[part * 128 : (part + 1) * 128], (128, 128))
            lse_ref[pl.ds(i * PARTS + part, 1), :] = jnp.transpose(square)[0:1, :]
        return carry

    lax.fori_loop(0, QUARTER // BLOCK, block, 0)
    y_ref[QUARTER : QUARTER + 32, :] = stacked(lse_ref[...])
    member = quarter_member(lens_ref, place_ref[0], place_ref[1]).astype(BF16)
    attn_sums = jnp.dot(member, y_ref[0:QUARTER, :], preferred_element_type=F32)
    sums = jnp.sum(own_ref[:, 96:112, :].astype(F32), axis=0)
    input_sums = (sums[0:8] + pltpu.roll(sums[0:8], 64, 1)) + sums[8:16]
    means_ref[...] = jnp.where(lanes(GROUPS) < 64, input_sums, attn_sums) / lengths_of(lens_ref)


def pool_kernel(doc_ref, means_ref, w_ref, query_ref, row_ref, own_ref, means_out_ref, logits_ref, out_ref):
    columns = [means_ref[z, :, 0:64] for z in range(PLANE)]
    heads = [
        means_ref[z, :, 64:128] + means_ref[z + 1, :, 64:128] for z in range(0, PLANE, 2)
    ]
    means = jnp.concatenate(heads, axis=1)
    projected = jnp.dot(stacked(means), w_ref[...], preferred_element_type=F32)
    pooled = jnp.concatenate(columns, axis=1) + folded(projected)
    own_ref[...] = pooled
    means_out_ref[...] = means
    unit = pooled / jnp.sqrt(jnp.sum(pooled * pooled, axis=1, keepdims=True) + NORM_EPS)
    logits = folded(
        lax.dot_general(stacked(unit), query_ref[:, :MODEL], NT, preferred_element_type=F32)
    )
    logits = logits * (RECIPROCAL_TEMP / row_ref[0:1, :])
    logits_ref[...] = logits
    group = doc_ref[0] * GROUPS + lax.broadcasted_iota(jnp.int32, logits.shape, 0)
    target = (group == row_ref[8:9, :].astype(jnp.int32)).astype(F32)
    total = jnp.sum(jnp.exp(logits), axis=0, keepdims=True)
    chosen = jnp.sum(target * logits, axis=0, keepdims=True)
    sums = jnp.concatenate(
        [row[:, n : n + 128] for row in (total, chosen) for n in range(0, HELD, 128)], axis=0
    )
    out_ref[...] = jnp.broadcast_to(sums[None], (DOCS, 8, 128))


def prepare_kernel(place_ref, pooled_ref, w_ref, out_ref):
    head = place_ref[2]
    pooled = pooled_ref[...]
    norms = jnp.sqrt(jnp.sum(pooled * pooled, axis=1, keepdims=True) + NORM_EPS)
    unit = pooled / norms
    w_head = w_ref[pl.ds(pl.multiple_of(head * HEAD_DIM, HEAD_DIM), HEAD_DIM), :]
    w_twice = jnp.concatenate([w_head, w_head], axis=0)
    out_ref[0:8, :] = folded(
        lax.dot_general(stacked(unit), w_twice, NT, preferred_element_type=F32)
    )
    z = 2 * head + place_ref[1]
    part = unit[:, 0:64]
    for n in range(1, PLANE):
        part = jnp.where(z == n, unit[:, n * HALF : (n + 1) * HALF], part)
    out_ref[8:16, :] = jnp.concatenate([part, part], axis=1)
    out_ref[16:24, :] = jnp.broadcast_to(norms, (GROUPS, 128))


def query_kernel(query_ref, out_ref):
    query = query_ref[:, :MODEL].astype(F32)
    squares = lax.dot_general(
        jnp.ones((8, MODEL), F32), query * query, NT, precision=EXACT, preferred_element_type=F32
    )
    out_ref[0:8, :] = jnp.sqrt(squares + NORM_EPS)
    out_ref[8:16, :] = lax.dot_general(
        jnp.ones((8, 128), BF16), query_ref[:, MODEL:], NT, preferred_element_type=F32
    )


def loss_kernel(doc_ref, sums_ref, logits_ref, own_ref, query_ref, row_ref, w_ref, out_ref):
    sums = sums_ref[0]
    for n in range(1, DOCS):
        sums = sums + sums_ref[n]
    total = jnp.concatenate([sums[n : n + 1] for n in range(4)], axis=1)
    losses = jnp.log(sums[0:4]) - sums[4:8]
    loss = jnp.sum(jnp.sum(losses, axis=1, keepdims=True), axis=0, keepdims=True)
    query = query_ref[:, :MODEL]
    scale = RECIPROCAL_TEMP / row_ref[0:1, :]
    logits = logits_ref[...]
    group = doc_ref[0] * GROUPS + lax.broadcasted_iota(jnp.int32, logits.shape, 0)
    target = (group == row_ref[8:9, :].astype(jnp.int32)).astype(F32)
    weight = (jnp.exp(logits) / total - target) * (GRADIENT_FACTOR * scale)
    grad = folded(jnp.dot(stacked(weight), query, preferred_element_type=F32))
    own = own_ref[...]
    own_unit = own / jnp.sqrt(jnp.sum(own * own, axis=1, keepdims=True) + NORM_EPS)
    along = jnp.sum(own_unit * grad, axis=1, keepdims=True)
    spread = folded(
        lax.dot_general(stacked(grad), w_ref[...], NT, preferred_element_type=F32)
    )
    extra = jnp.where(lanes(GROUPS) < 64, along, loss)
    for z in range(PLANE):
        head = z // 2
        chunk = jnp.concatenate(
            [
                spread[:, head * HEAD_DIM : (head + 1) * HEAD_DIM],
                grad[:, z * HALF : (z + 1) * HALF],
            ],
            axis=1,
        )
        out_ref[z, 0:8, :] = chunk
        out_ref[z, 8:16, :] = extra


def mass_kernel(lens_ref, own_ref, y_ref, mass_ref, lse_ref, k_s, member_s):
    mine = own_ref[:, 0:64, :].reshape(QUARTER, 128)
    k_s[...] = jnp.where(lanes(QUARTER) < 64, mine, jnp.zeros_like(mine))
    for n in range(4):
        lse = y_ref[n * (QUARTER + 32) + QUARTER : (n + 1) * (QUARTER + 32), :].astype(F32)
        lse = (lse[16:24] + lse[8:16]) + lse[0:8]
        for part in range(8):
            at = n * QUARTER + part * 128
            lse_ref[:, at : at + 128] = jnp.broadcast_to(lse[part : part + 1, :], (8, 128))
        member = quarter_member(lens_ref, n // 2, n % 2)
        padded = jnp.concatenate([member, jnp.zeros((120, QUARTER), F32)], axis=0)
        member_s[:, n * QUARTER : (n + 1) * QUARTER] = padded.astype(BF16)

    def block(i, carry):
        rows = pl.ds(pl.multiple_of(i * BLOCK, BLOCK), BLOCK)
        sums = jnp.zeros((BLOCK, 128), F32)
        for n in range(4):
            cols = slice(n * QUARTER, (n + 1) * QUARTER)
            other = y_ref[n * (QUARTER + 32) : n * (QUARTER + 32) + QUARTER, :]
            scores = lax.dot_general(k_s[rows, :], other, NT, preferred_element_type=F32)
            prob = jnp.exp(scores - lse_ref[0:1, cols]).astype(BF16)
            sums = sums + lax.dot_general(
                prob, member_s[:, cols], NT, preferred_element_type=F32
            )
        for part in range(PARTS):
            mass_ref[i * PARTS + part] = jnp.transpose(sums[part * 128 : (part + 1) * 128])[0:8, :]
        return carry

    lax.fori_loop(0, QUARTER // BLOCK, block, 0)


def group_kernel(lens_ref, terms_ref, ready_ref, mass_ref, dattn_ref, grad_ref, loss_ref):
    sums = terms_ref[0]
    for n in range(1, PLANE):
        sums = sums + terms_ref[n]
    along = sums[8:16, 0:1]
    loss_ref[...] = sums[8:16, :] / QUERY_COUNT
    norms = ready_ref[16:24, :]
    raw = jnp.concatenate([sums[0:8, 0:64], sums[0:8, 0:64]], axis=1)
    dattn_ref[...] = (raw - ready_ref[0:8, :] * along) / norms / lengths_of(lens_ref)
    grad = (sums[0:8, 64:128] - ready_ref[8:16, 0:64] * along) / norms[:, 0:64]
    for z in range(PLANE):
        half = (z % 2) * HALF
        grad_ref[z] = jnp.concatenate([grad, mass_ref[z // 2, :, half : half + HALF]], axis=1)


def inputs_kernel(place_ref, lens_ref, parts_ref, means_ref, grad_inputs_ref, out_ref):
    grad = jnp.concatenate([parts_ref[z, :, 0:64] for z in range(PLANE)], axis=1)
    mine = local_member(lens_ref, place_ref[3])
    members = jnp.concatenate([mine, mine, mine, mine], axis=0).astype(BF16)
    grad_inputs_ref[...] = lax.dot_general(
        members, stacked(grad / lengths_of(lens_ref)[:, 0:1]), TN, preferred_element_type=F32
    ).astype(BF16)
    both = jnp.concatenate([grad, means_ref[...]], axis=1)
    out_ref[...] = jnp.concatenate([both, jnp.zeros_like(both)], axis=0).astype(BF16)


def value_kernel(lens_ref, parts_ref, w_ref, grad_v_ref):
    grad = jnp.concatenate([parts_ref[z, :, 0:64] for z in range(PLANE)], axis=1)
    grad = grad / lengths_of(lens_ref)[:, 0:1]
    dattn = folded(lax.dot_general(stacked(grad), w_ref[...], NT, preferred_element_type=F32))
    dattn = dattn.astype(BF16).astype(F32)
    dattn = jnp.concatenate([dattn, dattn, dattn, jnp.zeros_like(dattn)], axis=0).astype(BF16)
    for pair in range(HEAD_COUNT // 2):
        cols = slice(pair * 128, (pair + 1) * 128)
        both = []
        for head in (2 * pair, 2 * pair + 1):
            mass = jnp.concatenate(
                [parts_ref[2 * head, :, 64:128], parts_ref[2 * head + 1, :, 64:128]], axis=1
            )
            both.append(
                lax.dot_general(stacked(mass), dattn[:, cols], TN, preferred_element_type=F32)
            )
        grad_v_ref[:, cols] = jnp.where(lanes(ROWS) < 64, both[0], both[1]).astype(BF16)


def weight_kernel(in_ref, out_ref):
    out_ref[...] = lax.dot_general(
        in_ref[:, MODEL:], in_ref[:, :MODEL], TN, preferred_element_type=F32
    )


CHUNK = 512
TALL = 512


def row_kernel(place_ref, lens_ref, y_ref, lse_ref, x_ref, dattn_ref, out_ref, q_s, d_s, delta_s):
    lane = lanes(QUARTER)
    member = quarter_member(lens_ref, place_ref[0], place_ref[1]).astype(BF16)
    spread = lax.dot_general(
        member, dattn_ref[...].astype(BF16), TN, preferred_element_type=F32
    )
    spread = jnp.where(lane < 64, 0.0, spread)
    mine = y_ref[0:QUARTER, :]
    q_s[...] = jnp.where(lane < 64, mine, jnp.zeros_like(mine))
    d_s[...] = spread.astype(BF16)
    delta_s[...] = jnp.broadcast_to(
        jnp.sum(spread * mine.astype(F32), axis=1, keepdims=True), (QUARTER, 128)
    )

    def block(i, carry):
        rows = pl.ds(pl.multiple_of(i * TALL, TALL), TALL)
        columns = []
        for part in range(TALL // 128):
            line = lse_ref[pl.ds(i * (TALL // 128) + part, 1), :]
            columns.append(jnp.transpose(jnp.broadcast_to(line, (128, 128))))
        log_total = jnp.concatenate(columns, axis=0)[:, 0:1]
        delta = delta_s[rows, 0:1]
        total = jnp.zeros((TALL, 128), F32)
        for n in range(KEYS // CHUNK):
            part = x_ref[n * CHUNK : (n + 1) * CHUNK, :]
            scores = lax.dot_general(q_s[rows, :], part, NT, preferred_element_type=F32)
            prob_grad = lax.dot_general(d_s[rows, :], part, NT, preferred_element_type=F32)
            score_grad = (jnp.exp(scores - log_total) * (prob_grad - delta)).astype(BF16)
            total = total + jnp.dot(score_grad, part, preferred_element_type=F32)
        total = total * SCALE
        out_ref[rows, :] = jnp.concatenate([total[:, 0:64]] * 2, axis=1).astype(BF16)
        return carry

    lax.fori_loop(0, QUARTER // TALL, block, 0)


def column_kernel(
    lens_ref, own_ref, y_ref, lse_ref, dattn_ref, grad_q_ref, out_ref, y_s, k_s, v_s, delta_s
):
    lane = lanes(QUARTER)
    mine = own_ref[:, 0:64, :].reshape(QUARTER, 128)
    zero = jnp.zeros_like(mine)
    k_s[...] = jnp.where(lane < 64, mine, zero)
    v_s[...] = jnp.where(lane < 64, zero, mine)
    dattn = jnp.where(lanes(GROUPS) < 64, 0.0, dattn_ref[...]).astype(BF16)
    for n in range(4):
        rows = slice(n * QUARTER, (n + 1) * QUARTER)
        member = quarter_member(lens_ref, n // 2, n % 2)
        spread = lax.dot_general(member.astype(BF16), dattn, TN, preferred_element_type=F32)
        other = y_ref[n * (QUARTER + 32) : n * (QUARTER + 32) + QUARTER, :]
        y_s[rows, :] = jnp.where(lane < 64, other, spread.astype(BF16))
        products = lax.dot_general(dattn, other, NT, preferred_element_type=F32)
        delta_s[:, rows] = jnp.broadcast_to(
            jnp.sum(products * member, axis=0, keepdims=True), (8, QUARTER)
        )

    def block(i, carry):
        rows = pl.ds(pl.multiple_of(i * BLOCK, BLOCK), BLOCK)
        total = jnp.zeros((BLOCK, 128), F32)
        for n in range(KEYS // CHUNK):
            cols = slice(n * CHUNK, (n + 1) * CHUNK)
            part = y_s[cols, :]
            scores = lax.dot_general(k_s[rows, :], part, NT, preferred_element_type=F32)
            prob_grad = lax.dot_general(v_s[rows, :], part, NT, preferred_element_type=F32)
            score_grad = (
                jnp.exp(scores - lse_ref[0:1, cols]) * (prob_grad - delta_s[0:1, cols])
            ).astype(BF16)
            total = total + jnp.dot(score_grad, part, preferred_element_type=F32)
        both = jnp.where(lanes(BLOCK) < 64, total.astype(BF16), grad_q_ref[rows, :])
        count = BLOCK // HALF
        out_ref[pl.ds(i * count, count), :, :] = both.reshape(count, HALF, 128)
        return carry

    lax.fori_loop(0, QUARTER // BLOCK, block, 0)


SMEM = pl.BlockSpec(memory_space=pltpu.SMEM)
VMEM = pl.BlockSpec(memory_space=pltpu.VMEM)


def call(kernel, outs, scalars, arrays, scratch, estimate, name):
    return pl.pallas_call(
        kernel,
        out_shape=outs,
        in_specs=[SMEM] * len(scalars) + [VMEM] * len(arrays),
        out_specs=jax.tree.map(lambda _: VMEM, outs),
        scratch_shapes=scratch,
        compiler_params=params(bool(scratch)),
        cost_estimate=estimate,
        name=name,
    )(*scalars, *arrays)


def shape(dims, dtype):
    return jax.ShapeDtypeStruct(dims, dtype)


def body(inputs, q_heads, k_heads, v_heads, w_out, group_lens, query_emb, positive):
    plane = lax.axis_index("yl")
    half = lax.axis_index("zd")
    head = lax.axis_index(HEADS)
    first = lax.axis_index(SEQ) * ROWS
    doc = lax.axis_index(GRP).reshape(1).astype(jnp.int32)
    place = jnp.stack([plane, half, head, first]).astype(jnp.int32)
    lengths = group_lens[0]
    exchange = functools.partial(lax.all_to_all, split_axis=0, concat_axis=0)
    barrier = lax.optimization_barrier
    pairs = QUARTER * KEYS

    packed = call(
        pack_kernel, shape((PLANE, 112, 128), BF16), (place, lengths),
        (q_heads[0], k_heads[0], v_heads[0], inputs[0]), (), cost(0, 1000000), "pack",
    )
    tagged = jnp.concatenate(
        [query_emb, jnp.pad(positive.astype(BF16)[:, None], ((0, 0), (0, 127)))], axis=1
    )
    packed, tagged = barrier((packed, tagged))
    own = exchange(packed, ZED)
    queries = gather(tagged, ("yh", "yl", "xa", "xb"))
    own, queries = barrier((own, queries))
    keys = share(own[:, 0:64, :], SQUARE).reshape(KEYS, 128)
    queries = gather(queries, ("co",))
    own, keys, queries = barrier((own, keys, queries))

    mine, lse, means = call(
        forward_kernel,
        (
            shape((QUARTER + 32, 128), BF16),
            shape((8, 128), F32),
            shape((GROUPS, 128), F32),
        ),
        (place, lengths), (own, keys), [pltpu.VMEM((QUARTER, 128), BF16)],
        cost(pairs * 256 * 4, 3000000, pairs), "forward",
    )
    means = means + swap(means, ("yl",), 1)
    means = jnp.broadcast_to(means[None], (PLANE, GROUPS, 128))
    mine, means, queries = barrier((mine, means, queries))
    means = exchange(means, ZED)
    around = [swap(mine, SQUARE, flip) for flip in (1, 2, 3)]
    query_rows = call(
        query_kernel, shape((16, HELD), F32), (), (queries,), (), cost(6 * 2 * 8 * HELD * 1024, 1200000),
        "queries",
    )
    means, query_rows, around = barrier((means, query_rows, around))
    pooled_own, doc_means, logits, sums = call(
        pool_kernel,
        (
            shape((GROUPS, MODEL), F32),
            shape((GROUPS, WIDTH), F32),
            shape((GROUPS, HELD), F32),
            shape((DOCS, 8, 128), F32),
        ),
        (doc,), (means, w_out, queries, query_rows), (), cost(2 * 32 * 768 * 1024, 1800000), "pool",
    )
    sums = exchange(sums, GRP)
    square = [mine] + around
    rotated = [jnp.where(half == 0, square[n], square[n ^ 1]) for n in range(4)]
    ordered = [jnp.where(plane == 0, rotated[n], rotated[n ^ 2]) for n in range(4)]
    others = jnp.concatenate(ordered, axis=0)
    ready = call(
        prepare_kernel, shape((24, 128), F32), (place,), (pooled_own, w_out), (),
        cost(2 * 32 * 128 * 1024, 1200000), "prepare",
    )
    sums, others, ready = barrier((sums, others, ready))
    terms = call(
        loss_kernel, shape((PLANE, 16, 128), F32), (doc,),
        (sums, logits, pooled_own, queries, query_rows, w_out), (),
        cost(2 * 32 * 768 * 1024, 1800000, 2000), "loss",
    )
    terms, own, others = barrier((terms, own, others))
    terms = exchange(terms, ZED)
    mass, lse_rows = call(
        mass_kernel,
        (shape((GROUPS, 8, 128), F32), shape((8, KEYS), F32)),
        (lengths,), (own, others),
        [pltpu.VMEM((QUARTER, 128), BF16), pltpu.VMEM((128, KEYS), BF16)],
        cost(pairs * 256 * 4, 2500000, pairs), "mass",
    )
    terms, mass, lse_rows = barrier((terms, mass, lse_rows))

    dattn, grad_part, loss = call(
        group_kernel,
        (
            shape((GROUPS, 128), F32),
            shape((PLANE, GROUPS, 128), F32),
            shape((GROUPS, 128), F32),
        ),
        (lengths,), (terms, ready, mass), (), cost(0, 100000), "group",
    )
    mean_loss = loss[0, 64]
    grad_parts = exchange(grad_part, ZED)
    grad_rows = call(
        row_kernel, shape((QUARTER, 128), BF16), (place, lengths), (mine, lse, keys, dattn),
        [
            pltpu.VMEM((QUARTER, 128), BF16),
            pltpu.VMEM((QUARTER, 128), BF16),
            pltpu.VMEM((QUARTER, 128), F32),
        ],
        cost(pairs * 256 * 6, 2000000, pairs), "rows",
    )
    packed_grads = call(
        column_kernel, shape((PLANE, HALF, 128), BF16), (lengths,),
        (own, others, lse_rows, dattn, grad_rows),
        [
            pltpu.VMEM((KEYS, 128), BF16),
            pltpu.VMEM((QUARTER, 128), BF16),
            pltpu.VMEM((QUARTER, 128), BF16),
            pltpu.VMEM((8, KEYS), F32),
        ],
        cost(pairs * 256 * 6, 2500000, pairs), "columns",
    )
    packed_grads, grad_parts = barrier((packed_grads, grad_parts))
    grad_inputs, grads = call(
        inputs_kernel,
        (shape((ROWS, MODEL), BF16), shape((2 * GROUPS, MODEL + WIDTH), BF16)),
        (place, lengths), (grad_parts, doc_means), (), cost(2 * 32 * 128 * 1024, 1200000), "inputs",
    )
    home = exchange(packed_grads, ZED)
    all_grads = gather_pair(gather_pair(grads[0:GROUPS], ("yh", "xa")), ("xb", "co"))
    out = shape((ROWS, WIDTH), BF16)
    grad_v = call(
        value_kernel, out, (lengths,), (grad_parts, w_out), (), cost(0, 0),
        "values",
    )
    grad_w_out = call(
        weight_kernel, shape((WIDTH, MODEL), F32), (), (all_grads,), (),
        cost(0, 0), "weights",
    )
    grad_q, grad_k = call(
        unpack_kernel, (out, out), (), (home,), (), cost(0, 0), "unpack"
    )
    return (mean_loss, grad_inputs[None], grad_q[None], grad_k[None], grad_v[None], grad_w_out)


def solution(mesh):
    fine = Mesh(mesh.devices.reshape((2,) * 9), GRP + SEQ)
    rows = P(GRP, SEQ, None)
    return jax.shard_map(
        body,
        mesh=fine,
        in_specs=(
            rows,
            rows,
            rows,
            rows,
            P(),
            P(GRP, None),
            P(GRP + SEQ, None),
            P(GRP + SEQ),
        ),
        out_specs=(P(), rows, rows, rows, rows, P()),
        check_vma=False,
    )
```

```python
import functools

import jax
import jax.numpy as jnp
from jax import lax
from jax.experimental import pallas as pl
from jax.experimental.pallas import tpu as pltpu
from jax.sharding import Mesh, PartitionSpec as P

HEAD_COUNT = 8
HEAD_DIM = 64
GROUPS = 8
DOCS = 16
MODEL = 1024
WIDTH = 512
ROWS = 128
HALF = 64
QUARTER = 1024
PLANE = 16
SCALE = HEAD_DIM ** (-0.5)

RECIPROCAL_TEMP = 20.0
GRADIENT_FACTOR = 64.0
NORM_EPS = 1e-06
QUERY_COUNT = 8192
EXACT = lax.Precision.HIGHEST

BF16 = jnp.bfloat16
F32 = jnp.float32

GRP = ("yh", "xa", "xb", "co")
SEQ = ("yl", "za", "zb", "zc", "zd")
ZED = ("za", "zb", "zc", "zd")
SQUARE = ("yl", "zd")
HEADS = ("za", "zb", "zc")
NT = (((1,), (1,)), ((), ()))
TN = (((0,), (0,)), ((), ()))

HELD = 512


def params(large):
    return pltpu.CompilerParams(vmem_limit_bytes=(40 if large else 12) << 20)


def cost(flops, moved, exps=0):
    return pl.CostEstimate(flops=int(flops), bytes_accessed=int(moved), transcendentals=int(exps))


def share(value, axes):
    count = 2 ** len(axes)
    return lax.all_to_all(
        jnp.broadcast_to(value[None], (count,) + value.shape), axes, split_axis=0, concat_axis=0
    )


def swap(value, axes, flip):
    count = 2 ** len(axes)
    return lax.ppermute(value, axes, [(i, i ^ flip) for i in range(count)])


def gather(value, axes):
    for axis in axes:
        other = swap(value, (axis,), 1)
        first = lax.axis_index(axis) == 0
        value = jnp.where(
            first,
            jnp.concatenate([value, other], axis=0),
            jnp.concatenate([other, value], axis=0),
        )
    return value


def three(value):
    high = value.astype(BF16)
    rest = value - high.astype(F32)
    middle = rest.astype(BF16)
    low = (rest - middle.astype(F32)).astype(BF16)
    return high, middle, low


def stacked(value):
    parts = [part.astype(F32) for part in three(value)]
    parts.append(jnp.zeros_like(value))
    return jnp.concatenate(parts, axis=0).astype(BF16)


def folded(product):
    return (product[16:24] + product[8:16]) + product[0:8]


def column_of(values):
    row = lax.broadcasted_iota(jnp.int32, (GROUPS, 128), 0)
    out = jnp.full((GROUPS, 128), values[0])
    for n in range(1, GROUPS):
        out = jnp.where(row == n, values[n], out)
    return out


def member_of(position, lens_ref):
    ends = [lens_ref[0]]
    for n in range(1, GROUPS):
        ends.append(ends[-1] + lens_ref[n])
    last = column_of(ends)
    first = last - column_of([lens_ref[n] for n in range(GROUPS)])
    return ((position >= first[:, 0:1]) & (position < last[:, 0:1])).astype(F32)


def lengths_of(lens_ref):
    return column_of([lens_ref[n] for n in range(GROUPS)]).astype(F32)


def quarter_member(lens_ref, plane, half):
    row = lax.broadcasted_iota(jnp.int32, (GROUPS, QUARTER), 1)
    position = plane * (PLANE * ROWS) + (row >> 6) * ROWS + half * HALF + (row & 63)
    return member_of(position, lens_ref)


def local_member(lens_ref, first):
    return member_of(first + lax.broadcasted_iota(jnp.int32, (GROUPS, ROWS), 1), lens_ref)


def halves(packed):
    return jnp.concatenate([packed[:, :, 0:64], packed[:, :, 64:128]], axis=1)


def lanes(rows):
    return lax.broadcasted_iota(jnp.int32, (rows, 128), 1)


def pack_kernel(place_ref, lens_ref, q_ref, k_ref, v_ref, inputs_ref, out_ref):
    mine = local_member(lens_ref, place_ref[3]).astype(BF16)
    sums = jnp.dot(mine, inputs_ref[...], preferred_element_type=F32)
    high, middle, low = [part.astype(F32) for part in three(sums)]
    zero = jnp.zeros((GROUPS, HALF), F32)
    for head in range(HEAD_COUNT):
        cols = slice(head * HEAD_DIM, (head + 1) * HEAD_DIM)
        for half in range(2):
            rows = slice(half * HALF, (half + 1) * HALF)
            place = 2 * head + half
            out_ref[place, 0:64, :] = jnp.concatenate([k_ref[rows, cols], v_ref[rows, cols]], axis=1)
            query = q_ref[rows, cols] * jnp.asarray(SCALE, BF16)
            out_ref[place, 64:96, :] = jnp.concatenate([query[0:32], query[32:64]], axis=1)
            part = slice(place * HALF, (place + 1) * HALF)
            upper = jnp.concatenate([high[:, part], middle[:, part]], axis=1)
            lower = jnp.concatenate([low[:, part], zero], axis=1)
            out_ref[place, 96:112, :] = jnp.concatenate([upper, lower], axis=0).astype(BF16)


def unpack_kernel(in_ref, q_ref, k_ref):
    for pair in range(HEAD_COUNT // 2):
        cols = slice(pair * 128, (pair + 1) * 128)
        for half in range(2):
            rows = slice(half * HALF, (half + 1) * HALF)
            first, second = in_ref[4 * pair + half], in_ref[4 * pair + 2 + half]
            k_ref[rows, cols] = jnp.concatenate([first[:, 0:64], second[:, 0:64]], axis=1)
            q_ref[rows, cols] = jnp.concatenate([first[:, 64:128], second[:, 64:128]], axis=1)


BLOCK = 256
PARTS = BLOCK // 128


KEYS = 4 * QUARTER


def forward_kernel(
    place_ref, lens_ref, own_ref, x_ref, y_ref, lse_ref, means_ref, q_s
):
    queries = halves(own_ref[:, 64:96, :]).reshape(QUARTER, HEAD_DIM)
    q_s[...] = jnp.concatenate([queries, jnp.zeros_like(queries)], axis=1)

    def block(i, carry):
        rows = pl.ds(pl.multiple_of(i * BLOCK, BLOCK), BLOCK)
        scores = lax.dot_general(q_s[rows, :], x_ref[...], NT, preferred_element_type=F32)
        top = jnp.max(scores, axis=1, keepdims=True)
        grown = jnp.exp(scores - top)
        total = jnp.sum(grown, axis=1, keepdims=True)
        prob = (grown * (1.0 / total)).astype(BF16)
        mixed = jnp.dot(prob, x_ref[...], preferred_element_type=F32).astype(BF16)
        y_ref[rows, :] = jnp.where(lanes(BLOCK) < 64, q_s[rows, :], mixed)
        log_total = top + jnp.log(total)
        for part in range(PARTS):
            square = jnp.broadcast_to(log_total[part * 128 : (part + 1) * 128], (128, 128))
            lse_ref[pl.ds(i * PARTS + part, 1), :] = jnp.transpose(square)[0:1, :]
        return carry

    lax.fori_loop(0, QUARTER // BLOCK, block, 0)
    y_ref[QUARTER : QUARTER + 32, :] = stacked(lse_ref[...])
    member = quarter_member(lens_ref, place_ref[0], place_ref[1]).astype(BF16)
    attn_sums = jnp.dot(member, y_ref[0:QUARTER, :], preferred_element_type=F32)
    sums = jnp.sum(own_ref[:, 96:112, :].astype(F32), axis=0)
    input_sums = (sums[0:8] + pltpu.roll(sums[0:8], 64, 1)) + sums[8:16]
    means = jnp.where(lanes(GROUPS) < 64, input_sums, attn_sums) / lengths_of(lens_ref)
    means_ref[...] = jnp.concatenate([means, means], axis=0)


def pool_kernel(doc_ref, means_ref, w_ref, query_ref, row_ref, own_ref, means_out_ref, logits_ref, out_ref):
    columns = [means_ref[z, 0:8, 0:64] for z in range(PLANE)]
    heads = [
        means_ref[z, 0:8, 64:128] + means_ref[z + 1, 0:8, 64:128] for z in range(0, PLANE, 2)
    ]
    means = jnp.concatenate(heads, axis=1)
    projected = jnp.dot(stacked(means), w_ref[...], preferred_element_type=F32)
    pooled = jnp.concatenate(columns, axis=1) + folded(projected)
    own_ref[...] = pooled
    means_out_ref[...] = means
    unit = pooled / jnp.sqrt(jnp.sum(pooled * pooled, axis=1, keepdims=True) + NORM_EPS)
    logits = folded(
        lax.dot_general(stacked(unit), query_ref[:, :MODEL], NT, preferred_element_type=F32)
    )
    logits = logits * (RECIPROCAL_TEMP / row_ref[0:1, :])
    logits_ref[...] = logits
    group = doc_ref[0] * GROUPS + lax.broadcasted_iota(jnp.int32, logits.shape, 0)
    target = (group == row_ref[8:9, :].astype(jnp.int32)).astype(F32)
    total = jnp.sum(jnp.exp(logits), axis=0, keepdims=True)
    chosen = jnp.sum(target * logits, axis=0, keepdims=True)
    sums = jnp.concatenate(
        [row[:, n : n + 128] for row in (total, chosen) for n in range(0, HELD, 128)], axis=0
    )
    out_ref[...] = jnp.broadcast_to(sums[None], (DOCS, 8, 128))


def prepare_kernel(place_ref, pooled_ref, w_ref, out_ref):
    head = place_ref[2]
    pooled = pooled_ref[...]
    norms = jnp.sqrt(jnp.sum(pooled * pooled, axis=1, keepdims=True) + NORM_EPS)
    unit = pooled / norms
    w_head = w_ref[pl.ds(pl.multiple_of(head * HEAD_DIM, HEAD_DIM), HEAD_DIM), :]
    w_twice = jnp.concatenate([w_head, w_head], axis=0)
    out_ref[0:8, :] = folded(
        lax.dot_general(stacked(unit), w_twice, NT, preferred_element_type=F32)
    )
    z = 2 * head + place_ref[1]
    part = unit[:, 0:64]
    for n in range(1, PLANE):
        part = jnp.where(z == n, unit[:, n * HALF : (n + 1) * HALF], part)
    out_ref[8:16, :] = jnp.concatenate([part, part], axis=1)
    out_ref[16:24, :] = jnp.broadcast_to(norms, (GROUPS, 128))


def query_kernel(query_ref, out_ref):
    query = query_ref[:, :MODEL].astype(F32)
    squares = lax.dot_general(
        jnp.ones((8, MODEL), F32), query * query, NT, precision=EXACT, preferred_element_type=F32
    )
    out_ref[0:8, :] = jnp.sqrt(squares + NORM_EPS)
    out_ref[8:16, :] = lax.dot_general(
        jnp.ones((8, 128), BF16), query_ref[:, MODEL:], NT, preferred_element_type=F32
    )


def loss_kernel(doc_ref, sums_ref, logits_ref, own_ref, query_ref, row_ref, w_ref, out_ref):
    sums = sums_ref[0]
    for n in range(1, DOCS):
        sums = sums + sums_ref[n]
    total = jnp.concatenate([sums[n : n + 1] for n in range(4)], axis=1)
    losses = jnp.log(sums[0:4]) - sums[4:8]
    loss = jnp.sum(jnp.sum(losses, axis=1, keepdims=True), axis=0, keepdims=True)
    query = query_ref[:, :MODEL]
    scale = RECIPROCAL_TEMP / row_ref[0:1, :]
    logits = logits_ref[...]
    group = doc_ref[0] * GROUPS + lax.broadcasted_iota(jnp.int32, logits.shape, 0)
    target = (group == row_ref[8:9, :].astype(jnp.int32)).astype(F32)
    weight = (jnp.exp(logits) / total - target) * (GRADIENT_FACTOR * scale)
    grad = folded(jnp.dot(stacked(weight), query, preferred_element_type=F32))
    own = own_ref[...]
    own_unit = own / jnp.sqrt(jnp.sum(own * own, axis=1, keepdims=True) + NORM_EPS)
    along = jnp.sum(own_unit * grad, axis=1, keepdims=True)
    spread = folded(
        lax.dot_general(stacked(grad), w_ref[...], NT, preferred_element_type=F32)
    )
    extra = jnp.where(lanes(GROUPS) < 64, along, loss)
    for z in range(PLANE):
        head = z // 2
        chunk = jnp.concatenate(
            [
                spread[:, head * HEAD_DIM : (head + 1) * HEAD_DIM],
                grad[:, z * HALF : (z + 1) * HALF],
            ],
            axis=1,
        )
        out_ref[z, 0:8, :] = chunk
        out_ref[z, 8:16, :] = extra


def mass_kernel(lens_ref, own_ref, y_ref, mass_ref, lse_ref, k_s, member_s):
    mine = own_ref[:, 0:64, :].reshape(QUARTER, 128)
    k_s[...] = jnp.where(lanes(QUARTER) < 64, mine, jnp.zeros_like(mine))
    for n in range(4):
        lse = y_ref[n * (QUARTER + 32) + QUARTER : (n + 1) * (QUARTER + 32), :].astype(F32)
        lse = (lse[16:24] + lse[8:16]) + lse[0:8]
        for part in range(8):
            at = n * QUARTER + part * 128
            lse_ref[:, at : at + 128] = jnp.broadcast_to(lse[part : part + 1, :], (8, 128))
        member = quarter_member(lens_ref, n // 2, n % 2)
        padded = jnp.concatenate([member, jnp.zeros((120, QUARTER), F32)], axis=0)
        member_s[:, n * QUARTER : (n + 1) * QUARTER] = padded.astype(BF16)

    def block(i, carry):
        rows = pl.ds(pl.multiple_of(i * BLOCK, BLOCK), BLOCK)
        sums = jnp.zeros((BLOCK, 128), F32)
        for n in range(4):
            cols = slice(n * QUARTER, (n + 1) * QUARTER)
            other = y_ref[n * (QUARTER + 32) : n * (QUARTER + 32) + QUARTER, :]
            scores = lax.dot_general(k_s[rows, :], other, NT, preferred_element_type=F32)
            prob = jnp.exp(scores - lse_ref[0:1, cols]).astype(BF16)
            sums = sums + lax.dot_general(
                prob, member_s[:, cols], NT, preferred_element_type=F32
            )
        for part in range(PARTS):
            mass_ref[i * PARTS + part] = jnp.transpose(sums[part * 128 : (part + 1) * 128])[0:8, :]
        return carry

    lax.fori_loop(0, QUARTER // BLOCK, block, 0)


def group_kernel(lens_ref, terms_ref, ready_ref, mass_ref, dattn_ref, grad_ref, loss_ref):
    sums = terms_ref[0]
    for n in range(1, PLANE):
        sums = sums + terms_ref[n]
    along = sums[8:16, 0:1]
    loss_ref[...] = sums[8:16, :] / QUERY_COUNT
    norms = ready_ref[16:24, :]
    raw = jnp.concatenate([sums[0:8, 0:64], sums[0:8, 0:64]], axis=1)
    dattn_ref[...] = (raw - ready_ref[0:8, :] * along) / norms / lengths_of(lens_ref)
    grad = (sums[0:8, 64:128] - ready_ref[8:16, 0:64] * along) / norms[:, 0:64]
    for z in range(PLANE):
        half = (z % 2) * HALF
        grad_ref[z] = jnp.concatenate([grad, mass_ref[z // 2, :, half : half + HALF]], axis=1)


def inputs_kernel(place_ref, lens_ref, parts_ref, means_ref, grad_inputs_ref, out_ref):
    grad = jnp.concatenate([parts_ref[z, :, 0:64] for z in range(PLANE)], axis=1)
    mine = local_member(lens_ref, place_ref[3])
    members = jnp.concatenate([mine, mine, mine, mine], axis=0).astype(BF16)
    grad_inputs_ref[...] = lax.dot_general(
        members, stacked(grad / lengths_of(lens_ref)[:, 0:1]), TN, preferred_element_type=F32
    ).astype(BF16)
    both = jnp.concatenate([grad, means_ref[...]], axis=1)
    wide = (MODEL + WIDTH) // 2
    both = jnp.concatenate([both[:, :wide], both[:, wide:]], axis=0)
    out_ref[...] = jnp.broadcast_to(both.astype(BF16)[None], (DOCS, 2 * GROUPS, wide))


def value_kernel(lens_ref, parts_ref, w_ref, grad_v_ref):
    grad = jnp.concatenate([parts_ref[z, :, 0:64] for z in range(PLANE)], axis=1)
    grad = grad / lengths_of(lens_ref)[:, 0:1]
    dattn = folded(lax.dot_general(stacked(grad), w_ref[...], NT, preferred_element_type=F32))
    dattn = dattn.astype(BF16).astype(F32)
    dattn = jnp.concatenate([dattn, dattn, dattn, jnp.zeros_like(dattn)], axis=0).astype(BF16)
    for pair in range(HEAD_COUNT // 2):
        cols = slice(pair * 128, (pair + 1) * 128)
        both = []
        for head in (2 * pair, 2 * pair + 1):
            mass = jnp.concatenate(
                [parts_ref[2 * head, :, 64:128], parts_ref[2 * head + 1, :, 64:128]], axis=1
            )
            both.append(
                lax.dot_general(stacked(mass), dattn[:, cols], TN, preferred_element_type=F32)
            )
        grad_v_ref[:, cols] = jnp.where(lanes(ROWS) < 64, both[0], both[1]).astype(BF16)


def weight_kernel(in_ref, out_ref):
    wide = (MODEL + WIDTH) // 2
    both = in_ref[...].astype(F32)
    both = [both[:, n : n + 8].reshape(DOCS * GROUPS, wide) for n in (0, 8)]
    both = jnp.concatenate(both, axis=1).astype(BF16)
    out_ref[...] = lax.dot_general(
        both[:, MODEL:], both[:, :MODEL], TN, preferred_element_type=F32
    )


CHUNK = 512
TALL = 512


def row_kernel(
    place_ref, lens_ref, y_ref, lse_ref, x_ref, dattn_ref, grad_k_ref, out_ref, q_s, d_s, delta_s
):
    lane = lanes(QUARTER)
    member = quarter_member(lens_ref, place_ref[0], place_ref[1]).astype(BF16)
    spread = lax.dot_general(
        member, dattn_ref[...].astype(BF16), TN, preferred_element_type=F32
    )
    spread = jnp.where(lane < 64, 0.0, spread)
    mine = y_ref[0:QUARTER, :]
    q_s[...] = jnp.where(lane < 64, mine, jnp.zeros_like(mine))
    d_s[...] = spread.astype(BF16)
    delta_s[...] = jnp.broadcast_to(
        jnp.sum(spread * mine.astype(F32), axis=1, keepdims=True), (QUARTER, 128)
    )

    def block(i, carry):
        rows = pl.ds(pl.multiple_of(i * TALL, TALL), TALL)
        columns = []
        for part in range(TALL // 128):
            line = lse_ref[pl.ds(i * (TALL // 128) + part, 1), :]
            columns.append(jnp.transpose(jnp.broadcast_to(line, (128, 128))))
        log_total = jnp.concatenate(columns, axis=0)[:, 0:1]
        delta = delta_s[rows, 0:1]
        total = jnp.zeros((TALL, 128), F32)
        for n in range(KEYS // CHUNK):
            part = x_ref[n * CHUNK : (n + 1) * CHUNK, :]
            scores = lax.dot_general(q_s[rows, :], part, NT, preferred_element_type=F32)
            prob_grad = lax.dot_general(d_s[rows, :], part, NT, preferred_element_type=F32)
            score_grad = (jnp.exp(scores - log_total) * (prob_grad - delta)).astype(BF16)
            total = total + jnp.dot(score_grad, part, preferred_element_type=F32)
        total = total * SCALE
        total = jnp.concatenate([total[:, 0:64]] * 2, axis=1).astype(BF16)
        both = jnp.where(lanes(TALL) < 64, grad_k_ref[rows, :], total)
        count = TALL // HALF
        out_ref[pl.ds(i * count, count), :, :] = both.reshape(count, HALF, 128)
        return carry

    lax.fori_loop(0, QUARTER // TALL, block, 0)


def column_kernel(
    lens_ref, own_ref, y_ref, lse_ref, dattn_ref, out_ref, y_s, k_s, v_s, delta_s
):
    lane = lanes(QUARTER)
    mine = own_ref[:, 0:64, :].reshape(QUARTER, 128)
    zero = jnp.zeros_like(mine)
    k_s[...] = jnp.where(lane < 64, mine, zero)
    v_s[...] = jnp.where(lane < 64, zero, mine)
    dattn = jnp.where(lanes(GROUPS) < 64, 0.0, dattn_ref[...]).astype(BF16)
    for n in range(4):
        rows = slice(n * QUARTER, (n + 1) * QUARTER)
        member = quarter_member(lens_ref, n // 2, n % 2)
        spread = lax.dot_general(member.astype(BF16), dattn, TN, preferred_element_type=F32)
        other = y_ref[n * (QUARTER + 32) : n * (QUARTER + 32) + QUARTER, :]
        y_s[rows, :] = jnp.where(lane < 64, other, spread.astype(BF16))
        products = lax.dot_general(dattn, other, NT, preferred_element_type=F32)
        delta_s[:, rows] = jnp.broadcast_to(
            jnp.sum(products * member, axis=0, keepdims=True), (8, QUARTER)
        )

    def block(i, carry):
        rows = pl.ds(pl.multiple_of(i * BLOCK, BLOCK), BLOCK)
        total = jnp.zeros((BLOCK, 128), F32)
        for n in range(KEYS // CHUNK):
            cols = slice(n * CHUNK, (n + 1) * CHUNK)
            part = y_s[cols, :]
            scores = lax.dot_general(k_s[rows, :], part, NT, preferred_element_type=F32)
            prob_grad = lax.dot_general(v_s[rows, :], part, NT, preferred_element_type=F32)
            score_grad = (
                jnp.exp(scores - lse_ref[0:1, cols]) * (prob_grad - delta_s[0:1, cols])
            ).astype(BF16)
            total = total + jnp.dot(score_grad, part, preferred_element_type=F32)
        out_ref[rows, :] = total.astype(BF16)
        return carry

    lax.fori_loop(0, QUARTER // BLOCK, block, 0)


SMEM = pl.BlockSpec(memory_space=pltpu.SMEM)
VMEM = pl.BlockSpec(memory_space=pltpu.VMEM)


def call(kernel, outs, scalars, arrays, scratch, estimate, name):
    return pl.pallas_call(
        kernel,
        out_shape=outs,
        in_specs=[SMEM] * len(scalars) + [VMEM] * len(arrays),
        out_specs=jax.tree.map(lambda _: VMEM, outs),
        scratch_shapes=scratch,
        compiler_params=params(bool(scratch) or name == "pack"),
        cost_estimate=estimate,
        name=name,
    )(*scalars, *arrays)


def shape(dims, dtype):
    return jax.ShapeDtypeStruct(dims, dtype)


def body(inputs, q_heads, k_heads, v_heads, w_out, group_lens, query_emb, positive):
    plane = lax.axis_index("yl")
    half = lax.axis_index("zd")
    head = lax.axis_index(HEADS)
    first = lax.axis_index(SEQ) * ROWS
    doc = lax.axis_index(GRP).reshape(1).astype(jnp.int32)
    place = jnp.stack([plane, half, head, first]).astype(jnp.int32)
    lengths = group_lens[0]
    exchange = functools.partial(lax.all_to_all, split_axis=0, concat_axis=0)
    barrier = lax.optimization_barrier
    pairs = QUARTER * KEYS

    packed = call(
        pack_kernel, shape((PLANE, 112, 128), BF16), (place, lengths),
        (q_heads[0], k_heads[0], v_heads[0], inputs[0]), (), cost(0, 1000000), "pack",
    )
    tagged = jnp.concatenate(
        [query_emb, jnp.pad(positive.astype(BF16)[:, None], ((0, 0), (0, 127)))], axis=1
    )
    packed, tagged = barrier((packed, tagged))
    own = exchange(packed, ZED)
    queries = gather(tagged, ("yh", "yl", "xa"))
    own, queries = barrier((own, queries))
    keys = share(own[:, 0:64, :], SQUARE).reshape(KEYS, 128)
    queries = gather(queries, ("xb", "co"))
    own, keys, queries = barrier((own, keys, queries))

    mine, lse, means = call(
        forward_kernel,
        (
            shape((QUARTER + 32, 128), BF16),
            shape((8, 128), F32),
            shape((2 * GROUPS, 128), F32),
        ),
        (place, lengths), (own, keys), [pltpu.VMEM((QUARTER, 128), BF16)],
        cost(pairs * 256 * 4, 3000000, pairs), "forward",
    )
    means = means + swap(means, ("yl",), 1)
    means = jnp.broadcast_to(means[None], (PLANE, 2 * GROUPS, 128))
    mine, means, queries = barrier((mine, means, queries))
    means = exchange(means, ZED)
    around = [swap(mine, SQUARE, flip) for flip in (1, 2, 3)]
    query_rows = call(
        query_kernel, shape((16, HELD), F32), (), (queries,), (), cost(6 * 2 * 8 * HELD * 1024, 1200000),
        "queries",
    )
    means, query_rows, around = barrier((means, query_rows, around))
    pooled_own, doc_means, logits, sums = call(
        pool_kernel,
        (
            shape((GROUPS, MODEL), F32),
            shape((GROUPS, WIDTH), F32),
            shape((GROUPS, HELD), F32),
            shape((DOCS, 8, 128), F32),
        ),
        (doc,), (means, w_out, queries, query_rows), (), cost(2 * 32 * 768 * 1024, 1800000), "pool",
    )
    sums = exchange(sums, GRP)
    square = [mine] + around
    rotated = [jnp.where(half == 0, square[n], square[n ^ 1]) for n in range(4)]
    ordered = [jnp.where(plane == 0, rotated[n], rotated[n ^ 2]) for n in range(4)]
    others = jnp.concatenate(ordered, axis=0)
    ready = call(
        prepare_kernel, shape((24, 128), F32), (place,), (pooled_own, w_out), (),
        cost(2 * 32 * 128 * 1024, 1200000), "prepare",
    )
    sums, others, ready = barrier((sums, others, ready))
    terms = call(
        loss_kernel, shape((PLANE, 16, 128), F32), (doc,),
        (sums, logits, pooled_own, queries, query_rows, w_out), (),
        cost(2 * 32 * 768 * 1024, 1800000, 2000), "loss",
    )
    terms, own, others = barrier((terms, own, others))
    terms = exchange(terms, ZED)
    mass, lse_rows = call(
        mass_kernel,
        (shape((GROUPS, 8, 128), F32), shape((8, KEYS), F32)),
        (lengths,), (own, others),
        [pltpu.VMEM((QUARTER, 128), BF16), pltpu.VMEM((128, KEYS), BF16)],
        cost(pairs * 256 * 4, 2500000, pairs), "mass",
    )
    terms, mass, lse_rows = barrier((terms, mass, lse_rows))

    dattn, grad_part, loss = call(
        group_kernel,
        (
            shape((GROUPS, 128), F32),
            shape((PLANE, GROUPS, 128), F32),
            shape((GROUPS, 128), F32),
        ),
        (lengths,), (terms, ready, mass), (), cost(0, 100000), "group",
    )
    mean_loss = loss[0, 64]
    grad_parts = exchange(grad_part, ZED)
    grad_columns = call(
        column_kernel, shape((QUARTER, 128), BF16), (lengths,),
        (own, others, lse_rows, dattn),
        [
            pltpu.VMEM((KEYS, 128), BF16),
            pltpu.VMEM((QUARTER, 128), BF16),
            pltpu.VMEM((QUARTER, 128), BF16),
            pltpu.VMEM((8, KEYS), F32),
        ],
        cost(pairs * 256 * 6, 2500000, pairs), "columns",
    )
    grad_inputs, grads = call(
        inputs_kernel,
        (shape((ROWS, MODEL), BF16), shape((DOCS, 2 * GROUPS, (MODEL + WIDTH) // 2), BF16)),
        (place, lengths), (grad_parts, doc_means), (), cost(2 * 32 * 128 * 1024, 1200000), "inputs",
    )
    grad_columns, grads = barrier((grad_columns, grads))
    all_grads = exchange(grads, GRP)
    packed_grads = call(
        row_kernel, shape((PLANE, HALF, 128), BF16), (place, lengths),
        (mine, lse, keys, dattn, grad_columns),
        [
            pltpu.VMEM((QUARTER, 128), BF16),
            pltpu.VMEM((QUARTER, 128), BF16),
            pltpu.VMEM((QUARTER, 128), F32),
        ],
        cost(pairs * 256 * 6, 2000000, pairs), "rows",
    )
    packed_grads, grad_parts = barrier((packed_grads, grad_parts))
    home = exchange(packed_grads, ZED)
    out = shape((ROWS, WIDTH), BF16)
    grad_v = call(
        value_kernel, out, (lengths,), (grad_parts, w_out), (), cost(2 * 32 * 512 * 1024, 1300000),
        "values",
    )
    grad_w_out = call(
        weight_kernel, shape((WIDTH, MODEL), F32), (), (all_grads,), (),
        cost(2 * 384 * 512 * 1024, 3000000), "weights",
    )
    grad_q, grad_k = call(
        unpack_kernel, (out, out), (), (home,), (), cost(0, 500000), "unpack"
    )
    return (mean_loss, grad_inputs[None], grad_q[None], grad_k[None], grad_v[None], grad_w_out)


def solution(mesh):
    fine = Mesh(mesh.devices.reshape((2,) * 9), GRP + SEQ)
    rows = P(GRP, SEQ, None)
    return jax.shard_map(
        body,
        mesh=fine,
        in_specs=(
            rows,
            rows,
            rows,
            rows,
            P(),
            P(GRP, None),
            P(GRP + SEQ, None),
            P(GRP + SEQ),
        ),
        out_specs=(P(), rows, rows, rows, rows, P()),
        check_vma=False,
    )
```

```python
import functools

import jax
import jax.numpy as jnp
from jax import lax
from jax.experimental import pallas as pl
from jax.experimental.pallas import tpu as pltpu
from jax.sharding import Mesh, PartitionSpec as P

HEAD_COUNT = 8
HEAD_DIM = 64
GROUPS = 8
DOCS = 16
MODEL = 1024
WIDTH = 512
ROWS = 128
HALF = 64
QUARTER = 1024
PLANE = 16
SCALE = HEAD_DIM ** (-0.5)

RECIPROCAL_TEMP = 20.0
GRADIENT_FACTOR = 64.0
NORM_EPS = 1e-06
QUERY_COUNT = 8192
EXACT = lax.Precision.HIGHEST

BF16 = jnp.bfloat16
F32 = jnp.float32

GRP = ("yh", "xa", "xb", "co")
SEQ = ("yl", "za", "zb", "zc", "zd")
ZED = ("za", "zb", "zc", "zd")
SQUARE = ("yl", "zd")
HEADS = ("za", "zb", "zc")
NT = (((1,), (1,)), ((), ()))
TN = (((0,), (0,)), ((), ()))

HELD = 512


def params(mebibytes):
    return pltpu.CompilerParams(vmem_limit_bytes=mebibytes << 20)


def cost(flops, moved, exps=0):
    return pl.CostEstimate(flops=int(flops), bytes_accessed=int(moved), transcendentals=int(exps))


def share(value, axes):
    count = 2 ** len(axes)
    return lax.all_to_all(
        jnp.broadcast_to(value[None], (count,) + value.shape), axes, split_axis=0, concat_axis=0
    )


def swap(value, axes, flip):
    count = 2 ** len(axes)
    return lax.ppermute(value, axes, [(i, i ^ flip) for i in range(count)])


def gather(value, axes):
    for axis in axes:
        other = swap(value, (axis,), 1)
        first = lax.axis_index(axis) == 0
        value = jnp.where(
            first,
            jnp.concatenate([value, other], axis=0),
            jnp.concatenate([other, value], axis=0),
        )
    return value


def three(value):
    high = value.astype(BF16)
    rest = value - high.astype(F32)
    middle = rest.astype(BF16)
    low = (rest - middle.astype(F32)).astype(BF16)
    return high, middle, low


def stacked(value):
    parts = [part.astype(F32) for part in three(value)]
    parts.append(jnp.zeros_like(value))
    return jnp.concatenate(parts, axis=0).astype(BF16)


def folded(product):
    return (product[16:24] + product[8:16]) + product[0:8]


def column_of(values):
    row = lax.broadcasted_iota(jnp.int32, (GROUPS, 128), 0)
    out = jnp.full((GROUPS, 128), values[0])
    for n in range(1, GROUPS):
        out = jnp.where(row == n, values[n], out)
    return out


def member_of(position, lens_ref):
    ends = [lens_ref[0]]
    for n in range(1, GROUPS):
        ends.append(ends[-1] + lens_ref[n])
    last = column_of(ends)
    first = last - column_of([lens_ref[n] for n in range(GROUPS)])
    return ((position >= first[:, 0:1]) & (position < last[:, 0:1])).astype(F32)


def lengths_of(lens_ref):
    return column_of([lens_ref[n] for n in range(GROUPS)]).astype(F32)


def quarter_member(lens_ref, plane, half):
    row = lax.broadcasted_iota(jnp.int32, (GROUPS, QUARTER), 1)
    position = plane * (PLANE * ROWS) + (row >> 6) * ROWS + half * HALF + (row & 63)
    return member_of(position, lens_ref)


def local_member(lens_ref, first):
    return member_of(first + lax.broadcasted_iota(jnp.int32, (GROUPS, ROWS), 1), lens_ref)


def halves(packed):
    return jnp.concatenate([packed[:, :, 0:64], packed[:, :, 64:128]], axis=1)


def lanes(rows):
    return lax.broadcasted_iota(jnp.int32, (rows, 128), 1)


def pack_kernel(place_ref, lens_ref, q_ref, k_ref, v_ref, inputs_ref, out_ref):
    mine = local_member(lens_ref, place_ref[3]).astype(BF16)
    sums = jnp.dot(mine, inputs_ref[...], preferred_element_type=F32)
    high, middle, low = [part.astype(F32) for part in three(sums)]
    zero = jnp.zeros((GROUPS, HALF), F32)
    for head in range(HEAD_COUNT):
        cols = slice(head * HEAD_DIM, (head + 1) * HEAD_DIM)
        for half in range(2):
            rows = slice(half * HALF, (half + 1) * HALF)
            place = 2 * head + half
            out_ref[place, 0:64, :] = jnp.concatenate([k_ref[rows, cols], v_ref[rows, cols]], axis=1)
            query = q_ref[rows, cols] * jnp.asarray(SCALE, BF16)
            out_ref[place, 64:96, :] = jnp.concatenate([query[0:32], query[32:64]], axis=1)
            part = slice(place * HALF, (place + 1) * HALF)
            upper = jnp.concatenate([high[:, part], middle[:, part]], axis=1)
            lower = jnp.concatenate([low[:, part], zero], axis=1)
            out_ref[place, 96:112, :] = jnp.concatenate([upper, lower], axis=0).astype(BF16)


def unpack_kernel(in_ref, q_ref, k_ref):
    for pair in range(HEAD_COUNT // 2):
        cols = slice(pair * 128, (pair + 1) * 128)
        for half in range(2):
            rows = slice(half * HALF, (half + 1) * HALF)
            first, second = in_ref[4 * pair + half], in_ref[4 * pair + 2 + half]
            k_ref[rows, cols] = jnp.concatenate([first[:, 0:64], second[:, 0:64]], axis=1)
            q_ref[rows, cols] = jnp.concatenate([first[:, 64:128], second[:, 64:128]], axis=1)


BLOCK = 256
PARTS = BLOCK // 128


KEYS = 4 * QUARTER
SPARE = 544


def forward_kernel(
    place_ref, lens_ref, own_ref, all_ref, x_ref, y_ref, spare_ref, lse_ref, means_ref, q_s
):
    for n in range(4):
        x_ref[n * QUARTER : (n + 1) * QUARTER, :] = all_ref[n, :, 0:64, :].reshape(QUARTER, 128)
    queries = halves(own_ref[:, 64:96, :]).reshape(QUARTER, HEAD_DIM)
    q_s[...] = jnp.concatenate([queries, jnp.zeros_like(queries)], axis=1)

    def block(i, carry):
        rows = pl.ds(pl.multiple_of(i * BLOCK, BLOCK), BLOCK)
        scores = lax.dot_general(q_s[rows, :], x_ref[...], NT, preferred_element_type=F32)
        top = jnp.max(scores, axis=1, keepdims=True)
        grown = jnp.exp(scores - top)
        total = jnp.sum(grown, axis=1, keepdims=True)
        prob = (grown * (1.0 / total)).astype(BF16)
        mixed = jnp.dot(prob, x_ref[...], preferred_element_type=F32).astype(BF16)
        y_ref[rows, :] = jnp.where(lanes(BLOCK) < 64, q_s[rows, :], mixed)
        log_total = top + jnp.log(total)
        for part in range(PARTS):
            square = jnp.broadcast_to(log_total[part * 128 : (part + 1) * 128], (128, 128))
            lse_ref[pl.ds(i * PARTS + part, 1), :] = jnp.transpose(square)[0:1, :]
        return carry

    lax.fori_loop(0, QUARTER // BLOCK, block, 0)
    spare_ref[0:512, :] = jnp.concatenate(
        [y_ref[0:512, :][:, 64:128], y_ref[512:1024, :][:, 64:128]], axis=1
    )
    spare_ref[512:SPARE, :] = stacked(lse_ref[...])
    member = quarter_member(lens_ref, place_ref[0], place_ref[1]).astype(BF16)
    attn_sums = jnp.dot(member, y_ref[0:QUARTER, :], preferred_element_type=F32)
    sums = jnp.sum(own_ref[:, 96:112, :].astype(F32), axis=0)
    input_sums = (sums[0:8] + pltpu.roll(sums[0:8], 64, 1)) + sums[8:16]
    means = jnp.where(lanes(GROUPS) < 64, input_sums, attn_sums) / lengths_of(lens_ref)
    means_ref[...] = jnp.concatenate([means, means], axis=0)


def pool_kernel(doc_ref, means_ref, w_ref, query_ref, row_ref, own_ref, means_out_ref, logits_ref, out_ref):
    columns = [means_ref[z, 0:8, 0:64] for z in range(PLANE)]
    heads = [
        means_ref[z, 0:8, 64:128] + means_ref[z + 1, 0:8, 64:128] for z in range(0, PLANE, 2)
    ]
    means = jnp.concatenate(heads, axis=1)
    projected = jnp.dot(stacked(means), w_ref[...], preferred_element_type=F32)
    pooled = jnp.concatenate(columns, axis=1) + folded(projected)
    own_ref[...] = pooled
    means_out_ref[...] = means
    unit = pooled / jnp.sqrt(jnp.sum(pooled * pooled, axis=1, keepdims=True) + NORM_EPS)
    logits = folded(
        lax.dot_general(stacked(unit), query_ref[:, :MODEL], NT, preferred_element_type=F32)
    )
    logits = logits * (RECIPROCAL_TEMP / row_ref[0:1, :])
    logits_ref[...] = logits
    group = doc_ref[0] * GROUPS + lax.broadcasted_iota(jnp.int32, logits.shape, 0)
    target = (group == row_ref[8:9, :].astype(jnp.int32)).astype(F32)
    total = jnp.sum(jnp.exp(logits), axis=0, keepdims=True)
    chosen = jnp.sum(target * logits, axis=0, keepdims=True)
    sums = jnp.concatenate(
        [row[:, n : n + 128] for row in (total, chosen) for n in range(0, HELD, 128)], axis=0
    )
    out_ref[...] = jnp.broadcast_to(sums[None], (DOCS, 8, 128))


def prepare_kernel(place_ref, pooled_ref, w_ref, out_ref):
    head = place_ref[2]
    pooled = pooled_ref[...]
    norms = jnp.sqrt(jnp.sum(pooled * pooled, axis=1, keepdims=True) + NORM_EPS)
    unit = pooled / norms
    w_head = w_ref[pl.ds(pl.multiple_of(head * HEAD_DIM, HEAD_DIM), HEAD_DIM), :]
    w_twice = jnp.concatenate([w_head, w_head], axis=0)
    out_ref[0:8, :] = folded(
        lax.dot_general(stacked(unit), w_twice, NT, preferred_element_type=F32)
    )
    z = 2 * head + place_ref[1]
    part = unit[:, 0:64]
    for n in range(1, PLANE):
        part = jnp.where(z == n, unit[:, n * HALF : (n + 1) * HALF], part)
    out_ref[8:16, :] = jnp.concatenate([part, part], axis=1)
    out_ref[16:24, :] = jnp.broadcast_to(norms, (GROUPS, 128))


def query_kernel(query_ref, out_ref):
    query = query_ref[:, :MODEL].astype(F32)
    squares = lax.dot_general(
        jnp.ones((8, MODEL), F32), query * query, NT, precision=EXACT, preferred_element_type=F32
    )
    out_ref[0:8, :] = jnp.sqrt(squares + NORM_EPS)
    out_ref[8:16, :] = lax.dot_general(
        jnp.ones((8, 128), BF16), query_ref[:, MODEL:], NT, preferred_element_type=F32
    )


def loss_kernel(doc_ref, sums_ref, logits_ref, own_ref, query_ref, row_ref, w_ref, out_ref):
    sums = sums_ref[0]
    for n in range(1, DOCS):
        sums = sums + sums_ref[n]
    total = jnp.concatenate([sums[n : n + 1] for n in range(4)], axis=1)
    losses = jnp.log(sums[0:4]) - sums[4:8]
    loss = jnp.sum(jnp.sum(losses, axis=1, keepdims=True), axis=0, keepdims=True)
    query = query_ref[:, :MODEL]
    scale = RECIPROCAL_TEMP / row_ref[0:1, :]
    logits = logits_ref[...]
    group = doc_ref[0] * GROUPS + lax.broadcasted_iota(jnp.int32, logits.shape, 0)
    target = (group == row_ref[8:9, :].astype(jnp.int32)).astype(F32)
    weight = (jnp.exp(logits) / total - target) * (GRADIENT_FACTOR * scale)
    grad = folded(jnp.dot(stacked(weight), query, preferred_element_type=F32))
    own = own_ref[...]
    own_unit = own / jnp.sqrt(jnp.sum(own * own, axis=1, keepdims=True) + NORM_EPS)
    along = jnp.sum(own_unit * grad, axis=1, keepdims=True)
    spread = folded(
        lax.dot_general(stacked(grad), w_ref[...], NT, preferred_element_type=F32)
    )
    extra = jnp.where(lanes(GROUPS) < 64, along, loss)
    for z in range(PLANE):
        head = z // 2
        chunk = jnp.concatenate(
            [
                spread[:, head * HEAD_DIM : (head + 1) * HEAD_DIM],
                grad[:, z * HALF : (z + 1) * HALF],
            ],
            axis=1,
        )
        out_ref[z, 0:8, :] = chunk
        out_ref[z, 8:16, :] = extra


def mass_kernel(lens_ref, own_ref, all_ref, spare_ref, mass_ref, lse_ref, y_ref, k_s, member_s):
    mine = own_ref[:, 0:64, :].reshape(QUARTER, 128)
    k_s[...] = jnp.where(lanes(QUARTER) < 64, mine, jnp.zeros_like(mine))
    for n in range(4):
        queries = halves(all_ref[n, :, 64:96, :]).reshape(QUARTER, HEAD_DIM)
        y_ref[n * QUARTER : (n + 1) * QUARTER, :] = jnp.concatenate(
            [queries, jnp.zeros_like(queries)], axis=1
        )
        lse = spare_ref[n * SPARE + 512 : (n + 1) * SPARE, :].astype(F32)
        lse = (lse[16:24] + lse[8:16]) + lse[0:8]
        for part in range(8):
            at = n * QUARTER + part * 128
            lse_ref[:, at : at + 128] = jnp.broadcast_to(lse[part : part + 1, :], (8, 128))
        member = quarter_member(lens_ref, n // 2, n % 2)
        padded = jnp.concatenate([member, jnp.zeros((120, QUARTER), F32)], axis=0)
        member_s[:, n * QUARTER : (n + 1) * QUARTER] = padded.astype(BF16)

    def block(i, carry):
        rows = pl.ds(pl.multiple_of(i * BLOCK, BLOCK), BLOCK)
        sums = jnp.zeros((BLOCK, 128), F32)
        for n in range(4):
            cols = slice(n * QUARTER, (n + 1) * QUARTER)
            scores = lax.dot_general(k_s[rows, :], y_ref[cols, :], NT, preferred_element_type=F32)
            prob = jnp.exp(scores - lse_ref[0:1, cols]).astype(BF16)
            sums = sums + lax.dot_general(
                prob, member_s[:, cols], NT, preferred_element_type=F32
            )
        for part in range(PARTS):
            mass_ref[i * PARTS + part] = jnp.transpose(sums[part * 128 : (part + 1) * 128])[0:8, :]
        return carry

    lax.fori_loop(0, QUARTER // BLOCK, block, 0)


def group_kernel(lens_ref, terms_ref, ready_ref, mass_ref, dattn_ref, grad_ref, loss_ref):
    sums = terms_ref[0]
    for n in range(1, PLANE):
        sums = sums + terms_ref[n]
    along = sums[8:16, 0:1]
    loss_ref[...] = sums[8:16, :] / QUERY_COUNT
    norms = ready_ref[16:24, :]
    raw = jnp.concatenate([sums[0:8, 0:64], sums[0:8, 0:64]], axis=1)
    dattn_ref[...] = (raw - ready_ref[0:8, :] * along) / norms / lengths_of(lens_ref)
    grad = (sums[0:8, 64:128] - ready_ref[8:16, 0:64] * along) / norms[:, 0:64]
    for z in range(PLANE):
        half = (z % 2) * HALF
        grad_ref[z] = jnp.concatenate([grad, mass_ref[z // 2, :, half : half + HALF]], axis=1)


def inputs_kernel(place_ref, lens_ref, parts_ref, means_ref, grad_inputs_ref, out_ref):
    grad = jnp.concatenate([parts_ref[z, :, 0:64] for z in range(PLANE)], axis=1)
    mine = local_member(lens_ref, place_ref[3])
    members = jnp.concatenate([mine, mine, mine, mine], axis=0).astype(BF16)
    grad_inputs_ref[...] = lax.dot_general(
        members, stacked(grad / lengths_of(lens_ref)[:, 0:1]), TN, preferred_element_type=F32
    ).astype(BF16)
    both = jnp.concatenate([grad, means_ref[...]], axis=1)
    wide = (MODEL + WIDTH) // 2
    both = jnp.concatenate([both[:, :wide], both[:, wide:]], axis=0)
    out_ref[...] = jnp.broadcast_to(both.astype(BF16)[None], (DOCS, 2 * GROUPS, wide))


def value_kernel(lens_ref, parts_ref, w_ref, grad_v_ref):
    grad = jnp.concatenate([parts_ref[z, :, 0:64] for z in range(PLANE)], axis=1)
    grad = grad / lengths_of(lens_ref)[:, 0:1]
    dattn = folded(lax.dot_general(stacked(grad), w_ref[...], NT, preferred_element_type=F32))
    dattn = dattn.astype(BF16).astype(F32)
    dattn = jnp.concatenate([dattn, dattn, dattn, jnp.zeros_like(dattn)], axis=0).astype(BF16)
    for pair in range(HEAD_COUNT // 2):
        cols = slice(pair * 128, (pair + 1) * 128)
        both = []
        for head in (2 * pair, 2 * pair + 1):
            mass = jnp.concatenate(
                [parts_ref[2 * head, :, 64:128], parts_ref[2 * head + 1, :, 64:128]], axis=1
            )
            both.append(
                lax.dot_general(stacked(mass), dattn[:, cols], TN, preferred_element_type=F32)
            )
        grad_v_ref[:, cols] = jnp.where(lanes(ROWS) < 64, both[0], both[1]).astype(BF16)


def weight_kernel(in_ref, out_ref):
    wide = (MODEL + WIDTH) // 2
    both = in_ref[...].astype(F32)
    both = [both[:, n : n + 8].reshape(DOCS * GROUPS, wide) for n in (0, 8)]
    both = jnp.concatenate(both, axis=1).astype(BF16)
    out_ref[...] = lax.dot_general(
        both[:, MODEL:], both[:, :MODEL], TN, preferred_element_type=F32
    )


CHUNK = 512
TALL = 512


def row_kernel(
    place_ref, lens_ref, y_ref, lse_ref, x_ref, dattn_ref, grad_k_ref, out_ref, q_s, d_s, delta_s
):
    lane = lanes(QUARTER)
    member = quarter_member(lens_ref, place_ref[0], place_ref[1]).astype(BF16)
    spread = lax.dot_general(
        member, dattn_ref[...].astype(BF16), TN, preferred_element_type=F32
    )
    spread = jnp.where(lane < 64, 0.0, spread)
    mine = y_ref[0:QUARTER, :]
    q_s[...] = jnp.where(lane < 64, mine, jnp.zeros_like(mine))
    d_s[...] = spread.astype(BF16)
    delta_s[...] = jnp.broadcast_to(
        jnp.sum(spread * mine.astype(F32), axis=1, keepdims=True), (QUARTER, 128)
    )

    def block(i, carry):
        rows = pl.ds(pl.multiple_of(i * TALL, TALL), TALL)
        columns = []
        for part in range(TALL // 128):
            line = lse_ref[pl.ds(i * (TALL // 128) + part, 1), :]
            columns.append(jnp.transpose(jnp.broadcast_to(line, (128, 128))))
        log_total = jnp.concatenate(columns, axis=0)[:, 0:1]
        delta = delta_s[rows, 0:1]
        total = jnp.zeros((TALL, 128), F32)
        for n in range(KEYS // CHUNK):
            part = x_ref[n * CHUNK : (n + 1) * CHUNK, :]
            scores = lax.dot_general(q_s[rows, :], part, NT, preferred_element_type=F32)
            prob_grad = lax.dot_general(d_s[rows, :], part, NT, preferred_element_type=F32)
            score_grad = (jnp.exp(scores - log_total) * (prob_grad - delta)).astype(BF16)
            total = total + jnp.dot(score_grad, part, preferred_element_type=F32)
        total = total * SCALE
        total = jnp.concatenate([total[:, 0:64]] * 2, axis=1).astype(BF16)
        both = jnp.where(lanes(TALL) < 64, grad_k_ref[rows, :], total)
        count = TALL // HALF
        out_ref[pl.ds(i * count, count), :, :] = both.reshape(count, HALF, 128)
        return carry

    lax.fori_loop(0, QUARTER // TALL, block, 0)


def column_kernel(
    lens_ref, own_ref, y_ref, spare_ref, lse_ref, dattn_ref, out_ref, y_s, k_s, v_s, delta_s
):
    lane = lanes(QUARTER)
    mine = own_ref[:, 0:64, :].reshape(QUARTER, 128)
    zero = jnp.zeros_like(mine)
    k_s[...] = jnp.where(lane < 64, mine, zero)
    v_s[...] = jnp.where(lane < 64, zero, mine)
    early = jnp.where(lanes(GROUPS) < 64, dattn_ref[...], 0.0).astype(BF16)
    dattn = jnp.where(lanes(GROUPS) < 64, 0.0, dattn_ref[...]).astype(BF16)
    for n in range(4):
        rows = slice(n * QUARTER, (n + 1) * QUARTER)
        member = quarter_member(lens_ref, n // 2, n % 2)
        spread = lax.dot_general(member.astype(BF16), dattn, TN, preferred_element_type=F32)
        y_s[rows, :] = jnp.where(lane < 64, y_ref[rows, :], spread.astype(BF16))
        attn = spare_ref[n * SPARE : n * SPARE + 512, :]
        products = jnp.concatenate(
            [
                lax.dot_general(part, attn, NT, preferred_element_type=F32)
                for part in (early, dattn)
            ],
            axis=1,
        )
        delta_s[:, rows] = jnp.broadcast_to(
            jnp.sum(products * member, axis=0, keepdims=True), (8, QUARTER)
        )

    def block(i, carry):
        rows = pl.ds(pl.multiple_of(i * BLOCK, BLOCK), BLOCK)
        total = jnp.zeros((BLOCK, 128), F32)
        for n in range(KEYS // CHUNK):
            cols = slice(n * CHUNK, (n + 1) * CHUNK)
            part = y_s[cols, :]
            scores = lax.dot_general(k_s[rows, :], part, NT, preferred_element_type=F32)
            prob_grad = lax.dot_general(v_s[rows, :], part, NT, preferred_element_type=F32)
            score_grad = (
                jnp.exp(scores - lse_ref[0:1, cols]) * (prob_grad - delta_s[0:1, cols])
            ).astype(BF16)
            total = total + jnp.dot(score_grad, part, preferred_element_type=F32)
        out_ref[rows, :] = total.astype(BF16)
        return carry

    lax.fori_loop(0, QUARTER // BLOCK, block, 0)


SMEM = pl.BlockSpec(memory_space=pltpu.SMEM)
VMEM = pl.BlockSpec(memory_space=pltpu.VMEM)


def call(kernel, outs, scalars, arrays, scratch, estimate, name):
    return pl.pallas_call(
        kernel,
        out_shape=outs,
        in_specs=[SMEM] * len(scalars) + [VMEM] * len(arrays),
        out_specs=jax.tree.map(lambda _: VMEM, outs),
        scratch_shapes=scratch,
        compiler_params=params(56 if name == "pack" else 40 if scratch else 12),
        cost_estimate=estimate,
        name=name,
    )(*scalars, *arrays)


def shape(dims, dtype):
    return jax.ShapeDtypeStruct(dims, dtype)


def body(inputs, q_heads, k_heads, v_heads, w_out, group_lens, query_emb, positive):
    plane = lax.axis_index("yl")
    half = lax.axis_index("zd")
    head = lax.axis_index(HEADS)
    first = lax.axis_index(SEQ) * ROWS
    doc = lax.axis_index(GRP).reshape(1).astype(jnp.int32)
    place = jnp.stack([plane, half, head, first]).astype(jnp.int32)
    lengths = group_lens[0]
    exchange = functools.partial(lax.all_to_all, split_axis=0, concat_axis=0)
    barrier = lax.optimization_barrier
    pairs = QUARTER * KEYS

    packed = call(
        pack_kernel, shape((PLANE, 112, 128), BF16), (place, lengths),
        (q_heads[0], k_heads[0], v_heads[0], inputs[0]), (), cost(0, 1000000), "pack",
    )
    tagged = jnp.concatenate(
        [query_emb, jnp.pad(positive.astype(BF16)[:, None], ((0, 0), (0, 127)))], axis=1
    )
    packed, tagged = barrier((packed, tagged))
    own = exchange(packed, ZED)
    queries = gather(tagged, ("yh", "yl", "xa"))
    own, queries = barrier((own, queries))
    keys = share(own[:, 0:96, :], SQUARE)
    queries = gather(queries, ("xb", "co"))
    own, keys, queries = barrier((own, keys, queries))

    rows, mine, spare, lse, means = call(
        forward_kernel,
        (
            shape((KEYS, 128), BF16),
            shape((QUARTER, 128), BF16),
            shape((SPARE, 128), BF16),
            shape((8, 128), F32),
            shape((2 * GROUPS, 128), F32),
        ),
        (place, lengths), (own, keys), [pltpu.VMEM((QUARTER, 128), BF16)],
        cost(pairs * 256 * 4, 3000000, pairs), "forward",
    )
    means = means + swap(means, ("yl",), 1)
    means = jnp.broadcast_to(means[None], (PLANE, 2 * GROUPS, 128))
    spare, means, queries = barrier((spare, means, queries))
    means = exchange(means, ZED)
    around = [swap(spare, SQUARE, flip) for flip in (1, 2, 3)]
    query_rows = call(
        query_kernel, shape((16, HELD), F32), (), (queries,), (), cost(6 * 2 * 8 * HELD * 1024, 1200000),
        "queries",
    )
    means, query_rows, around = barrier((means, query_rows, around))
    pooled_own, doc_means, logits, sums = call(
        pool_kernel,
        (
            shape((GROUPS, MODEL), F32),
            shape((GROUPS, WIDTH), F32),
            shape((GROUPS, HELD), F32),
            shape((DOCS, 8, 128), F32),
        ),
        (doc,), (means, w_out, queries, query_rows), (), cost(2 * 32 * 768 * 1024, 1800000), "pool",
    )
    sums = exchange(sums, GRP)
    square = [spare] + around
    rotated = [jnp.where(half == 0, square[n], square[n ^ 1]) for n in range(4)]
    ordered = [jnp.where(plane == 0, rotated[n], rotated[n ^ 2]) for n in range(4)]
    others = jnp.concatenate(ordered, axis=0)
    ready = call(
        prepare_kernel, shape((24, 128), F32), (place,), (pooled_own, w_out), (),
        cost(2 * 32 * 128 * 1024, 1200000), "prepare",
    )
    sums, others, ready = barrier((sums, others, ready))
    terms = call(
        loss_kernel, shape((PLANE, 16, 128), F32), (doc,),
        (sums, logits, pooled_own, queries, query_rows, w_out), (),
        cost(2 * 32 * 768 * 1024, 1800000, 2000), "loss",
    )
    terms, own, keys, others = barrier((terms, own, keys, others))
    terms = exchange(terms, ZED)
    mass, lse_rows, columns = call(
        mass_kernel,
        (shape((GROUPS, 8, 128), F32), shape((8, KEYS), F32), shape((KEYS, 128), BF16)),
        (lengths,), (own, keys, others),
        [pltpu.VMEM((QUARTER, 128), BF16), pltpu.VMEM((128, KEYS), BF16)],
        cost(pairs * 256 * 4, 2500000, pairs), "mass",
    )
    terms, mass, lse_rows = barrier((terms, mass, lse_rows))

    dattn, grad_part, loss = call(
        group_kernel,
        (
            shape((GROUPS, 128), F32),
            shape((PLANE, GROUPS, 128), F32),
            shape((GROUPS, 128), F32),
        ),
        (lengths,), (terms, ready, mass), (), cost(0, 100000), "group",
    )
    mean_loss = loss[0, 64]
    grad_parts = exchange(grad_part, ZED)
    grad_columns = call(
        column_kernel, shape((QUARTER, 128), BF16), (lengths,),
        (own, columns, others, lse_rows, dattn),
        [
            pltpu.VMEM((KEYS, 128), BF16),
            pltpu.VMEM((QUARTER, 128), BF16),
            pltpu.VMEM((QUARTER, 128), BF16),
            pltpu.VMEM((8, KEYS), F32),
        ],
        cost(pairs * 256 * 6, 2500000, pairs), "columns",
    )
    grad_inputs, grads = call(
        inputs_kernel,
        (shape((ROWS, MODEL), BF16), shape((DOCS, 2 * GROUPS, (MODEL + WIDTH) // 2), BF16)),
        (place, lengths), (grad_parts, doc_means), (), cost(2 * 32 * 128 * 1024, 1200000), "inputs",
    )
    grad_columns, grads = barrier((grad_columns, grads))
    all_grads = exchange(grads, GRP)
    packed_grads = call(
        row_kernel, shape((PLANE, HALF, 128), BF16), (place, lengths),
        (mine, lse, rows, dattn, grad_columns),
        [
            pltpu.VMEM((QUARTER, 128), BF16),
            pltpu.VMEM((QUARTER, 128), BF16),
            pltpu.VMEM((QUARTER, 128), F32),
        ],
        cost(pairs * 256 * 6, 2000000, pairs), "rows",
    )
    packed_grads, grad_parts = barrier((packed_grads, grad_parts))
    home = exchange(packed_grads, ZED)
    out = shape((ROWS, WIDTH), BF16)
    grad_v = call(
        value_kernel, out, (lengths,), (grad_parts, w_out), (), cost(2 * 32 * 512 * 1024, 1300000),
        "values",
    )
    grad_w_out = call(
        weight_kernel, shape((WIDTH, MODEL), F32), (), (all_grads,), (),
        cost(2 * 384 * 512 * 1024, 3000000), "weights",
    )
    grad_q, grad_k = call(
        unpack_kernel, (out, out), (), (home,), (), cost(0, 500000), "unpack"
    )
    return (mean_loss, grad_inputs[None], grad_q[None], grad_k[None], grad_v[None], grad_w_out)


def solution(mesh):
    fine = Mesh(mesh.devices.reshape((2,) * 9), GRP + SEQ)
    rows = P(GRP, SEQ, None)
    return jax.shard_map(
        body,
        mesh=fine,
        in_specs=(
            rows,
            rows,
            rows,
            rows,
            P(),
            P(GRP, None),
            P(GRP + SEQ, None),
            P(GRP + SEQ),
        ),
        out_specs=(P(), rows, rows, rows, rows, P()),
        check_vma=False,
    )
```

```python
import functools

import jax
import jax.numpy as jnp
from jax import lax
from jax.experimental import pallas as pl
from jax.experimental.pallas import tpu as pltpu
from jax.sharding import Mesh, PartitionSpec as P

HEAD_COUNT = 8
HEAD_DIM = 64
GROUPS = 8
DOCS = 16
MODEL = 1024
WIDTH = 512
ROWS = 128
HALF = 64
QUARTER = 1024
PLANE = 16
SCALE = HEAD_DIM ** (-0.5)

RECIPROCAL_TEMP = 20.0
GRADIENT_FACTOR = 64.0
NORM_EPS = 1e-06
QUERY_COUNT = 8192
EXACT = lax.Precision.HIGHEST

BF16 = jnp.bfloat16
F32 = jnp.float32

GRP = ("yh", "xa", "xb", "co")
SEQ = ("yl", "za", "zb", "zc", "zd")
ZED = ("za", "zb", "zc", "zd")
SQUARE = ("yl", "zd")
HEADS = ("za", "zb", "zc")
NT = (((1,), (1,)), ((), ()))
TN = (((0,), (0,)), ((), ()))

HELD = 512


def params(mebibytes):
    return pltpu.CompilerParams(vmem_limit_bytes=mebibytes << 20)


def cost(flops, moved, exps=0):
    return pl.CostEstimate(flops=int(flops), bytes_accessed=int(moved), transcendentals=int(exps))


def share(value, axes):
    count = 2 ** len(axes)
    return lax.all_to_all(
        jnp.broadcast_to(value[None], (count,) + value.shape), axes, split_axis=0, concat_axis=0
    )


def swap(value, axes, flip):
    count = 2 ** len(axes)
    return lax.ppermute(value, axes, [(i, i ^ flip) for i in range(count)])


def gather(value, axes):
    for axis in axes:
        other = swap(value, (axis,), 1)
        first = lax.axis_index(axis) == 0
        value = jnp.where(
            first,
            jnp.concatenate([value, other], axis=0),
            jnp.concatenate([other, value], axis=0),
        )
    return value


def three(value):
    high = value.astype(BF16)
    rest = value - high.astype(F32)
    middle = rest.astype(BF16)
    low = (rest - middle.astype(F32)).astype(BF16)
    return high, middle, low


def stacked(value):
    parts = [part.astype(F32) for part in three(value)]
    parts.append(jnp.zeros_like(value))
    return jnp.concatenate(parts, axis=0).astype(BF16)


def folded(product):
    return (product[16:24] + product[8:16]) + product[0:8]


def column_of(values):
    row = lax.broadcasted_iota(jnp.int32, (GROUPS, 128), 0)
    out = jnp.full((GROUPS, 128), values[0])
    for n in range(1, GROUPS):
        out = jnp.where(row == n, values[n], out)
    return out


def member_of(position, lens_ref):
    ends = [lens_ref[0]]
    for n in range(1, GROUPS):
        ends.append(ends[-1] + lens_ref[n])
    last = column_of(ends)
    first = last - column_of([lens_ref[n] for n in range(GROUPS)])
    return ((position >= first[:, 0:1]) & (position < last[:, 0:1])).astype(F32)


def lengths_of(lens_ref):
    return column_of([lens_ref[n] for n in range(GROUPS)]).astype(F32)


def quarter_member(lens_ref, plane, half):
    row = lax.broadcasted_iota(jnp.int32, (GROUPS, QUARTER), 1)
    position = plane * (PLANE * ROWS) + (row >> 6) * ROWS + half * HALF + (row & 63)
    return member_of(position, lens_ref)


def local_member(lens_ref, first):
    return member_of(first + lax.broadcasted_iota(jnp.int32, (GROUPS, ROWS), 1), lens_ref)


def halves(packed):
    return jnp.concatenate([packed[:, :, 0:64], packed[:, :, 64:128]], axis=1)


def lanes(rows):
    return lax.broadcasted_iota(jnp.int32, (rows, 128), 1)


def pack_kernel(place_ref, lens_ref, q_ref, k_ref, v_ref, inputs_ref, out_ref):
    mine = local_member(lens_ref, place_ref[3]).astype(BF16)
    sums = jnp.dot(mine, inputs_ref[...], preferred_element_type=F32)
    high, middle, low = [part.astype(F32) for part in three(sums)]
    zero = jnp.zeros((GROUPS, HALF), F32)
    for head in range(HEAD_COUNT):
        cols = slice(head * HEAD_DIM, (head + 1) * HEAD_DIM)
        for half in range(2):
            rows = slice(half * HALF, (half + 1) * HALF)
            place = 2 * head + half
            out_ref[place, 0:64, :] = jnp.concatenate([k_ref[rows, cols], v_ref[rows, cols]], axis=1)
            query = q_ref[rows, cols] * jnp.asarray(SCALE, BF16)
            out_ref[place, 64:96, :] = jnp.concatenate([query[0:32], query[32:64]], axis=1)
            part = slice(place * HALF, (place + 1) * HALF)
            upper = jnp.concatenate([high[:, part], middle[:, part]], axis=1)
            lower = jnp.concatenate([low[:, part], zero], axis=1)
            out_ref[place, 96:112, :] = jnp.concatenate([upper, lower], axis=0).astype(BF16)


def unpack_kernel(in_ref, q_ref, k_ref):
    for pair in range(HEAD_COUNT // 2):
        cols = slice(pair * 128, (pair + 1) * 128)
        for half in range(2):
            rows = slice(half * HALF, (half + 1) * HALF)
            first, second = in_ref[4 * pair + half], in_ref[4 * pair + 2 + half]
            k_ref[rows, cols] = jnp.concatenate([first[:, 0:64], second[:, 0:64]], axis=1)
            q_ref[rows, cols] = jnp.concatenate([first[:, 64:128], second[:, 64:128]], axis=1)


BLOCK = 256
PARTS = BLOCK // 128


KEYS = 4 * QUARTER
SPARE = 512


def forward_kernel(
    place_ref, lens_ref, own_ref, all_ref, x_ref, y_ref, spare_ref, lse_ref, means_ref, q_s
):
    for n in range(4):
        x_ref[n * QUARTER : (n + 1) * QUARTER, :] = all_ref[n, :, 0:64, :].reshape(QUARTER, 128)
    queries = halves(own_ref[:, 64:96, :]).reshape(QUARTER, HEAD_DIM)
    q_s[...] = jnp.concatenate([queries, jnp.zeros_like(queries)], axis=1)

    def block(i, carry):
        rows = pl.ds(pl.multiple_of(i * BLOCK, BLOCK), BLOCK)
        scores = lax.dot_general(q_s[rows, :], x_ref[...], NT, preferred_element_type=F32)
        top = jnp.max(scores, axis=1, keepdims=True)
        grown = jnp.exp(scores - top)
        total = jnp.sum(grown, axis=1, keepdims=True)
        prob = (grown * (1.0 / total)).astype(BF16)
        mixed = jnp.dot(prob, x_ref[...], preferred_element_type=F32).astype(BF16)
        y_ref[rows, :] = jnp.where(lanes(BLOCK) < 64, q_s[rows, :], mixed)
        log_total = top + jnp.log(total)
        for part in range(PARTS):
            square = jnp.broadcast_to(log_total[part * 128 : (part + 1) * 128], (128, 128))
            lse_ref[pl.ds(i * PARTS + part, 1), :] = jnp.transpose(square)[0:1, :]
        return carry

    lax.fori_loop(0, QUARTER // BLOCK, block, 0)
    spare_ref[...] = jnp.concatenate(
        [y_ref[0:512, :][:, 64:128], y_ref[512:1024, :][:, 64:128]], axis=1
    )
    member = quarter_member(lens_ref, place_ref[0], place_ref[1]).astype(BF16)
    attn_sums = jnp.dot(member, y_ref[0:QUARTER, :], preferred_element_type=F32)
    sums = jnp.sum(own_ref[:, 96:112, :].astype(F32), axis=0)
    input_sums = (sums[0:8] + pltpu.roll(sums[0:8], 64, 1)) + sums[8:16]
    means = jnp.where(lanes(GROUPS) < 64, input_sums, attn_sums) / lengths_of(lens_ref)
    means_ref[...] = jnp.concatenate([means, lse_ref[...]], axis=0)


def plane_kernel(mine_ref, other_ref, out_ref):
    mine, other = mine_ref[...], other_ref[...]
    both = jnp.concatenate([mine[0:8] + other[0:8], mine[8:16], other[8:16]], axis=0)
    out_ref[...] = jnp.broadcast_to(both[None], (PLANE, 3 * GROUPS, 128))


def pool_kernel(doc_ref, means_ref, w_ref, query_ref, row_ref, own_ref, means_out_ref, logits_ref, out_ref):
    columns = [means_ref[z, 0:8, 0:64] for z in range(PLANE)]
    heads = [
        means_ref[z, 0:8, 64:128] + means_ref[z + 1, 0:8, 64:128] for z in range(0, PLANE, 2)
    ]
    means = jnp.concatenate(heads, axis=1)
    projected = jnp.dot(stacked(means), w_ref[...], preferred_element_type=F32)
    pooled = jnp.concatenate(columns, axis=1) + folded(projected)
    own_ref[...] = pooled
    means_out_ref[...] = means
    unit = pooled / jnp.sqrt(jnp.sum(pooled * pooled, axis=1, keepdims=True) + NORM_EPS)
    logits = folded(
        lax.dot_general(stacked(unit), query_ref[:, :MODEL], NT, preferred_element_type=F32)
    )
    logits = logits * (RECIPROCAL_TEMP / row_ref[0:1, :])
    logits_ref[...] = logits
    group = doc_ref[0] * GROUPS + lax.broadcasted_iota(jnp.int32, logits.shape, 0)
    target = (group == row_ref[8:9, :].astype(jnp.int32)).astype(F32)
    total = jnp.sum(jnp.exp(logits), axis=0, keepdims=True)
    chosen = jnp.sum(target * logits, axis=0, keepdims=True)
    sums = jnp.concatenate(
        [row[:, n : n + 128] for row in (total, chosen) for n in range(0, HELD, 128)], axis=0
    )
    out_ref[...] = jnp.broadcast_to(sums[None], (DOCS, 8, 128))


def prepare_kernel(place_ref, pooled_ref, w_ref, out_ref):
    head = place_ref[2]
    pooled = pooled_ref[...]
    norms = jnp.sqrt(jnp.sum(pooled * pooled, axis=1, keepdims=True) + NORM_EPS)
    unit = pooled / norms
    w_head = w_ref[pl.ds(pl.multiple_of(head * HEAD_DIM, HEAD_DIM), HEAD_DIM), :]
    w_twice = jnp.concatenate([w_head, w_head], axis=0)
    out_ref[0:8, :] = folded(
        lax.dot_general(stacked(unit), w_twice, NT, preferred_element_type=F32)
    )
    z = 2 * head + place_ref[1]
    part = unit[:, 0:64]
    for n in range(1, PLANE):
        part = jnp.where(z == n, unit[:, n * HALF : (n + 1) * HALF], part)
    out_ref[8:16, :] = jnp.concatenate([part, part], axis=1)
    out_ref[16:24, :] = jnp.broadcast_to(norms, (GROUPS, 128))


def query_kernel(query_ref, out_ref):
    query = query_ref[:, :MODEL].astype(F32)
    squares = lax.dot_general(
        jnp.ones((8, MODEL), F32), query * query, NT, precision=EXACT, preferred_element_type=F32
    )
    out_ref[0:8, :] = jnp.sqrt(squares + NORM_EPS)
    out_ref[8:16, :] = lax.dot_general(
        jnp.ones((8, 128), BF16), query_ref[:, MODEL:], NT, preferred_element_type=F32
    )


def loss_kernel(doc_ref, sums_ref, logits_ref, own_ref, query_ref, row_ref, w_ref, out_ref):
    sums = sums_ref[0]
    for n in range(1, DOCS):
        sums = sums + sums_ref[n]
    total = jnp.concatenate([sums[n : n + 1] for n in range(4)], axis=1)
    losses = jnp.log(sums[0:4]) - sums[4:8]
    loss = jnp.sum(jnp.sum(losses, axis=1, keepdims=True), axis=0, keepdims=True)
    query = query_ref[:, :MODEL]
    scale = RECIPROCAL_TEMP / row_ref[0:1, :]
    logits = logits_ref[...]
    group = doc_ref[0] * GROUPS + lax.broadcasted_iota(jnp.int32, logits.shape, 0)
    target = (group == row_ref[8:9, :].astype(jnp.int32)).astype(F32)
    weight = (jnp.exp(logits) / total - target) * (GRADIENT_FACTOR * scale)
    grad = folded(jnp.dot(stacked(weight), query, preferred_element_type=F32))
    own = own_ref[...]
    own_unit = own / jnp.sqrt(jnp.sum(own * own, axis=1, keepdims=True) + NORM_EPS)
    along = jnp.sum(own_unit * grad, axis=1, keepdims=True)
    spread = folded(
        lax.dot_general(stacked(grad), w_ref[...], NT, preferred_element_type=F32)
    )
    extra = jnp.where(lanes(GROUPS) < 64, along, loss)
    for z in range(PLANE):
        head = z // 2
        chunk = jnp.concatenate(
            [
                spread[:, head * HEAD_DIM : (head + 1) * HEAD_DIM],
                grad[:, z * HALF : (z + 1) * HALF],
            ],
            axis=1,
        )
        out_ref[z, 0:8, :] = chunk
        out_ref[z, 8:16, :] = extra


def mass_kernel(
    place_ref, lens_ref, own_ref, all_ref, means_ref, mass_ref, lse_ref, y_ref, k_s, member_s
):
    mine = own_ref[:, 0:64, :].reshape(QUARTER, 128)
    k_s[...] = jnp.where(lanes(QUARTER) < 64, mine, jnp.zeros_like(mine))
    for n in range(4):
        queries = halves(all_ref[n, :, 64:96, :]).reshape(QUARTER, HEAD_DIM)
        y_ref[n * QUARTER : (n + 1) * QUARTER, :] = jnp.concatenate(
            [queries, jnp.zeros_like(queries)], axis=1
        )
        both = means_ref[2 * place_ref[2] + n % 2]
        lse = jnp.where(place_ref[0] == n // 2, both[8:16], both[16:24])
        for part in range(8):
            at = n * QUARTER + part * 128
            lse_ref[:, at : at + 128] = jnp.broadcast_to(lse[part : part + 1, :], (8, 128))
        member = quarter_member(lens_ref, n // 2, n % 2)
        padded = jnp.concatenate([member, jnp.zeros((120, QUARTER), F32)], axis=0)
        member_s[:, n * QUARTER : (n + 1) * QUARTER] = padded.astype(BF16)

    def block(i, carry):
        rows = pl.ds(pl.multiple_of(i * BLOCK, BLOCK), BLOCK)
        sums = jnp.zeros((BLOCK, 128), F32)
        for n in range(4):
            cols = slice(n * QUARTER, (n + 1) * QUARTER)
            scores = lax.dot_general(k_s[rows, :], y_ref[cols, :], NT, preferred_element_type=F32)
            prob = jnp.exp(scores - lse_ref[0:1, cols]).astype(BF16)
            sums = sums + lax.dot_general(
                prob, member_s[:, cols], NT, preferred_element_type=F32
            )
        for part in range(PARTS):
            mass_ref[i * PARTS + part] = jnp.transpose(sums[part * 128 : (part + 1) * 128])[0:8, :]
        return carry

    lax.fori_loop(0, QUARTER // BLOCK, block, 0)


def rows_of(line):
    return jnp.concatenate([line[:, n : n + 128] for n in range(0, QUARTER, 128)], axis=0)


def group_kernel(
    place_ref, lens_ref, terms_ref, ready_ref, mass_ref, spare_ref, other_ref,
    dattn_ref, grad_ref, loss_ref, delta_ref,
):
    sums = terms_ref[0]
    for n in range(1, PLANE):
        sums = sums + terms_ref[n]
    along = sums[8:16, 0:1]
    loss_ref[...] = sums[8:16, :] / QUERY_COUNT
    norms = ready_ref[16:24, :]
    raw = jnp.concatenate([sums[0:8, 0:64], sums[0:8, 0:64]], axis=1)
    dattn = (raw - ready_ref[0:8, :] * along) / norms / lengths_of(lens_ref)
    dattn_ref[...] = dattn
    lane = lanes(GROUPS)
    ends = [
        jnp.where(lane < 64, dattn, 0.0).astype(BF16),
        jnp.where(lane < 64, 0.0, dattn).astype(BF16),
    ]
    for n, (attn, plane) in enumerate(
        ((spare_ref, place_ref[0]), (other_ref, 1 - place_ref[0]))
    ):
        products = jnp.concatenate(
            [lax.dot_general(part, attn[...], NT, preferred_element_type=F32) for part in ends],
            axis=1,
        )
        member = quarter_member(lens_ref, plane, place_ref[1])
        delta_ref[n * 8 : (n + 1) * 8, :] = rows_of(
            jnp.sum(products * member, axis=0, keepdims=True)
        )
    grad = (sums[0:8, 64:128] - ready_ref[8:16, 0:64] * along) / norms[:, 0:64]
    for z in range(PLANE):
        half = (z % 2) * HALF
        grad_ref[z] = jnp.concatenate([grad, mass_ref[z // 2, :, half : half + HALF]], axis=1)


def inputs_kernel(place_ref, lens_ref, parts_ref, means_ref, grad_inputs_ref, out_ref):
    grad = jnp.concatenate([parts_ref[z, :, 0:64] for z in range(PLANE)], axis=1)
    mine = local_member(lens_ref, place_ref[3])
    members = jnp.concatenate([mine, mine, mine, mine], axis=0).astype(BF16)
    grad_inputs_ref[...] = lax.dot_general(
        members, stacked(grad / lengths_of(lens_ref)[:, 0:1]), TN, preferred_element_type=F32
    ).astype(BF16)
    both = jnp.concatenate([grad, means_ref[...]], axis=1)
    wide = (MODEL + WIDTH) // 2
    both = jnp.concatenate([both[:, :wide], both[:, wide:]], axis=0)
    out_ref[...] = jnp.broadcast_to(both.astype(BF16)[None], (DOCS, 2 * GROUPS, wide))


def value_kernel(lens_ref, parts_ref, w_ref, grad_v_ref):
    grad = jnp.concatenate([parts_ref[z, :, 0:64] for z in range(PLANE)], axis=1)
    grad = grad / lengths_of(lens_ref)[:, 0:1]
    dattn = folded(lax.dot_general(stacked(grad), w_ref[...], NT, preferred_element_type=F32))
    dattn = dattn.astype(BF16).astype(F32)
    dattn = jnp.concatenate([dattn, dattn, dattn, jnp.zeros_like(dattn)], axis=0).astype(BF16)
    for pair in range(HEAD_COUNT // 2):
        cols = slice(pair * 128, (pair + 1) * 128)
        both = []
        for head in (2 * pair, 2 * pair + 1):
            mass = jnp.concatenate(
                [parts_ref[2 * head, :, 64:128], parts_ref[2 * head + 1, :, 64:128]], axis=1
            )
            both.append(
                lax.dot_general(stacked(mass), dattn[:, cols], TN, preferred_element_type=F32)
            )
        grad_v_ref[:, cols] = jnp.where(lanes(ROWS) < 64, both[0], both[1]).astype(BF16)


def weight_kernel(in_ref, out_ref):
    wide = (MODEL + WIDTH) // 2
    both = in_ref[...].astype(F32)
    both = [both[:, n : n + 8].reshape(DOCS * GROUPS, wide) for n in (0, 8)]
    both = jnp.concatenate(both, axis=1).astype(BF16)
    out_ref[...] = lax.dot_general(
        both[:, MODEL:], both[:, :MODEL], TN, preferred_element_type=F32
    )


CHUNK = 512
TALL = 512


def row_kernel(
    place_ref, lens_ref, y_ref, lse_ref, x_ref, dattn_ref, out_ref, q_s, d_s, delta_s
):
    lane = lanes(QUARTER)
    member = quarter_member(lens_ref, place_ref[0], place_ref[1]).astype(BF16)
    spread = lax.dot_general(
        member, dattn_ref[...].astype(BF16), TN, preferred_element_type=F32
    )
    spread = jnp.where(lane < 64, 0.0, spread)
    mine = y_ref[0:QUARTER, :]
    q_s[...] = jnp.where(lane < 64, mine, jnp.zeros_like(mine))
    d_s[...] = spread.astype(BF16)
    delta_s[...] = jnp.broadcast_to(
        jnp.sum(spread * mine.astype(F32), axis=1, keepdims=True), (QUARTER, 128)
    )

    def block(i, carry):
        rows = pl.ds(pl.multiple_of(i * TALL, TALL), TALL)
        columns = []
        for part in range(TALL // 128):
            line = lse_ref[pl.ds(i * (TALL // 128) + part, 1), :]
            columns.append(jnp.transpose(jnp.broadcast_to(line, (128, 128))))
        log_total = jnp.concatenate(columns, axis=0)[:, 0:1]
        delta = delta_s[rows, 0:1]
        total = jnp.zeros((TALL, 128), F32)
        for n in range(KEYS // CHUNK):
            part = x_ref[n * CHUNK : (n + 1) * CHUNK, :]
            scores = lax.dot_general(q_s[rows, :], part, NT, preferred_element_type=F32)
            prob_grad = lax.dot_general(d_s[rows, :], part, NT, preferred_element_type=F32)
            score_grad = (jnp.exp(scores - log_total) * (prob_grad - delta)).astype(BF16)
            total = total + jnp.dot(score_grad, part, preferred_element_type=F32)
        total = total * SCALE
        out_ref[rows, :] = jnp.concatenate([total[:, 0:64]] * 2, axis=1).astype(BF16)
        return carry

    lax.fori_loop(0, QUARTER // TALL, block, 0)


def column_kernel(
    place_ref, lens_ref, own_ref, y_ref, mine_ref, other_ref, lse_ref, dattn_ref, grad_q_ref,
    out_ref, y_s, k_s, v_s, delta_s,
):
    lane = lanes(QUARTER)
    mine = own_ref[:, 0:64, :].reshape(QUARTER, 128)
    zero = jnp.zeros_like(mine)
    k_s[...] = jnp.where(lane < 64, mine, zero)
    v_s[...] = jnp.where(lane < 64, zero, mine)
    dattn = jnp.where(lanes(GROUPS) < 64, 0.0, dattn_ref[...]).astype(BF16)
    for n in range(4):
        rows = slice(n * QUARTER, (n + 1) * QUARTER)
        member = quarter_member(lens_ref, n // 2, n % 2)
        spread = lax.dot_general(member.astype(BF16), dattn, TN, preferred_element_type=F32)
        y_s[rows, :] = jnp.where(lane < 64, y_ref[rows, :], spread.astype(BF16))
        delta = jnp.where(place_ref[1] == n % 2, mine_ref[...], other_ref[...])
        delta = jnp.where(place_ref[0] == n // 2, delta[0:8], delta[8:16])
        for part in range(8):
            at = n * QUARTER + part * 128
            delta_s[:, at : at + 128] = jnp.broadcast_to(delta[part : part + 1, :], (8, 128))

    def block(i, carry):
        rows = pl.ds(pl.multiple_of(i * TALL, TALL), TALL)
        total = jnp.zeros((TALL, 128), F32)
        for n in range(KEYS // CHUNK):
            cols = slice(n * CHUNK, (n + 1) * CHUNK)
            part = y_s[cols, :]
            scores = lax.dot_general(k_s[rows, :], part, NT, preferred_element_type=F32)
            prob_grad = lax.dot_general(v_s[rows, :], part, NT, preferred_element_type=F32)
            score_grad = (
                jnp.exp(scores - lse_ref[0:1, cols]) * (prob_grad - delta_s[0:1, cols])
            ).astype(BF16)
            total = total + jnp.dot(score_grad, part, preferred_element_type=F32)
        both = jnp.where(lanes(TALL) < 64, total.astype(BF16), grad_q_ref[rows, :])
        count = TALL // HALF
        out_ref[pl.ds(i * count, count), :, :] = both.reshape(count, HALF, 128)
        return carry

    lax.fori_loop(0, QUARTER // TALL, block, 0)


SMEM = pl.BlockSpec(memory_space=pltpu.SMEM)
VMEM = pl.BlockSpec(memory_space=pltpu.VMEM)


def call(kernel, outs, scalars, arrays, scratch, estimate, name):
    return pl.pallas_call(
        kernel,
        out_shape=outs,
        in_specs=[SMEM] * len(scalars) + [VMEM] * len(arrays),
        out_specs=jax.tree.map(lambda _: VMEM, outs),
        scratch_shapes=scratch,
        compiler_params=params(56 if name == "pack" else 40 if scratch else 12),
        cost_estimate=estimate,
        name=name,
    )(*scalars, *arrays)


def shape(dims, dtype):
    return jax.ShapeDtypeStruct(dims, dtype)


def body(inputs, q_heads, k_heads, v_heads, w_out, group_lens, query_emb, positive):
    plane = lax.axis_index("yl")
    half = lax.axis_index("zd")
    head = lax.axis_index(HEADS)
    first = lax.axis_index(SEQ) * ROWS
    doc = lax.axis_index(GRP).reshape(1).astype(jnp.int32)
    place = jnp.stack([plane, half, head, first]).astype(jnp.int32)
    lengths = group_lens[0]
    exchange = functools.partial(lax.all_to_all, split_axis=0, concat_axis=0)
    barrier = lax.optimization_barrier
    pairs = QUARTER * KEYS

    packed = call(
        pack_kernel, shape((PLANE, 112, 128), BF16), (place, lengths),
        (q_heads[0], k_heads[0], v_heads[0], inputs[0]), (), cost(0, 1000000), "pack",
    )
    packed, query_emb, positive = barrier((packed, query_emb, positive))
    tagged = jnp.concatenate(
        [query_emb, jnp.pad(positive.astype(BF16)[:, None], ((0, 0), (0, 127)))], axis=1
    )
    own = exchange(packed, ZED)
    queries = gather(tagged, ("yh", "yl", "xa"))
    own, queries = barrier((own, queries))
    keys = share(own[:, 0:96, :], SQUARE)
    queries = gather(queries, ("xb", "co"))
    query_rows = call(
        query_kernel, shape((16, HELD), F32), (), (queries,), (), cost(6 * 2 * 8 * HELD * 1024, 1200000),
        "queries",
    )
    own, keys, queries, query_rows = barrier((own, keys, queries, query_rows))

    rows, mine, spare, lse, means = call(
        forward_kernel,
        (
            shape((KEYS, 128), BF16),
            shape((QUARTER, 128), BF16),
            shape((SPARE, 128), BF16),
            shape((8, 128), F32),
            shape((2 * GROUPS, 128), F32),
        ),
        (place, lengths), (own, keys), [pltpu.VMEM((QUARTER, 128), BF16)],
        cost(pairs * 256 * 4, 3000000, pairs), "forward",
    )
    other_means = swap(means, ("yl",), 1)
    means = call(
        plane_kernel, shape((PLANE, 3 * GROUPS, 128), F32), (), (means, other_means), (),
        cost(0, 200000), "plane",
    )
    spare, means = barrier((spare, means))
    means = exchange(means, ZED)
    other_spare = swap(spare, ("yl",), 1)
    means, other_spare = barrier((means, other_spare))
    pooled_own, doc_means, logits, sums = call(
        pool_kernel,
        (
            shape((GROUPS, MODEL), F32),
            shape((GROUPS, WIDTH), F32),
            shape((GROUPS, HELD), F32),
            shape((DOCS, 8, 128), F32),
        ),
        (doc,), (means, w_out, queries, query_rows), (), cost(2 * 32 * 768 * 1024, 1800000), "pool",
    )
    sums = exchange(sums, GRP)
    ready = call(
        prepare_kernel, shape((24, 128), F32), (place,), (pooled_own, w_out), (),
        cost(2 * 32 * 128 * 1024, 1200000), "prepare",
    )
    sums, ready = barrier((sums, ready))
    terms = call(
        loss_kernel, shape((PLANE, 16, 128), F32), (doc,),
        (sums, logits, pooled_own, queries, query_rows, w_out), (),
        cost(2 * 32 * 768 * 1024, 1800000, 2000), "loss",
    )
    terms, own, keys = barrier((terms, own, keys))
    terms = exchange(terms, ZED)
    mass, lse_rows, columns = call(
        mass_kernel,
        (shape((GROUPS, 8, 128), F32), shape((8, KEYS), F32), shape((KEYS, 128), BF16)),
        (place, lengths), (own, keys, means),
        [pltpu.VMEM((QUARTER, 128), BF16), pltpu.VMEM((128, KEYS), BF16)],
        cost(pairs * 256 * 4, 2500000, pairs), "mass",
    )
    terms, mass, lse_rows = barrier((terms, mass, lse_rows))

    dattn, grad_part, loss, delta = call(
        group_kernel,
        (
            shape((GROUPS, 128), F32),
            shape((PLANE, GROUPS, 128), F32),
            shape((GROUPS, 128), F32),
            shape((2 * GROUPS, 128), F32),
        ),
        (place, lengths), (terms, ready, mass, spare, other_spare), (), cost(0, 100000), "group",
    )
    mean_loss = loss[0, 64]
    grad_parts = exchange(grad_part, ZED)
    other_delta = swap(delta, ("zd",), 1)
    grad_rows = call(
        row_kernel, shape((QUARTER, 128), BF16), (place, lengths), (mine, lse, rows, dattn),
        [
            pltpu.VMEM((QUARTER, 128), BF16),
            pltpu.VMEM((QUARTER, 128), BF16),
            pltpu.VMEM((QUARTER, 128), F32),
        ],
        cost(pairs * 256 * 6, 2000000, pairs), "rows",
    )
    grad_inputs, grads = call(
        inputs_kernel,
        (shape((ROWS, MODEL), BF16), shape((DOCS, 2 * GROUPS, (MODEL + WIDTH) // 2), BF16)),
        (place, lengths), (grad_parts, doc_means), (), cost(2 * 32 * 128 * 1024, 1200000), "inputs",
    )
    grad_rows, grads, other_delta = barrier((grad_rows, grads, other_delta))
    all_grads = exchange(grads, GRP)
    packed_grads = call(
        column_kernel, shape((PLANE, HALF, 128), BF16), (place, lengths),
        (own, columns, delta, other_delta, lse_rows, dattn, grad_rows),
        [
            pltpu.VMEM((KEYS, 128), BF16),
            pltpu.VMEM((QUARTER, 128), BF16),
            pltpu.VMEM((QUARTER, 128), BF16),
            pltpu.VMEM((8, KEYS), F32),
        ],
        cost(pairs * 256 * 6, 2500000, pairs), "columns",
    )
    packed_grads, grad_parts = barrier((packed_grads, grad_parts))
    home = exchange(packed_grads, ZED)
    out = shape((ROWS, WIDTH), BF16)
    grad_v = call(
        value_kernel, out, (lengths,), (grad_parts, w_out), (), cost(2 * 32 * 512 * 1024, 1300000),
        "values",
    )
    grad_w_out = call(
        weight_kernel, shape((WIDTH, MODEL), F32), (), (all_grads,), (),
        cost(2 * 384 * 512 * 1024, 3000000), "weights",
    )
    grad_q, grad_k = call(
        unpack_kernel, (out, out), (), (home,), (), cost(0, 500000), "unpack"
    )
    return (mean_loss, grad_inputs[None], grad_q[None], grad_k[None], grad_v[None], grad_w_out)


def solution(mesh):
    fine = Mesh(mesh.devices.reshape((2,) * 9), GRP + SEQ)
    rows = P(GRP, SEQ, None)
    return jax.shard_map(
        body,
        mesh=fine,
        in_specs=(
            rows,
            rows,
            rows,
            rows,
            P(),
            P(GRP, None),
            P(GRP + SEQ, None),
            P(GRP + SEQ),
        ),
        out_specs=(P(), rows, rows, rows, rows, P()),
        check_vma=False,
    )
```

```python
import functools

import jax
import jax.numpy as jnp
from jax import lax
from jax.experimental import pallas as pl
from jax.experimental.pallas import tpu as pltpu
from jax.sharding import Mesh, PartitionSpec as P

HEAD_COUNT = 8
HEAD_DIM = 64
GROUPS = 8
DOCS = 16
MODEL = 1024
WIDTH = 512
ROWS = 128
HALF = 64
QUARTER = 1024
PLANE = 16
SCALE = HEAD_DIM ** (-0.5)

RECIPROCAL_TEMP = 20.0
GRADIENT_FACTOR = 64.0
NORM_EPS = 1e-06
QUERY_COUNT = 8192
EXACT = lax.Precision.HIGHEST

BF16 = jnp.bfloat16
F32 = jnp.float32

GRP = ("yh", "xa", "xb", "co")
SEQ = ("yl", "za", "zb", "zc", "zd")
ZED = ("za", "zb", "zc", "zd")
SQUARE = ("yl", "zd")
HEADS = ("za", "zb", "zc")
NT = (((1,), (1,)), ((), ()))
TN = (((0,), (0,)), ((), ()))

HELD = 512


def params(mebibytes):
    return pltpu.CompilerParams(vmem_limit_bytes=mebibytes << 20)


def cost(flops, moved, exps=0):
    return pl.CostEstimate(flops=int(flops), bytes_accessed=int(moved), transcendentals=int(exps))


def share(value, axes):
    count = 2 ** len(axes)
    return lax.all_to_all(
        jnp.broadcast_to(value[None], (count,) + value.shape), axes, split_axis=0, concat_axis=0
    )


def swap(value, axes, flip):
    count = 2 ** len(axes)
    return lax.ppermute(value, axes, [(i, i ^ flip) for i in range(count)])


def gather(value, axes):
    for axis in axes:
        other = swap(value, (axis,), 1)
        first = lax.axis_index(axis) == 0
        value = jnp.where(
            first,
            jnp.concatenate([value, other], axis=0),
            jnp.concatenate([other, value], axis=0),
        )
    return value


def three(value):
    high = value.astype(BF16)
    rest = value - high.astype(F32)
    middle = rest.astype(BF16)
    low = (rest - middle.astype(F32)).astype(BF16)
    return high, middle, low


def stacked(value):
    parts = [part.astype(F32) for part in three(value)]
    parts.append(jnp.zeros_like(value))
    return jnp.concatenate(parts, axis=0).astype(BF16)


def folded(product):
    return (product[16:24] + product[8:16]) + product[0:8]


def column_of(values):
    row = lax.broadcasted_iota(jnp.int32, (GROUPS, 128), 0)
    out = jnp.full((GROUPS, 128), values[0])
    for n in range(1, GROUPS):
        out = jnp.where(row == n, values[n], out)
    return out


def member_of(position, lens_ref):
    ends = [lens_ref[0]]
    for n in range(1, GROUPS):
        ends.append(ends[-1] + lens_ref[n])
    last = column_of(ends)
    first = last - column_of([lens_ref[n] for n in range(GROUPS)])
    return ((position >= first[:, 0:1]) & (position < last[:, 0:1])).astype(F32)


def lengths_of(lens_ref):
    return column_of([lens_ref[n] for n in range(GROUPS)]).astype(F32)


def quarter_member(lens_ref, plane, half):
    row = lax.broadcasted_iota(jnp.int32, (GROUPS, QUARTER), 1)
    position = plane * (PLANE * ROWS) + (row >> 6) * ROWS + half * HALF + (row & 63)
    return member_of(position, lens_ref)


def local_member(lens_ref, first):
    return member_of(first + lax.broadcasted_iota(jnp.int32, (GROUPS, ROWS), 1), lens_ref)


def halves(packed):
    return jnp.concatenate([packed[:, :, 0:64], packed[:, :, 64:128]], axis=1)


def lanes(rows):
    return lax.broadcasted_iota(jnp.int32, (rows, 128), 1)


def pack_kernel(place_ref, lens_ref, q_ref, k_ref, v_ref, inputs_ref, out_ref):
    mine = local_member(lens_ref, place_ref[3]).astype(BF16)
    sums = jnp.dot(mine, inputs_ref[...], preferred_element_type=F32)
    high, middle, low = [part.astype(F32) for part in three(sums)]
    zero = jnp.zeros((GROUPS, HALF), F32)
    for head in range(HEAD_COUNT):
        cols = slice(head * HEAD_DIM, (head + 1) * HEAD_DIM)
        for half in range(2):
            rows = slice(half * HALF, (half + 1) * HALF)
            place = 2 * head + half
            out_ref[place, 0:64, :] = jnp.concatenate([k_ref[rows, cols], v_ref[rows, cols]], axis=1)
            query = q_ref[rows, cols] * jnp.asarray(SCALE, BF16)
            out_ref[place, 64:96, :] = jnp.concatenate([query[0:32], query[32:64]], axis=1)
            part = slice(place * HALF, (place + 1) * HALF)
            upper = jnp.concatenate([high[:, part], middle[:, part]], axis=1)
            lower = jnp.concatenate([low[:, part], zero], axis=1)
            out_ref[place, 96:112, :] = jnp.concatenate([upper, lower], axis=0).astype(BF16)


def unpack_kernel(in_ref, q_ref, k_ref):
    for pair in range(HEAD_COUNT // 2):
        cols = slice(pair * 128, (pair + 1) * 128)
        for half in range(2):
            rows = slice(half * HALF, (half + 1) * HALF)
            first, second = in_ref[4 * pair + half], in_ref[4 * pair + 2 + half]
            k_ref[rows, cols] = jnp.concatenate([first[:, 0:64], second[:, 0:64]], axis=1)
            q_ref[rows, cols] = jnp.concatenate([first[:, 64:128], second[:, 64:128]], axis=1)


BLOCK = 512
PARTS = BLOCK // 128


KEYS = 4 * QUARTER
SPARE = 512


def fill(all_ref, x_ref):
    for n in range(4):
        x_ref[n * QUARTER : (n + 1) * QUARTER, :] = all_ref[n, :, 0:64, :].reshape(QUARTER, 128)


def own_queries(own_ref):
    queries = halves(own_ref[:, 64:96, :]).reshape(QUARTER, HEAD_DIM)
    return jnp.concatenate([queries, jnp.zeros_like(queries)], axis=1)


def turned(lines):
    columns = []
    for part in range(8):
        line = jnp.broadcast_to(lines[part : part + 1, :], (128, 128))
        columns.append(jnp.transpose(line))
    return jnp.concatenate(columns, axis=0)


def forward_kernel(
    place_ref, lens_ref, own_ref, all_ref, spare_ref, lse_ref, means_ref, x_ref, y_ref, q_s
):
    fill(all_ref, x_ref)
    q_s[...] = own_queries(own_ref)

    def block(i, carry):
        rows = pl.ds(pl.multiple_of(i * BLOCK, BLOCK), BLOCK)
        scores = lax.dot_general(q_s[rows, :], x_ref[...], NT, preferred_element_type=F32)
        top = jnp.max(scores, axis=1, keepdims=True)
        grown = jnp.exp(scores - top)
        total = jnp.sum(grown, axis=1, keepdims=True)
        prob = (grown * (1.0 / total)).astype(BF16)
        mixed = jnp.dot(prob, x_ref[...], preferred_element_type=F32).astype(BF16)
        y_ref[rows, :] = jnp.where(lanes(BLOCK) < 64, q_s[rows, :], mixed)
        log_total = top + jnp.log(total)
        for part in range(PARTS):
            square = jnp.broadcast_to(log_total[part * 128 : (part + 1) * 128], (128, 128))
            lse_ref[pl.ds(i * PARTS + part, 1), :] = jnp.transpose(square)[0:1, :]
        return carry

    lax.fori_loop(0, QUARTER // BLOCK, block, 0)
    spare_ref[...] = jnp.concatenate(
        [y_ref[0:512, :][:, 64:128], y_ref[512:1024, :][:, 64:128]], axis=1
    )
    member = quarter_member(lens_ref, place_ref[0], place_ref[1]).astype(BF16)
    attn_sums = jnp.dot(member, y_ref[0:QUARTER, :], preferred_element_type=F32)
    sums = jnp.sum(own_ref[:, 96:112, :].astype(F32), axis=0)
    input_sums = (sums[0:8] + pltpu.roll(sums[0:8], 64, 1)) + sums[8:16]
    means = jnp.where(lanes(GROUPS) < 64, input_sums, attn_sums) / lengths_of(lens_ref)
    means_ref[...] = jnp.concatenate([means, lse_ref[...]], axis=0)


def plane_kernel(mine_ref, other_ref, out_ref):
    mine, other = mine_ref[...], other_ref[...]
    both = jnp.concatenate([mine[0:8] + other[0:8], mine[8:16], other[8:16]], axis=0)
    out_ref[...] = jnp.broadcast_to(both[None], (PLANE, 3 * GROUPS, 128))


def pool_kernel(doc_ref, means_ref, w_ref, query_ref, row_ref, own_ref, means_out_ref, logits_ref, out_ref):
    columns = [means_ref[z, 0:8, 0:64] for z in range(PLANE)]
    heads = [
        means_ref[z, 0:8, 64:128] + means_ref[z + 1, 0:8, 64:128] for z in range(0, PLANE, 2)
    ]
    means = jnp.concatenate(heads, axis=1)
    projected = jnp.dot(stacked(means), w_ref[...], preferred_element_type=F32)
    pooled = jnp.concatenate(columns, axis=1) + folded(projected)
    own_ref[...] = pooled
    means_out_ref[...] = means
    unit = pooled / jnp.sqrt(jnp.sum(pooled * pooled, axis=1, keepdims=True) + NORM_EPS)
    logits = folded(
        lax.dot_general(stacked(unit), query_ref[:, :MODEL], NT, preferred_element_type=F32)
    )
    logits = logits * (RECIPROCAL_TEMP / row_ref[0:1, :])
    logits_ref[...] = logits
    group = doc_ref[0] * GROUPS + lax.broadcasted_iota(jnp.int32, logits.shape, 0)
    target = (group == row_ref[8:9, :].astype(jnp.int32)).astype(F32)
    total = jnp.sum(jnp.exp(logits), axis=0, keepdims=True)
    chosen = jnp.sum(target * logits, axis=0, keepdims=True)
    sums = jnp.concatenate(
        [row[:, n : n + 128] for row in (total, chosen) for n in range(0, HELD, 128)], axis=0
    )
    out_ref[...] = jnp.broadcast_to(sums[None], (DOCS, 8, 128))


def prepare_kernel(place_ref, pooled_ref, w_ref, out_ref):
    head = place_ref[2]
    pooled = pooled_ref[...]
    norms = jnp.sqrt(jnp.sum(pooled * pooled, axis=1, keepdims=True) + NORM_EPS)
    unit = pooled / norms
    w_head = w_ref[pl.ds(pl.multiple_of(head * HEAD_DIM, HEAD_DIM), HEAD_DIM), :]
    w_twice = jnp.concatenate([w_head, w_head], axis=0)
    out_ref[0:8, :] = folded(
        lax.dot_general(stacked(unit), w_twice, NT, preferred_element_type=F32)
    )
    z = 2 * head + place_ref[1]
    part = unit[:, 0:64]
    for n in range(1, PLANE):
        part = jnp.where(z == n, unit[:, n * HALF : (n + 1) * HALF], part)
    out_ref[8:16, :] = jnp.concatenate([part, part], axis=1)
    out_ref[16:24, :] = jnp.broadcast_to(norms, (GROUPS, 128))


def query_kernel(query_ref, out_ref):
    query = query_ref[:, :MODEL].astype(F32)
    squares = lax.dot_general(
        jnp.ones((8, MODEL), F32), query * query, NT, precision=EXACT, preferred_element_type=F32
    )
    out_ref[0:8, :] = jnp.sqrt(squares + NORM_EPS)
    out_ref[8:16, :] = lax.dot_general(
        jnp.ones((8, 128), BF16), query_ref[:, MODEL:], NT, preferred_element_type=F32
    )


def loss_kernel(doc_ref, sums_ref, logits_ref, own_ref, query_ref, row_ref, w_ref, out_ref):
    sums = sums_ref[0]
    for n in range(1, DOCS):
        sums = sums + sums_ref[n]
    total = jnp.concatenate([sums[n : n + 1] for n in range(4)], axis=1)
    losses = jnp.log(sums[0:4]) - sums[4:8]
    loss = jnp.sum(jnp.sum(losses, axis=1, keepdims=True), axis=0, keepdims=True)
    query = query_ref[:, :MODEL]
    scale = RECIPROCAL_TEMP / row_ref[0:1, :]
    logits = logits_ref[...]
    group = doc_ref[0] * GROUPS + lax.broadcasted_iota(jnp.int32, logits.shape, 0)
    target = (group == row_ref[8:9, :].astype(jnp.int32)).astype(F32)
    weight = (jnp.exp(logits) / total - target) * (GRADIENT_FACTOR * scale)
    grad = folded(jnp.dot(stacked(weight), query, preferred_element_type=F32))
    own = own_ref[...]
    own_unit = own / jnp.sqrt(jnp.sum(own * own, axis=1, keepdims=True) + NORM_EPS)
    along = jnp.sum(own_unit * grad, axis=1, keepdims=True)
    spread = folded(
        lax.dot_general(stacked(grad), w_ref[...], NT, preferred_element_type=F32)
    )
    extra = jnp.where(lanes(GROUPS) < 64, along, loss)
    for z in range(PLANE):
        head = z // 2
        chunk = jnp.concatenate(
            [
                spread[:, head * HEAD_DIM : (head + 1) * HEAD_DIM],
                grad[:, z * HALF : (z + 1) * HALF],
            ],
            axis=1,
        )
        out_ref[z, 0:8, :] = chunk
        out_ref[z, 8:16, :] = extra


def mass_kernel(
    place_ref, lens_ref, own_ref, all_ref, means_ref, mass_ref, lse_ref, y_ref, k_s, member_s
):
    mine = own_ref[:, 0:64, :].reshape(QUARTER, 128)
    k_s[...] = jnp.where(lanes(QUARTER) < 64, mine, jnp.zeros_like(mine))
    for n in range(4):
        queries = halves(all_ref[n, :, 64:96, :]).reshape(QUARTER, HEAD_DIM)
        y_ref[n * QUARTER : (n + 1) * QUARTER, :] = jnp.concatenate(
            [queries, jnp.zeros_like(queries)], axis=1
        )
        both = means_ref[2 * place_ref[2] + n % 2]
        lse = jnp.where(place_ref[0] == n // 2, both[8:16], both[16:24])
        for part in range(8):
            at = n * QUARTER + part * 128
            lse_ref[:, at : at + 128] = jnp.broadcast_to(lse[part : part + 1, :], (8, 128))
        member = quarter_member(lens_ref, n // 2, n % 2)
        padded = jnp.concatenate([member, jnp.zeros((120, QUARTER), F32)], axis=0)
        member_s[:, n * QUARTER : (n + 1) * QUARTER] = padded.astype(BF16)

    def block(i, carry):
        rows = pl.ds(pl.multiple_of(i * BLOCK, BLOCK), BLOCK)
        sums = jnp.zeros((BLOCK, 128), F32)
        for n in range(4):
            cols = slice(n * QUARTER, (n + 1) * QUARTER)
            scores = lax.dot_general(k_s[rows, :], y_ref[cols, :], NT, preferred_element_type=F32)
            prob = jnp.exp(scores - lse_ref[0:1, cols]).astype(BF16)
            sums = sums + lax.dot_general(
                prob, member_s[:, cols], NT, preferred_element_type=F32
            )
        for part in range(PARTS):
            mass_ref[i * PARTS + part] = jnp.transpose(sums[part * 128 : (part + 1) * 128])[0:8, :]
        return carry

    lax.fori_loop(0, QUARTER // BLOCK, block, 0)


def rows_of(line):
    return jnp.concatenate([line[:, n : n + 128] for n in range(0, QUARTER, 128)], axis=0)


def group_kernel(
    place_ref, lens_ref, terms_ref, ready_ref, mass_ref, spare_ref, other_ref,
    dattn_ref, grad_ref, loss_ref, delta_ref,
):
    sums = terms_ref[0]
    for n in range(1, PLANE):
        sums = sums + terms_ref[n]
    along = sums[8:16, 0:1]
    loss_ref[...] = sums[8:16, :] / QUERY_COUNT
    norms = ready_ref[16:24, :]
    raw = jnp.concatenate([sums[0:8, 0:64], sums[0:8, 0:64]], axis=1)
    dattn = (raw - ready_ref[0:8, :] * along) / norms / lengths_of(lens_ref)
    dattn_ref[...] = dattn
    lane = lanes(GROUPS)
    ends = [
        jnp.where(lane < 64, dattn, 0.0).astype(BF16),
        jnp.where(lane < 64, 0.0, dattn).astype(BF16),
    ]
    for n, (attn, plane) in enumerate(
        ((spare_ref, place_ref[0]), (other_ref, 1 - place_ref[0]))
    ):
        products = jnp.concatenate(
            [lax.dot_general(part, attn[...], NT, preferred_element_type=F32) for part in ends],
            axis=1,
        )
        member = quarter_member(lens_ref, plane, place_ref[1])
        delta_ref[n * 8 : (n + 1) * 8, :] = rows_of(
            jnp.sum(products * member, axis=0, keepdims=True)
        )
    grad = (sums[0:8, 64:128] - ready_ref[8:16, 0:64] * along) / norms[:, 0:64]
    for z in range(PLANE):
        half = (z % 2) * HALF
        grad_ref[z] = jnp.concatenate([grad, mass_ref[z // 2, :, half : half + HALF]], axis=1)


def inputs_kernel(place_ref, lens_ref, parts_ref, means_ref, grad_inputs_ref, out_ref):
    grad = jnp.concatenate([parts_ref[z, :, 0:64] for z in range(PLANE)], axis=1)
    mine = local_member(lens_ref, place_ref[3])
    members = jnp.concatenate([mine, mine, mine, mine], axis=0).astype(BF16)
    grad_inputs_ref[...] = lax.dot_general(
        members, stacked(grad / lengths_of(lens_ref)[:, 0:1]), TN, preferred_element_type=F32
    ).astype(BF16)
    both = jnp.concatenate([grad, means_ref[...]], axis=1)
    wide = (MODEL + WIDTH) // 2
    both = jnp.concatenate([both[:, :wide], both[:, wide:]], axis=0)
    out_ref[...] = jnp.broadcast_to(both.astype(BF16)[None], (DOCS, 2 * GROUPS, wide))


def value_kernel(lens_ref, parts_ref, w_ref, grad_v_ref):
    grad = jnp.concatenate([parts_ref[z, :, 0:64] for z in range(PLANE)], axis=1)
    grad = grad / lengths_of(lens_ref)[:, 0:1]
    dattn = folded(lax.dot_general(stacked(grad), w_ref[...], NT, preferred_element_type=F32))
    dattn = dattn.astype(BF16).astype(F32)
    dattn = jnp.concatenate([dattn, dattn, dattn, jnp.zeros_like(dattn)], axis=0).astype(BF16)
    for pair in range(HEAD_COUNT // 2):
        cols = slice(pair * 128, (pair + 1) * 128)
        both = []
        for head in (2 * pair, 2 * pair + 1):
            mass = jnp.concatenate(
                [parts_ref[2 * head, :, 64:128], parts_ref[2 * head + 1, :, 64:128]], axis=1
            )
            both.append(
                lax.dot_general(stacked(mass), dattn[:, cols], TN, preferred_element_type=F32)
            )
        grad_v_ref[:, cols] = jnp.where(lanes(ROWS) < 64, both[0], both[1]).astype(BF16)


def weight_kernel(in_ref, out_ref):
    wide = (MODEL + WIDTH) // 2
    both = in_ref[...].astype(F32)
    both = [both[:, n : n + 8].reshape(DOCS * GROUPS, wide) for n in (0, 8)]
    both = jnp.concatenate(both, axis=1).astype(BF16)
    out_ref[...] = lax.dot_general(
        both[:, MODEL:], both[:, :MODEL], TN, preferred_element_type=F32
    )


CHUNK = 512
TALL = 1024


def row_kernel(
    place_ref, lens_ref, own_ref, all_ref, lse_ref, delta_ref, dattn_ref,
    out_ref, x_ref, q_s, d_s, delta_s, lse_s,
):
    fill(all_ref, x_ref)
    q_s[...] = own_queries(own_ref)
    member = quarter_member(lens_ref, place_ref[0], place_ref[1]).astype(BF16)
    spread = lax.dot_general(
        member, dattn_ref[...].astype(BF16), TN, preferred_element_type=F32
    )
    d_s[...] = jnp.where(lanes(QUARTER) < 64, 0.0, spread).astype(BF16)
    delta_s[...] = turned(delta_ref[0:8, :])
    lse_s[...] = turned(lse_ref[...])

    def block(i, carry):
        rows = pl.ds(pl.multiple_of(i * TALL, TALL), TALL)
        log_total, delta = lse_s[rows, 0:1], delta_s[rows, 0:1]
        total = jnp.zeros((TALL, 128), F32)
        for n in range(KEYS // CHUNK):
            part = x_ref[n * CHUNK : (n + 1) * CHUNK, :]
            scores = lax.dot_general(q_s[rows, :], part, NT, preferred_element_type=F32)
            prob_grad = lax.dot_general(d_s[rows, :], part, NT, preferred_element_type=F32)
            score_grad = (jnp.exp(scores - log_total) * (prob_grad - delta)).astype(BF16)
            total = total + jnp.dot(score_grad, part, preferred_element_type=F32)
        total = total * SCALE
        out_ref[rows, :] = jnp.concatenate([total[:, 0:64]] * 2, axis=1).astype(BF16)
        return carry

    lax.fori_loop(0, QUARTER // TALL, block, 0)


def column_kernel(
    place_ref, lens_ref, own_ref, y_ref, mine_ref, other_ref, lse_ref, dattn_ref, grad_q_ref,
    out_ref, y_s, k_s, v_s, delta_s,
):
    lane = lanes(QUARTER)
    mine = own_ref[:, 0:64, :].reshape(QUARTER, 128)
    zero = jnp.zeros_like(mine)
    k_s[...] = jnp.where(lane < 64, mine, zero)
    v_s[...] = jnp.where(lane < 64, zero, mine)
    dattn = jnp.where(lanes(GROUPS) < 64, 0.0, dattn_ref[...]).astype(BF16)
    for n in range(4):
        rows = slice(n * QUARTER, (n + 1) * QUARTER)
        member = quarter_member(lens_ref, n // 2, n % 2)
        spread = lax.dot_general(member.astype(BF16), dattn, TN, preferred_element_type=F32)
        y_s[rows, :] = jnp.where(lane < 64, y_ref[rows, :], spread.astype(BF16))
        delta = jnp.where(place_ref[1] == n % 2, mine_ref[...], other_ref[...])
        delta = jnp.where(place_ref[0] == n // 2, delta[0:8], delta[8:16])
        for part in range(8):
            at = n * QUARTER + part * 128
            delta_s[:, at : at + 128] = jnp.broadcast_to(delta[part : part + 1, :], (8, 128))

    def block(i, carry):
        rows = pl.ds(pl.multiple_of(i * TALL, TALL), TALL)
        total = jnp.zeros((TALL, 128), F32)
        for n in range(KEYS // CHUNK):
            cols = slice(n * CHUNK, (n + 1) * CHUNK)
            part = y_s[cols, :]
            scores = lax.dot_general(k_s[rows, :], part, NT, preferred_element_type=F32)
            prob_grad = lax.dot_general(v_s[rows, :], part, NT, preferred_element_type=F32)
            score_grad = (
                jnp.exp(scores - lse_ref[0:1, cols]) * (prob_grad - delta_s[0:1, cols])
            ).astype(BF16)
            total = total + jnp.dot(score_grad, part, preferred_element_type=F32)
        both = jnp.where(lanes(TALL) < 64, total.astype(BF16), grad_q_ref[rows, :])
        count = TALL // HALF
        out_ref[pl.ds(i * count, count), :, :] = both.reshape(count, HALF, 128)
        return carry

    lax.fori_loop(0, QUARTER // TALL, block, 0)


SMEM = pl.BlockSpec(memory_space=pltpu.SMEM)
VMEM = pl.BlockSpec(memory_space=pltpu.VMEM)


def call(kernel, outs, scalars, arrays, scratch, estimate, name):
    return pl.pallas_call(
        kernel,
        out_shape=outs,
        in_specs=[SMEM] * len(scalars) + [VMEM] * len(arrays),
        out_specs=jax.tree.map(lambda _: VMEM, outs),
        scratch_shapes=scratch,
        compiler_params=params(56 if name == "pack" else 40 if scratch else 12),
        cost_estimate=estimate,
        name=name,
    )(*scalars, *arrays)


def shape(dims, dtype):
    return jax.ShapeDtypeStruct(dims, dtype)


def body(inputs, q_heads, k_heads, v_heads, w_out, group_lens, query_emb, positive):
    plane = lax.axis_index("yl")
    half = lax.axis_index("zd")
    head = lax.axis_index(HEADS)
    first = lax.axis_index(SEQ) * ROWS
    doc = lax.axis_index(GRP).reshape(1).astype(jnp.int32)
    place = jnp.stack([plane, half, head, first]).astype(jnp.int32)
    lengths = group_lens[0]
    exchange = functools.partial(lax.all_to_all, split_axis=0, concat_axis=0)
    barrier = lax.optimization_barrier
    pairs = QUARTER * KEYS

    packed = call(
        pack_kernel, shape((PLANE, 112, 128), BF16), (place, lengths),
        (q_heads[0], k_heads[0], v_heads[0], inputs[0]), (), cost(0, 1000000), "pack",
    )
    packed, query_emb, positive = barrier((packed, query_emb, positive))
    tagged = jnp.concatenate(
        [query_emb, jnp.pad(positive.astype(BF16)[:, None], ((0, 0), (0, 127)))], axis=1
    )
    own = exchange(packed, ZED)
    queries = gather(tagged, ("yh", "yl", "xa"))
    own, queries = barrier((own, queries))
    keys = share(own[:, 0:96, :], SQUARE)
    queries = gather(queries, ("xb", "co"))
    query_rows = call(
        query_kernel, shape((16, HELD), F32), (), (queries,), (), cost(6 * 2 * 8 * HELD * 1024, 1200000),
        "queries",
    )
    own, keys, queries, query_rows = barrier((own, keys, queries, query_rows))

    spare, lse, means = call(
        forward_kernel,
        (
            shape((SPARE, 128), BF16),
            shape((8, 128), F32),
            shape((2 * GROUPS, 128), F32),
        ),
        (place, lengths), (own, keys),
        [
            pltpu.VMEM((KEYS, 128), BF16),
            pltpu.VMEM((QUARTER, 128), BF16),
            pltpu.VMEM((QUARTER, 128), BF16),
        ],
        cost(pairs * 256 * 4, 3000000, pairs), "forward",
    )
    other_means = swap(means, ("yl",), 1)
    means = call(
        plane_kernel, shape((PLANE, 3 * GROUPS, 128), F32), (), (means, other_means), (),
        cost(0, 200000), "plane",
    )
    spare, means = barrier((spare, means))
    means = exchange(means, ZED)
    other_spare = swap(spare, ("yl",), 1)
    means, other_spare = barrier((means, other_spare))
    pooled_own, doc_means, logits, sums = call(
        pool_kernel,
        (
            shape((GROUPS, MODEL), F32),
            shape((GROUPS, WIDTH), F32),
            shape((GROUPS, HELD), F32),
            shape((DOCS, 8, 128), F32),
        ),
        (doc,), (means, w_out, queries, query_rows), (), cost(2 * 32 * 768 * 1024, 1800000), "pool",
    )
    sums = exchange(sums, GRP)
    ready = call(
        prepare_kernel, shape((24, 128), F32), (place,), (pooled_own, w_out), (),
        cost(2 * 32 * 128 * 1024, 1200000), "prepare",
    )
    sums, ready = barrier((sums, ready))
    terms = call(
        loss_kernel, shape((PLANE, 16, 128), F32), (doc,),
        (sums, logits, pooled_own, queries, query_rows, w_out), (),
        cost(2 * 32 * 768 * 1024, 1800000, 2000), "loss",
    )
    terms, own, keys = barrier((terms, own, keys))
    terms = exchange(terms, ZED)
    mass, lse_rows, columns = call(
        mass_kernel,
        (shape((GROUPS, 8, 128), F32), shape((8, KEYS), F32), shape((KEYS, 128), BF16)),
        (place, lengths), (own, keys, means),
        [pltpu.VMEM((QUARTER, 128), BF16), pltpu.VMEM((128, KEYS), BF16)],
        cost(pairs * 256 * 4, 2500000, pairs), "mass",
    )
    terms, mass, lse_rows = barrier((terms, mass, lse_rows))

    dattn, grad_part, loss, delta = call(
        group_kernel,
        (
            shape((GROUPS, 128), F32),
            shape((PLANE, GROUPS, 128), F32),
            shape((GROUPS, 128), F32),
            shape((2 * GROUPS, 128), F32),
        ),
        (place, lengths), (terms, ready, mass, spare, other_spare), (), cost(0, 100000), "group",
    )
    mean_loss = loss[0, 64]
    grad_parts = exchange(grad_part, ZED)
    other_delta = swap(delta, ("zd",), 1)
    grad_rows = call(
        row_kernel, shape((QUARTER, 128), BF16), (place, lengths), (own, keys, lse, delta, dattn),
        [
            pltpu.VMEM((KEYS, 128), BF16),
            pltpu.VMEM((QUARTER, 128), BF16),
            pltpu.VMEM((QUARTER, 128), BF16),
            pltpu.VMEM((QUARTER, 128), F32),
            pltpu.VMEM((QUARTER, 128), F32),
        ],
        cost(pairs * 256 * 6, 2000000, pairs), "rows",
    )
    grad_inputs, grads = call(
        inputs_kernel,
        (shape((ROWS, MODEL), BF16), shape((DOCS, 2 * GROUPS, (MODEL + WIDTH) // 2), BF16)),
        (place, lengths), (grad_parts, doc_means), (), cost(2 * 32 * 128 * 1024, 1200000), "inputs",
    )
    grad_rows, grads, other_delta = barrier((grad_rows, grads, other_delta))
    all_grads = exchange(grads, GRP)
    packed_grads = call(
        column_kernel, shape((PLANE, HALF, 128), BF16), (place, lengths),
        (own, columns, delta, other_delta, lse_rows, dattn, grad_rows),
        [
            pltpu.VMEM((KEYS, 128), BF16),
            pltpu.VMEM((QUARTER, 128), BF16),
            pltpu.VMEM((QUARTER, 128), BF16),
            pltpu.VMEM((8, KEYS), F32),
        ],
        cost(pairs * 256 * 6, 2500000, pairs), "columns",
    )
    packed_grads, grad_parts = barrier((packed_grads, grad_parts))
    home = exchange(packed_grads, ZED)
    out = shape((ROWS, WIDTH), BF16)
    grad_v = call(
        value_kernel, out, (lengths,), (grad_parts, w_out), (), cost(2 * 32 * 512 * 1024, 1300000),
        "values",
    )
    grad_w_out = call(
        weight_kernel, shape((WIDTH, MODEL), F32), (), (all_grads,), (),
        cost(2 * 384 * 512 * 1024, 3000000), "weights",
    )
    grad_q, grad_k = call(
        unpack_kernel, (out, out), (), (home,), (), cost(0, 500000), "unpack"
    )
    return (mean_loss, grad_inputs[None], grad_q[None], grad_k[None], grad_v[None], grad_w_out)


def solution(mesh):
    fine = Mesh(mesh.devices.reshape((2,) * 9), GRP + SEQ)
    rows = P(GRP, SEQ, None)
    return jax.shard_map(
        body,
        mesh=fine,
        in_specs=(
            rows,
            rows,
            rows,
            rows,
            P(),
            P(GRP, None),
            P(GRP + SEQ, None),
            P(GRP + SEQ),
        ),
        out_specs=(P(), rows, rows, rows, rows, P()),
        check_vma=False,
    )
```

```python
import functools

import jax
import jax.numpy as jnp
from jax import lax
from jax.experimental import pallas as pl
from jax.experimental.pallas import tpu as pltpu
from jax.sharding import Mesh, PartitionSpec as P

HEAD_COUNT = 8
HEAD_DIM = 64
GROUPS = 8
DOCS = 16
MODEL = 1024
WIDTH = 512
ROWS = 128
HALF = 64
QUARTER = 1024
PLANE = 16
SCALE = HEAD_DIM ** (-0.5)

RECIPROCAL_TEMP = 20.0
GRADIENT_FACTOR = 64.0
NORM_EPS = 1e-06
QUERY_COUNT = 8192
EXACT = lax.Precision.HIGHEST

BF16 = jnp.bfloat16
F32 = jnp.float32

NEG_LARGE = -1e30

GRP = ("yh", "xa", "xb", "co")
SEQ = ("yl", "za", "zb", "zc", "zd")
ZED = ("za", "zb", "zc", "zd")
SQUARE = ("yl", "zd")
HEADS = ("za", "zb", "zc")
NT = (((1,), (1,)), ((), ()))
TN = (((0,), (0,)), ((), ()))

HELD = 512


def params(mebibytes):
    return pltpu.CompilerParams(vmem_limit_bytes=mebibytes << 20)


def cost(flops, moved, exps=0):
    return pl.CostEstimate(flops=int(flops), bytes_accessed=int(moved), transcendentals=int(exps))


def share(value, axes):
    count = 2 ** len(axes)
    return lax.all_to_all(
        jnp.broadcast_to(value[None], (count,) + value.shape), axes, split_axis=0, concat_axis=0
    )


def swap(value, axes, flip):
    count = 2 ** len(axes)
    return lax.ppermute(value, axes, [(i, i ^ flip) for i in range(count)])


def gather(value, axes):
    for axis in axes:
        other = swap(value, (axis,), 1)
        first = lax.axis_index(axis) == 0
        value = jnp.where(
            first,
            jnp.concatenate([value, other], axis=0),
            jnp.concatenate([other, value], axis=0),
        )
    return value


def three(value):
    high = value.astype(BF16)
    rest = value - high.astype(F32)
    middle = rest.astype(BF16)
    low = (rest - middle.astype(F32)).astype(BF16)
    return high, middle, low


def stacked(value):
    parts = [part.astype(F32) for part in three(value)]
    parts.append(jnp.zeros_like(value))
    return jnp.concatenate(parts, axis=0).astype(BF16)


def folded(product):
    return (product[16:24] + product[8:16]) + product[0:8]


def column_of(values):
    row = lax.broadcasted_iota(jnp.int32, (GROUPS, 128), 0)
    out = jnp.full((GROUPS, 128), values[0])
    for n in range(1, GROUPS):
        out = jnp.where(row == n, values[n], out)
    return out


def member_of(position, lens_ref):
    ends = [lens_ref[0]]
    for n in range(1, GROUPS):
        ends.append(ends[-1] + lens_ref[n])
    last = column_of(ends)
    first = last - column_of([lens_ref[n] for n in range(GROUPS)])
    return ((position >= first[:, 0:1]) & (position < last[:, 0:1])).astype(F32)


def lengths_of(lens_ref):
    return column_of([lens_ref[n] for n in range(GROUPS)]).astype(F32)


def quarter_member(lens_ref, plane, half):
    row = lax.broadcasted_iota(jnp.int32, (GROUPS, QUARTER), 1)
    position = plane * (PLANE * ROWS) + (row >> 6) * ROWS + half * HALF + (row & 63)
    return member_of(position, lens_ref)


def local_member(lens_ref, first):
    return member_of(first + lax.broadcasted_iota(jnp.int32, (GROUPS, ROWS), 1), lens_ref)


def halves(packed):
    return jnp.concatenate([packed[:, :, 0:64], packed[:, :, 64:128]], axis=1)


def lanes(rows):
    return lax.broadcasted_iota(jnp.int32, (rows, 128), 1)


def pack_kernel(place_ref, lens_ref, q_ref, k_ref, v_ref, inputs_ref, out_ref):
    mine = local_member(lens_ref, place_ref[3]).astype(BF16)
    sums = jnp.dot(mine, inputs_ref[...], preferred_element_type=F32)
    high, middle, low = [part.astype(F32) for part in three(sums)]
    zero = jnp.zeros((GROUPS, HALF), F32)
    for head in range(HEAD_COUNT):
        cols = slice(head * HEAD_DIM, (head + 1) * HEAD_DIM)
        for half in range(2):
            rows = slice(half * HALF, (half + 1) * HALF)
            place = 2 * head + half
            out_ref[place, 0:64, :] = jnp.concatenate([k_ref[rows, cols], v_ref[rows, cols]], axis=1)
            query = q_ref[rows, cols] * jnp.asarray(SCALE, BF16)
            out_ref[place, 64:96, :] = jnp.concatenate([query[0:32], query[32:64]], axis=1)
            part = slice(place * HALF, (place + 1) * HALF)
            upper = jnp.concatenate([high[:, part], middle[:, part]], axis=1)
            lower = jnp.concatenate([low[:, part], zero], axis=1)
            out_ref[place, 96:112, :] = jnp.concatenate([upper, lower], axis=0).astype(BF16)


def unpack_kernel(in_ref, q_ref, k_ref):
    for pair in range(HEAD_COUNT // 2):
        cols = slice(pair * 128, (pair + 1) * 128)
        for half in range(2):
            rows = slice(half * HALF, (half + 1) * HALF)
            first, second = in_ref[4 * pair + half], in_ref[4 * pair + 2 + half]
            k_ref[rows, cols] = jnp.concatenate([first[:, 0:64], second[:, 0:64]], axis=1)
            q_ref[rows, cols] = jnp.concatenate([first[:, 64:128], second[:, 64:128]], axis=1)


BLOCK = 512
PARTS = BLOCK // 128


KEYS = 4 * QUARTER
SPARE = 512
CHUNK = 512
TALL = 1024


def fill(all_ref, x_ref):
    for n in range(4):
        x_ref[n * QUARTER : (n + 1) * QUARTER, :] = all_ref[n, :, 0:64, :].reshape(QUARTER, 128)


def own_queries(own_ref):
    queries = halves(own_ref[:, 64:96, :]).reshape(QUARTER, HEAD_DIM)
    return jnp.concatenate([queries, jnp.zeros_like(queries)], axis=1)


def turned(lines):
    columns = []
    for part in range(8):
        line = jnp.broadcast_to(lines[part : part + 1, :], (128, 128))
        columns.append(jnp.transpose(line))
    return jnp.concatenate(columns, axis=0)


def forward_kernel(
    place_ref, lens_ref, own_ref, all_ref, spare_ref, lse_ref, means_ref, x_ref, y_ref, q_s
):
    fill(all_ref, x_ref)
    q_s[...] = own_queries(own_ref)

    top = jnp.full((QUARTER, 128), NEG_LARGE, F32)
    for n in range(KEYS // CHUNK):
        part = x_ref[n * CHUNK : (n + 1) * CHUNK, :]
        scores = lax.dot_general(q_s[...], part, NT, preferred_element_type=F32)
        for m in range(0, CHUNK, 128):
            top = jnp.maximum(top, scores[:, m : m + 128])
    top = jnp.max(top, axis=1, keepdims=True)
    sums = jnp.zeros((QUARTER, 128), F32)
    mixed = jnp.zeros((QUARTER, 128), F32)
    for n in range(KEYS // CHUNK):
        part = x_ref[n * CHUNK : (n + 1) * CHUNK, :]
        scores = lax.dot_general(q_s[...], part, NT, preferred_element_type=F32)
        grown = jnp.exp(scores - top)
        for m in range(0, CHUNK, 128):
            sums = sums + grown[:, m : m + 128]
        mixed = mixed + jnp.dot(grown.astype(BF16), part, preferred_element_type=F32)
    total = jnp.sum(sums, axis=1, keepdims=True)
    y_ref[...] = (mixed * (1.0 / total)).astype(BF16)
    log_total = top + jnp.log(total)
    for part in range(8):
        square = jnp.broadcast_to(log_total[part * 128 : (part + 1) * 128], (128, 128))
        lse_ref[part : part + 1, :] = jnp.transpose(square)[0:1, :]

    spare_ref[...] = jnp.concatenate(
        [y_ref[0:512, :][:, 64:128], y_ref[512:1024, :][:, 64:128]], axis=1
    )
    member = quarter_member(lens_ref, place_ref[0], place_ref[1]).astype(BF16)
    attn_sums = jnp.dot(member, y_ref[0:QUARTER, :], preferred_element_type=F32)
    sums = jnp.sum(own_ref[:, 96:112, :].astype(F32), axis=0)
    input_sums = (sums[0:8] + pltpu.roll(sums[0:8], 64, 1)) + sums[8:16]
    means = jnp.where(lanes(GROUPS) < 64, input_sums, attn_sums) / lengths_of(lens_ref)
    means_ref[...] = jnp.concatenate([means, lse_ref[...]], axis=0)


def plane_kernel(mine_ref, other_ref, out_ref):
    mine, other = mine_ref[...], other_ref[...]
    both = jnp.concatenate([mine[0:8] + other[0:8], mine[8:16], other[8:16]], axis=0)
    out_ref[...] = jnp.broadcast_to(both[None], (PLANE, 3 * GROUPS, 128))


def pool_kernel(doc_ref, means_ref, w_ref, query_ref, row_ref, own_ref, means_out_ref, logits_ref, out_ref):
    columns = [means_ref[z, 0:8, 0:64] for z in range(PLANE)]
    heads = [
        means_ref[z, 0:8, 64:128] + means_ref[z + 1, 0:8, 64:128] for z in range(0, PLANE, 2)
    ]
    means = jnp.concatenate(heads, axis=1)
    projected = jnp.dot(stacked(means), w_ref[...], preferred_element_type=F32)
    pooled = jnp.concatenate(columns, axis=1) + folded(projected)
    own_ref[...] = pooled
    means_out_ref[...] = means
    unit = pooled / jnp.sqrt(jnp.sum(pooled * pooled, axis=1, keepdims=True) + NORM_EPS)
    logits = folded(
        lax.dot_general(stacked(unit), query_ref[:, :MODEL], NT, preferred_element_type=F32)
    )
    logits = logits * (RECIPROCAL_TEMP / row_ref[0:1, :])
    logits_ref[...] = logits
    group = doc_ref[0] * GROUPS + lax.broadcasted_iota(jnp.int32, logits.shape, 0)
    target = (group == row_ref[8:9, :].astype(jnp.int32)).astype(F32)
    total = jnp.sum(jnp.exp(logits), axis=0, keepdims=True)
    chosen = jnp.sum(target * logits, axis=0, keepdims=True)
    sums = jnp.concatenate(
        [row[:, n : n + 128] for row in (total, chosen) for n in range(0, HELD, 128)], axis=0
    )
    out_ref[...] = jnp.broadcast_to(sums[None], (DOCS, 8, 128))


def prepare_kernel(place_ref, pooled_ref, w_ref, out_ref):
    head = place_ref[2]
    pooled = pooled_ref[...]
    norms = jnp.sqrt(jnp.sum(pooled * pooled, axis=1, keepdims=True) + NORM_EPS)
    unit = pooled / norms
    w_head = w_ref[pl.ds(pl.multiple_of(head * HEAD_DIM, HEAD_DIM), HEAD_DIM), :]
    w_twice = jnp.concatenate([w_head, w_head], axis=0)
    out_ref[0:8, :] = folded(
        lax.dot_general(stacked(unit), w_twice, NT, preferred_element_type=F32)
    )
    z = 2 * head + place_ref[1]
    part = unit[:, 0:64]
    for n in range(1, PLANE):
        part = jnp.where(z == n, unit[:, n * HALF : (n + 1) * HALF], part)
    out_ref[8:16, :] = jnp.concatenate([part, part], axis=1)
    out_ref[16:24, :] = jnp.broadcast_to(norms, (GROUPS, 128))


def query_kernel(query_ref, out_ref):
    query = query_ref[:, :MODEL].astype(F32)
    squares = lax.dot_general(
        jnp.ones((8, MODEL), F32), query * query, NT, precision=EXACT, preferred_element_type=F32
    )
    out_ref[0:8, :] = jnp.sqrt(squares + NORM_EPS)
    out_ref[8:16, :] = lax.dot_general(
        jnp.ones((8, 128), BF16), query_ref[:, MODEL:], NT, preferred_element_type=F32
    )


def loss_kernel(doc_ref, sums_ref, logits_ref, own_ref, query_ref, row_ref, w_ref, out_ref):
    sums = sums_ref[0]
    for n in range(1, DOCS):
        sums = sums + sums_ref[n]
    total = jnp.concatenate([sums[n : n + 1] for n in range(4)], axis=1)
    losses = jnp.log(sums[0:4]) - sums[4:8]
    loss = jnp.sum(jnp.sum(losses, axis=1, keepdims=True), axis=0, keepdims=True)
    query = query_ref[:, :MODEL]
    scale = RECIPROCAL_TEMP / row_ref[0:1, :]
    logits = logits_ref[...]
    group = doc_ref[0] * GROUPS + lax.broadcasted_iota(jnp.int32, logits.shape, 0)
    target = (group == row_ref[8:9, :].astype(jnp.int32)).astype(F32)
    weight = (jnp.exp(logits) / total - target) * (GRADIENT_FACTOR * scale)
    grad = folded(jnp.dot(stacked(weight), query, preferred_element_type=F32))
    own = own_ref[...]
    own_unit = own / jnp.sqrt(jnp.sum(own * own, axis=1, keepdims=True) + NORM_EPS)
    along = jnp.sum(own_unit * grad, axis=1, keepdims=True)
    spread = folded(
        lax.dot_general(stacked(grad), w_ref[...], NT, preferred_element_type=F32)
    )
    extra = jnp.where(lanes(GROUPS) < 64, along, loss)
    for z in range(PLANE):
        head = z // 2
        chunk = jnp.concatenate(
            [
                spread[:, head * HEAD_DIM : (head + 1) * HEAD_DIM],
                grad[:, z * HALF : (z + 1) * HALF],
            ],
            axis=1,
        )
        out_ref[z, 0:8, :] = chunk
        out_ref[z, 8:16, :] = extra


def mass_kernel(
    place_ref, lens_ref, own_ref, all_ref, means_ref, mass_ref, lse_ref, y_ref, k_s, member_s
):
    mine = own_ref[:, 0:64, :].reshape(QUARTER, 128)
    k_s[...] = jnp.where(lanes(QUARTER) < 64, mine, jnp.zeros_like(mine))
    for n in range(4):
        queries = halves(all_ref[n, :, 64:96, :]).reshape(QUARTER, HEAD_DIM)
        y_ref[n * QUARTER : (n + 1) * QUARTER, :] = jnp.concatenate(
            [queries, jnp.zeros_like(queries)], axis=1
        )
        both = means_ref[2 * place_ref[2] + n % 2]
        lse = jnp.where(place_ref[0] == n // 2, both[8:16], both[16:24])
        for part in range(8):
            at = n * QUARTER + part * 128
            lse_ref[:, at : at + 128] = jnp.broadcast_to(lse[part : part + 1, :], (8, 128))
        member = quarter_member(lens_ref, n // 2, n % 2)
        padded = jnp.concatenate([member, jnp.zeros((120, QUARTER), F32)], axis=0)
        member_s[:, n * QUARTER : (n + 1) * QUARTER] = padded.astype(BF16)

    def block(i, carry):
        rows = pl.ds(pl.multiple_of(i * BLOCK, BLOCK), BLOCK)
        sums = jnp.zeros((BLOCK, 128), F32)
        for n in range(4):
            cols = slice(n * QUARTER, (n + 1) * QUARTER)
            scores = lax.dot_general(k_s[rows, :], y_ref[cols, :], NT, preferred_element_type=F32)
            prob = jnp.exp(scores - lse_ref[0:1, cols]).astype(BF16)
            sums = sums + lax.dot_general(
                prob, member_s[:, cols], NT, preferred_element_type=F32
            )
        for part in range(PARTS):
            mass_ref[i * PARTS + part] = jnp.transpose(sums[part * 128 : (part + 1) * 128])[0:8, :]
        return carry

    lax.fori_loop(0, QUARTER // BLOCK, block, 0)


def rows_of(line):
    return jnp.concatenate([line[:, n : n + 128] for n in range(0, QUARTER, 128)], axis=0)


def group_kernel(
    place_ref, lens_ref, terms_ref, ready_ref, mass_ref, spare_ref, other_ref,
    dattn_ref, grad_ref, loss_ref, delta_ref,
):
    sums = terms_ref[0]
    for n in range(1, PLANE):
        sums = sums + terms_ref[n]
    along = sums[8:16, 0:1]
    loss_ref[...] = sums[8:16, :] / QUERY_COUNT
    norms = ready_ref[16:24, :]
    raw = jnp.concatenate([sums[0:8, 0:64], sums[0:8, 0:64]], axis=1)
    dattn = (raw - ready_ref[0:8, :] * along) / norms / lengths_of(lens_ref)
    dattn_ref[...] = dattn
    lane = lanes(GROUPS)
    ends = [
        jnp.where(lane < 64, dattn, 0.0).astype(BF16),
        jnp.where(lane < 64, 0.0, dattn).astype(BF16),
    ]
    for n, (attn, plane) in enumerate(
        ((spare_ref, place_ref[0]), (other_ref, 1 - place_ref[0]))
    ):
        products = jnp.concatenate(
            [lax.dot_general(part, attn[...], NT, preferred_element_type=F32) for part in ends],
            axis=1,
        )
        member = quarter_member(lens_ref, plane, place_ref[1])
        delta_ref[n * 8 : (n + 1) * 8, :] = rows_of(
            jnp.sum(products * member, axis=0, keepdims=True)
        )
    grad = (sums[0:8, 64:128] - ready_ref[8:16, 0:64] * along) / norms[:, 0:64]
    for z in range(PLANE):
        half = (z % 2) * HALF
        grad_ref[z] = jnp.concatenate([grad, mass_ref[z // 2, :, half : half + HALF]], axis=1)


def inputs_kernel(place_ref, lens_ref, parts_ref, means_ref, grad_inputs_ref, out_ref):
    grad = jnp.concatenate([parts_ref[z, :, 0:64] for z in range(PLANE)], axis=1)
    mine = local_member(lens_ref, place_ref[3])
    members = jnp.concatenate([mine, mine, mine, mine], axis=0).astype(BF16)
    grad_inputs_ref[...] = lax.dot_general(
        members, stacked(grad / lengths_of(lens_ref)[:, 0:1]), TN, preferred_element_type=F32
    ).astype(BF16)
    both = jnp.concatenate([grad, means_ref[...]], axis=1)
    wide = (MODEL + WIDTH) // 2
    both = jnp.concatenate([both[:, :wide], both[:, wide:]], axis=0)
    out_ref[...] = jnp.broadcast_to(both.astype(BF16)[None], (DOCS, 2 * GROUPS, wide))


def value_kernel(lens_ref, parts_ref, w_ref, grad_v_ref):
    grad = jnp.concatenate([parts_ref[z, :, 0:64] for z in range(PLANE)], axis=1)
    grad = grad / lengths_of(lens_ref)[:, 0:1]
    dattn = folded(lax.dot_general(stacked(grad), w_ref[...], NT, preferred_element_type=F32))
    dattn = dattn.astype(BF16).astype(F32)
    dattn = jnp.concatenate([dattn, dattn, dattn, jnp.zeros_like(dattn)], axis=0).astype(BF16)
    for pair in range(HEAD_COUNT // 2):
        cols = slice(pair * 128, (pair + 1) * 128)
        both = []
        for head in (2 * pair, 2 * pair + 1):
            mass = jnp.concatenate(
                [parts_ref[2 * head, :, 64:128], parts_ref[2 * head + 1, :, 64:128]], axis=1
            )
            both.append(
                lax.dot_general(stacked(mass), dattn[:, cols], TN, preferred_element_type=F32)
            )
        grad_v_ref[:, cols] = jnp.where(lanes(ROWS) < 64, both[0], both[1]).astype(BF16)


def weight_kernel(in_ref, out_ref):
    wide = (MODEL + WIDTH) // 2
    both = in_ref[...].astype(F32)
    both = [both[:, n : n + 8].reshape(DOCS * GROUPS, wide) for n in (0, 8)]
    both = jnp.concatenate(both, axis=1).astype(BF16)
    out_ref[...] = lax.dot_general(
        both[:, MODEL:], both[:, :MODEL], TN, preferred_element_type=F32
    )


def row_kernel(
    place_ref, lens_ref, own_ref, all_ref, lse_ref, delta_ref, dattn_ref,
    out_ref, x_ref, q_s, d_s, delta_s, lse_s,
):
    fill(all_ref, x_ref)
    q_s[...] = own_queries(own_ref)
    member = quarter_member(lens_ref, place_ref[0], place_ref[1]).astype(BF16)
    spread = lax.dot_general(
        member, dattn_ref[...].astype(BF16), TN, preferred_element_type=F32
    )
    d_s[...] = jnp.where(lanes(QUARTER) < 64, 0.0, spread).astype(BF16)
    delta_s[...] = turned(delta_ref[0:8, :])
    lse_s[...] = turned(lse_ref[...])

    def block(i, carry):
        rows = pl.ds(pl.multiple_of(i * TALL, TALL), TALL)
        log_total, delta = lse_s[rows, 0:1], delta_s[rows, 0:1]
        total = jnp.zeros((TALL, 128), F32)
        for n in range(KEYS // CHUNK):
            part = x_ref[n * CHUNK : (n + 1) * CHUNK, :]
            scores = lax.dot_general(q_s[rows, :], part, NT, preferred_element_type=F32)
            prob_grad = lax.dot_general(d_s[rows, :], part, NT, preferred_element_type=F32)
            score_grad = (jnp.exp(scores - log_total) * (prob_grad - delta)).astype(BF16)
            total = total + jnp.dot(score_grad, part, preferred_element_type=F32)
        total = total * SCALE
        out_ref[rows, :] = jnp.concatenate([total[:, 0:64]] * 2, axis=1).astype(BF16)
        return carry

    lax.fori_loop(0, QUARTER // TALL, block, 0)


def column_kernel(
    place_ref, lens_ref, own_ref, y_ref, mine_ref, other_ref, lse_ref, dattn_ref, grad_q_ref,
    out_ref, y_s, k_s, v_s, delta_s,
):
    lane = lanes(QUARTER)
    mine = own_ref[:, 0:64, :].reshape(QUARTER, 128)
    zero = jnp.zeros_like(mine)
    k_s[...] = jnp.where(lane < 64, mine, zero)
    v_s[...] = jnp.where(lane < 64, zero, mine)
    dattn = jnp.where(lanes(GROUPS) < 64, 0.0, dattn_ref[...]).astype(BF16)
    for n in range(4):
        rows = slice(n * QUARTER, (n + 1) * QUARTER)
        member = quarter_member(lens_ref, n // 2, n % 2)
        spread = lax.dot_general(member.astype(BF16), dattn, TN, preferred_element_type=F32)
        y_s[rows, :] = jnp.where(lane < 64, y_ref[rows, :], spread.astype(BF16))
        delta = jnp.where(place_ref[1] == n % 2, mine_ref[...], other_ref[...])
        delta = jnp.where(place_ref[0] == n // 2, delta[0:8], delta[8:16])
        for part in range(8):
            at = n * QUARTER + part * 128
            delta_s[:, at : at + 128] = jnp.broadcast_to(delta[part : part + 1, :], (8, 128))

    def block(i, carry):
        rows = pl.ds(pl.multiple_of(i * TALL, TALL), TALL)
        total = jnp.zeros((TALL, 128), F32)
        for n in range(KEYS // CHUNK):
            cols = slice(n * CHUNK, (n + 1) * CHUNK)
            part = y_s[cols, :]
            scores = lax.dot_general(k_s[rows, :], part, NT, preferred_element_type=F32)
            prob_grad = lax.dot_general(v_s[rows, :], part, NT, preferred_element_type=F32)
            score_grad = (
                jnp.exp(scores - lse_ref[0:1, cols]) * (prob_grad - delta_s[0:1, cols])
            ).astype(BF16)
            total = total + jnp.dot(score_grad, part, preferred_element_type=F32)
        both = jnp.where(lanes(TALL) < 64, total.astype(BF16), grad_q_ref[rows, :])
        count = TALL // HALF
        out_ref[pl.ds(i * count, count), :, :] = both.reshape(count, HALF, 128)
        return carry

    lax.fori_loop(0, QUARTER // TALL, block, 0)


SMEM = pl.BlockSpec(memory_space=pltpu.SMEM)
VMEM = pl.BlockSpec(memory_space=pltpu.VMEM)


def call(kernel, outs, scalars, arrays, scratch, estimate, name):
    return pl.pallas_call(
        kernel,
        out_shape=outs,
        in_specs=[SMEM] * len(scalars) + [VMEM] * len(arrays),
        out_specs=jax.tree.map(lambda _: VMEM, outs),
        scratch_shapes=scratch,
        compiler_params=params(56 if name == "pack" else 40 if scratch else 12),
        cost_estimate=estimate,
        name=name,
    )(*scalars, *arrays)


def shape(dims, dtype):
    return jax.ShapeDtypeStruct(dims, dtype)


def body(inputs, q_heads, k_heads, v_heads, w_out, group_lens, query_emb, positive):
    plane = lax.axis_index("yl")
    half = lax.axis_index("zd")
    head = lax.axis_index(HEADS)
    first = lax.axis_index(SEQ) * ROWS
    doc = lax.axis_index(GRP).reshape(1).astype(jnp.int32)
    place = jnp.stack([plane, half, head, first]).astype(jnp.int32)
    lengths = group_lens[0]
    exchange = functools.partial(lax.all_to_all, split_axis=0, concat_axis=0)
    barrier = lax.optimization_barrier
    pairs = QUARTER * KEYS

    packed = call(
        pack_kernel, shape((PLANE, 112, 128), BF16), (place, lengths),
        (q_heads[0], k_heads[0], v_heads[0], inputs[0]), (), cost(0, 1000000), "pack",
    )
    packed, query_emb, positive = barrier((packed, query_emb, positive))
    tagged = jnp.concatenate(
        [query_emb, jnp.pad(positive.astype(BF16)[:, None], ((0, 0), (0, 127)))], axis=1
    )
    own = exchange(packed, ZED)
    queries = gather(tagged, ("yh", "yl", "xa"))
    own, queries = barrier((own, queries))
    keys = share(own[:, 0:96, :], SQUARE)
    queries = gather(queries, ("xb", "co"))
    query_rows = call(
        query_kernel, shape((16, HELD), F32), (), (queries,), (), cost(6 * 2 * 8 * HELD * 1024, 1200000),
        "queries",
    )
    own, keys, queries, query_rows = barrier((own, keys, queries, query_rows))

    spare, lse, means = call(
        forward_kernel,
        (
            shape((SPARE, 128), BF16),
            shape((8, 128), F32),
            shape((2 * GROUPS, 128), F32),
        ),
        (place, lengths), (own, keys),
        [
            pltpu.VMEM((KEYS, 128), BF16),
            pltpu.VMEM((QUARTER, 128), BF16),
            pltpu.VMEM((QUARTER, 128), BF16),
        ],
        cost(pairs * 256 * 4, 3000000, pairs), "forward",
    )
    other_means = swap(means, ("yl",), 1)
    means = call(
        plane_kernel, shape((PLANE, 3 * GROUPS, 128), F32), (), (means, other_means), (),
        cost(0, 200000), "plane",
    )
    spare, means = barrier((spare, means))
    means = exchange(means, ZED)
    other_spare = swap(spare, ("yl",), 1)
    means, other_spare = barrier((means, other_spare))
    pooled_own, doc_means, logits, sums = call(
        pool_kernel,
        (
            shape((GROUPS, MODEL), F32),
            shape((GROUPS, WIDTH), F32),
            shape((GROUPS, HELD), F32),
            shape((DOCS, 8, 128), F32),
        ),
        (doc,), (means, w_out, queries, query_rows), (), cost(2 * 32 * 768 * 1024, 1800000), "pool",
    )
    sums = exchange(sums, GRP)
    ready = call(
        prepare_kernel, shape((24, 128), F32), (place,), (pooled_own, w_out), (),
        cost(2 * 32 * 128 * 1024, 1200000), "prepare",
    )
    sums, ready = barrier((sums, ready))
    terms = call(
        loss_kernel, shape((PLANE, 16, 128), F32), (doc,),
        (sums, logits, pooled_own, queries, query_rows, w_out), (),
        cost(2 * 32 * 768 * 1024, 1800000, 2000), "loss",
    )
    terms, own, keys = barrier((terms, own, keys))
    terms = exchange(terms, ZED)
    mass, lse_rows, columns = call(
        mass_kernel,
        (shape((GROUPS, 8, 128), F32), shape((8, KEYS), F32), shape((KEYS, 128), BF16)),
        (place, lengths), (own, keys, means),
        [pltpu.VMEM((QUARTER, 128), BF16), pltpu.VMEM((128, KEYS), BF16)],
        cost(pairs * 256 * 4, 2500000, pairs), "mass",
    )
    terms, mass, lse_rows = barrier((terms, mass, lse_rows))

    dattn, grad_part, loss, delta = call(
        group_kernel,
        (
            shape((GROUPS, 128), F32),
            shape((PLANE, GROUPS, 128), F32),
            shape((GROUPS, 128), F32),
            shape((2 * GROUPS, 128), F32),
        ),
        (place, lengths), (terms, ready, mass, spare, other_spare), (), cost(0, 100000), "group",
    )
    mean_loss = loss[0, 64]
    grad_parts = exchange(grad_part, ZED)
    other_delta = swap(delta, ("zd",), 1)
    grad_rows = call(
        row_kernel, shape((QUARTER, 128), BF16), (place, lengths), (own, keys, lse, delta, dattn),
        [
            pltpu.VMEM((KEYS, 128), BF16),
            pltpu.VMEM((QUARTER, 128), BF16),
            pltpu.VMEM((QUARTER, 128), BF16),
            pltpu.VMEM((QUARTER, 128), F32),
            pltpu.VMEM((QUARTER, 128), F32),
        ],
        cost(pairs * 256 * 6, 2000000, pairs), "rows",
    )
    grad_inputs, grads = call(
        inputs_kernel,
        (shape((ROWS, MODEL), BF16), shape((DOCS, 2 * GROUPS, (MODEL + WIDTH) // 2), BF16)),
        (place, lengths), (grad_parts, doc_means), (), cost(2 * 32 * 128 * 1024, 1200000), "inputs",
    )
    grad_rows, grads, other_delta = barrier((grad_rows, grads, other_delta))
    all_grads = exchange(grads, GRP)
    packed_grads = call(
        column_kernel, shape((PLANE, HALF, 128), BF16), (place, lengths),
        (own, columns, delta, other_delta, lse_rows, dattn, grad_rows),
        [
            pltpu.VMEM((KEYS, 128), BF16),
            pltpu.VMEM((QUARTER, 128), BF16),
            pltpu.VMEM((QUARTER, 128), BF16),
            pltpu.VMEM((8, KEYS), F32),
        ],
        cost(pairs * 256 * 6, 2500000, pairs), "columns",
    )
    packed_grads, grad_parts = barrier((packed_grads, grad_parts))
    home = exchange(packed_grads, ZED)
    out = shape((ROWS, WIDTH), BF16)
    grad_v = call(
        value_kernel, out, (lengths,), (grad_parts, w_out), (), cost(2 * 32 * 512 * 1024, 1300000),
        "values",
    )
    grad_w_out = call(
        weight_kernel, shape((WIDTH, MODEL), F32), (), (all_grads,), (),
        cost(2 * 384 * 512 * 1024, 3000000), "weights",
    )
    grad_q, grad_k = call(
        unpack_kernel, (out, out), (), (home,), (), cost(0, 500000), "unpack"
    )
    return (mean_loss, grad_inputs[None], grad_q[None], grad_k[None], grad_v[None], grad_w_out)


def solution(mesh):
    fine = Mesh(mesh.devices.reshape((2,) * 9), GRP + SEQ)
    rows = P(GRP, SEQ, None)
    return jax.shard_map(
        body,
        mesh=fine,
        in_specs=(
            rows,
            rows,
            rows,
            rows,
            P(),
            P(GRP, None),
            P(GRP + SEQ, None),
            P(GRP + SEQ),
        ),
        out_specs=(P(), rows, rows, rows, rows, P()),
        check_vma=False,
    )
```

```python
import functools

import jax
import jax.numpy as jnp
from jax import lax
from jax.experimental import pallas as pl
from jax.experimental.pallas import tpu as pltpu
from jax.sharding import Mesh, PartitionSpec as P

HEAD_COUNT = 8
HEAD_DIM = 64
GROUPS = 8
DOCS = 16
MODEL = 1024
WIDTH = 512
ROWS = 128
HALF = 64
QUARTER = 1024
PLANE = 16
SCALE = HEAD_DIM ** (-0.5)

RECIPROCAL_TEMP = 20.0
GRADIENT_FACTOR = 64.0
NORM_EPS = 1e-06
QUERY_COUNT = 8192
EXACT = lax.Precision.HIGHEST

BF16 = jnp.bfloat16
F32 = jnp.float32

GRP = ("yh", "xa", "xb", "co")
SEQ = ("yl", "za", "zb", "zc", "zd")
ZED = ("za", "zb", "zc", "zd")
SQUARE = ("yl", "zd")
HEADS = ("za", "zb", "zc")
NT = (((1,), (1,)), ((), ()))
TN = (((0,), (0,)), ((), ()))

HELD = 512


def params(mebibytes):
    return pltpu.CompilerParams(vmem_limit_bytes=mebibytes << 20)


def cost(flops, moved, exps=0):
    return pl.CostEstimate(flops=int(flops), bytes_accessed=int(moved), transcendentals=int(exps))


def share(value, axes):
    count = 2 ** len(axes)
    return lax.all_to_all(
        jnp.broadcast_to(value[None], (count,) + value.shape), axes, split_axis=0, concat_axis=0
    )


def swap(value, axes, flip):
    count = 2 ** len(axes)
    return lax.ppermute(value, axes, [(i, i ^ flip) for i in range(count)])


def gather(value, axes):
    for axis in axes:
        other = swap(value, (axis,), 1)
        first = lax.axis_index(axis) == 0
        value = jnp.where(
            first,
            jnp.concatenate([value, other], axis=0),
            jnp.concatenate([other, value], axis=0),
        )
    return value


def three(value):
    high = value.astype(BF16)
    rest = value - high.astype(F32)
    middle = rest.astype(BF16)
    low = (rest - middle.astype(F32)).astype(BF16)
    return high, middle, low


def stacked(value):
    parts = [part.astype(F32) for part in three(value)]
    parts.append(jnp.zeros_like(value))
    return jnp.concatenate(parts, axis=0).astype(BF16)


def folded(product):
    return (product[16:24] + product[8:16]) + product[0:8]


def column_of(values):
    row = lax.broadcasted_iota(jnp.int32, (GROUPS, 128), 0)
    out = jnp.full((GROUPS, 128), values[0])
    for n in range(1, GROUPS):
        out = jnp.where(row == n, values[n], out)
    return out


def member_of(position, lens_ref):
    ends = [lens_ref[0]]
    for n in range(1, GROUPS):
        ends.append(ends[-1] + lens_ref[n])
    last = column_of(ends)
    first = last - column_of([lens_ref[n] for n in range(GROUPS)])
    return ((position >= first[:, 0:1]) & (position < last[:, 0:1])).astype(F32)


def lengths_of(lens_ref):
    return column_of([lens_ref[n] for n in range(GROUPS)]).astype(F32)


def quarter_member(lens_ref, plane, half):
    row = lax.broadcasted_iota(jnp.int32, (GROUPS, QUARTER), 1)
    position = plane * (PLANE * ROWS) + (row >> 6) * ROWS + half * HALF + (row & 63)
    return member_of(position, lens_ref)


def local_member(lens_ref, first):
    return member_of(first + lax.broadcasted_iota(jnp.int32, (GROUPS, ROWS), 1), lens_ref)


def halves(packed):
    return jnp.concatenate([packed[:, :, 0:64], packed[:, :, 64:128]], axis=1)


def lanes(rows):
    return lax.broadcasted_iota(jnp.int32, (rows, 128), 1)


def pack_kernel(place_ref, lens_ref, q_ref, k_ref, v_ref, inputs_ref, out_ref):
    mine = local_member(lens_ref, place_ref[3]).astype(BF16)
    sums = jnp.dot(mine, inputs_ref[...], preferred_element_type=F32)
    high, middle, low = [part.astype(F32) for part in three(sums)]
    zero = jnp.zeros((GROUPS, HALF), F32)
    for head in range(HEAD_COUNT):
        cols = slice(head * HEAD_DIM, (head + 1) * HEAD_DIM)
        for half in range(2):
            rows = slice(half * HALF, (half + 1) * HALF)
            place = 2 * head + half
            out_ref[place, 0:64, :] = jnp.concatenate([k_ref[rows, cols], v_ref[rows, cols]], axis=1)
            query = q_ref[rows, cols] * jnp.asarray(SCALE, BF16)
            out_ref[place, 64:96, :] = jnp.concatenate([query[0:32], query[32:64]], axis=1)
            part = slice(place * HALF, (place + 1) * HALF)
            upper = jnp.concatenate([high[:, part], middle[:, part]], axis=1)
            lower = jnp.concatenate([low[:, part], zero], axis=1)
            out_ref[place, 96:112, :] = jnp.concatenate([upper, lower], axis=0).astype(BF16)


def unpack_kernel(in_ref, q_ref, k_ref):
    for pair in range(HEAD_COUNT // 2):
        cols = slice(pair * 128, (pair + 1) * 128)
        for half in range(2):
            rows = slice(half * HALF, (half + 1) * HALF)
            first, second = in_ref[4 * pair + half], in_ref[4 * pair + 2 + half]
            k_ref[rows, cols] = jnp.concatenate([first[:, 0:64], second[:, 0:64]], axis=1)
            q_ref[rows, cols] = jnp.concatenate([first[:, 64:128], second[:, 64:128]], axis=1)


BLOCK = 512
PARTS = BLOCK // 128


KEYS = 4 * QUARTER
SPARE = 512
CHUNK = 512
SHORT = 256
TALL = 1024


def fill(all_ref, x_ref):
    for n in range(4):
        x_ref[n * QUARTER : (n + 1) * QUARTER, :] = all_ref[n, :, 0:64, :].reshape(QUARTER, 128)


def own_queries(own_ref):
    queries = halves(own_ref[:, 64:96, :]).reshape(QUARTER, HEAD_DIM)
    return jnp.concatenate([queries, jnp.zeros_like(queries)], axis=1)


def turned(lines):
    columns = []
    for part in range(8):
        line = jnp.broadcast_to(lines[part : part + 1, :], (128, 128))
        columns.append(jnp.transpose(line))
    return jnp.concatenate(columns, axis=0)


def forward_kernel(
    place_ref, lens_ref, own_ref, all_ref, spare_ref, lse_ref, means_ref, x_ref, y_ref, q_s
):
    fill(all_ref, x_ref)
    q_s[...] = own_queries(own_ref)

    def block(i, carry):
        rows = pl.ds(pl.multiple_of(i * SHORT, SHORT), SHORT)
        scores = lax.dot_general(q_s[rows, :], x_ref[...], NT, preferred_element_type=F32)
        top = jnp.max(scores, axis=1, keepdims=True)
        grown = jnp.exp(scores - top)
        total = jnp.sum(grown, axis=1, keepdims=True)
        mixed = jnp.dot(grown.astype(BF16), x_ref[...], preferred_element_type=F32)
        y_ref[rows, :] = (mixed * (1.0 / total)).astype(BF16)
        log_total = top + jnp.log(total)
        for part in range(SHORT // 128):
            square = jnp.broadcast_to(log_total[part * 128 : (part + 1) * 128], (128, 128))
            lse_ref[pl.ds(i * (SHORT // 128) + part, 1), :] = jnp.transpose(square)[0:1, :]
        return carry

    lax.fori_loop(0, QUARTER // SHORT, block, 0)
    spare_ref[...] = jnp.concatenate(
        [y_ref[0:512, :][:, 64:128], y_ref[512:1024, :][:, 64:128]], axis=1
    )
    member = quarter_member(lens_ref, place_ref[0], place_ref[1]).astype(BF16)
    attn_sums = jnp.dot(member, y_ref[0:QUARTER, :], preferred_element_type=F32)
    sums = jnp.sum(own_ref[:, 96:112, :].astype(F32), axis=0)
    input_sums = (sums[0:8] + pltpu.roll(sums[0:8], 64, 1)) + sums[8:16]
    means = jnp.where(lanes(GROUPS) < 64, input_sums, attn_sums) / lengths_of(lens_ref)
    means_ref[...] = jnp.concatenate([means, lse_ref[...]], axis=0)


def plane_kernel(mine_ref, other_ref, out_ref):
    mine, other = mine_ref[...], other_ref[...]
    both = jnp.concatenate([mine[0:8] + other[0:8], mine[8:16], other[8:16]], axis=0)
    out_ref[...] = jnp.broadcast_to(both[None], (PLANE, 3 * GROUPS, 128))


def pool_kernel(doc_ref, means_ref, w_ref, query_ref, row_ref, own_ref, means_out_ref, logits_ref, out_ref):
    columns = [means_ref[z, 0:8, 0:64] for z in range(PLANE)]
    heads = [
        means_ref[z, 0:8, 64:128] + means_ref[z + 1, 0:8, 64:128] for z in range(0, PLANE, 2)
    ]
    means = jnp.concatenate(heads, axis=1)
    projected = jnp.dot(stacked(means), w_ref[...], preferred_element_type=F32)
    pooled = jnp.concatenate(columns, axis=1) + folded(projected)
    own_ref[...] = pooled
    means_out_ref[...] = means
    unit = pooled / jnp.sqrt(jnp.sum(pooled * pooled, axis=1, keepdims=True) + NORM_EPS)
    logits = folded(
        lax.dot_general(stacked(unit), query_ref[:, :MODEL], NT, preferred_element_type=F32)
    )
    logits = logits * (RECIPROCAL_TEMP / row_ref[0:1, :])
    logits_ref[...] = logits
    group = doc_ref[0] * GROUPS + lax.broadcasted_iota(jnp.int32, logits.shape, 0)
    target = (group == row_ref[8:9, :].astype(jnp.int32)).astype(F32)
    total = jnp.sum(jnp.exp(logits), axis=0, keepdims=True)
    chosen = jnp.sum(target * logits, axis=0, keepdims=True)
    sums = jnp.concatenate(
        [row[:, n : n + 128] for row in (total, chosen) for n in range(0, HELD, 128)], axis=0
    )
    out_ref[...] = jnp.broadcast_to(sums[None], (DOCS, 8, 128))


def prepare_kernel(place_ref, pooled_ref, w_ref, out_ref):
    head = place_ref[2]
    pooled = pooled_ref[...]
    norms = jnp.sqrt(jnp.sum(pooled * pooled, axis=1, keepdims=True) + NORM_EPS)
    unit = pooled / norms
    w_head = w_ref[pl.ds(pl.multiple_of(head * HEAD_DIM, HEAD_DIM), HEAD_DIM), :]
    w_twice = jnp.concatenate([w_head, w_head], axis=0)
    out_ref[0:8, :] = folded(
        lax.dot_general(stacked(unit), w_twice, NT, preferred_element_type=F32)
    )
    z = 2 * head + place_ref[1]
    part = unit[:, 0:64]
    for n in range(1, PLANE):
        part = jnp.where(z == n, unit[:, n * HALF : (n + 1) * HALF], part)
    out_ref[8:16, :] = jnp.concatenate([part, part], axis=1)
    out_ref[16:24, :] = jnp.broadcast_to(norms, (GROUPS, 128))


def query_kernel(query_ref, out_ref):
    query = query_ref[:, :MODEL].astype(F32)
    squares = lax.dot_general(
        jnp.ones((8, MODEL), F32), query * query, NT, precision=EXACT, preferred_element_type=F32
    )
    out_ref[0:8, :] = jnp.sqrt(squares + NORM_EPS)
    out_ref[8:16, :] = lax.dot_general(
        jnp.ones((8, 128), BF16), query_ref[:, MODEL:], NT, preferred_element_type=F32
    )


def loss_kernel(doc_ref, sums_ref, logits_ref, own_ref, query_ref, row_ref, w_ref, out_ref):
    sums = sums_ref[0]
    for n in range(1, DOCS):
        sums = sums + sums_ref[n]
    total = jnp.concatenate([sums[n : n + 1] for n in range(4)], axis=1)
    losses = jnp.log(sums[0:4]) - sums[4:8]
    loss = jnp.sum(jnp.sum(losses, axis=1, keepdims=True), axis=0, keepdims=True)
    query = query_ref[:, :MODEL]
    scale = RECIPROCAL_TEMP / row_ref[0:1, :]
    logits = logits_ref[...]
    group = doc_ref[0] * GROUPS + lax.broadcasted_iota(jnp.int32, logits.shape, 0)
    target = (group == row_ref[8:9, :].astype(jnp.int32)).astype(F32)
    weight = (jnp.exp(logits) / total - target) * (GRADIENT_FACTOR * scale)
    grad = folded(jnp.dot(stacked(weight), query, preferred_element_type=F32))
    own = own_ref[...]
    own_unit = own / jnp.sqrt(jnp.sum(own * own, axis=1, keepdims=True) + NORM_EPS)
    along = jnp.sum(own_unit * grad, axis=1, keepdims=True)
    spread = folded(
        lax.dot_general(stacked(grad), w_ref[...], NT, preferred_element_type=F32)
    )
    extra = jnp.where(lanes(GROUPS) < 64, along, loss)
    for z in range(PLANE):
        head = z // 2
        chunk = jnp.concatenate(
            [
                spread[:, head * HEAD_DIM : (head + 1) * HEAD_DIM],
                grad[:, z * HALF : (z + 1) * HALF],
            ],
            axis=1,
        )
        out_ref[z, 0:8, :] = chunk
        out_ref[z, 8:16, :] = extra


def mass_kernel(
    place_ref, lens_ref, own_ref, all_ref, means_ref, mass_ref, lse_ref, y_ref, k_s, member_s
):
    mine = own_ref[:, 0:64, :].reshape(QUARTER, 128)
    k_s[...] = jnp.where(lanes(QUARTER) < 64, mine, jnp.zeros_like(mine))
    for n in range(4):
        queries = halves(all_ref[n, :, 64:96, :]).reshape(QUARTER, HEAD_DIM)
        y_ref[n * QUARTER : (n + 1) * QUARTER, :] = jnp.concatenate(
            [queries, jnp.zeros_like(queries)], axis=1
        )
        both = means_ref[2 * place_ref[2] + n % 2]
        lse = jnp.where(place_ref[0] == n // 2, both[8:16], both[16:24])
        for part in range(8):
            at = n * QUARTER + part * 128
            lse_ref[:, at : at + 128] = jnp.broadcast_to(lse[part : part + 1, :], (8, 128))
        member = quarter_member(lens_ref, n // 2, n % 2)
        padded = jnp.concatenate([member, jnp.zeros((120, QUARTER), F32)], axis=0)
        member_s[:, n * QUARTER : (n + 1) * QUARTER] = padded.astype(BF16)

    def block(i, carry):
        rows = pl.ds(pl.multiple_of(i * BLOCK, BLOCK), BLOCK)
        sums = jnp.zeros((BLOCK, 128), F32)
        for n in range(4):
            cols = slice(n * QUARTER, (n + 1) * QUARTER)
            scores = lax.dot_general(k_s[rows, :], y_ref[cols, :], NT, preferred_element_type=F32)
            prob = jnp.exp(scores - lse_ref[0:1, cols]).astype(BF16)
            sums = sums + lax.dot_general(
                prob, member_s[:, cols], NT, preferred_element_type=F32
            )
        for part in range(PARTS):
            mass_ref[i * PARTS + part] = jnp.transpose(sums[part * 128 : (part + 1) * 128])[0:8, :]
        return carry

    lax.fori_loop(0, QUARTER // BLOCK, block, 0)


def rows_of(line):
    return jnp.concatenate([line[:, n : n + 128] for n in range(0, QUARTER, 128)], axis=0)


def group_kernel(
    place_ref, lens_ref, terms_ref, ready_ref, mass_ref, spare_ref, other_ref,
    dattn_ref, grad_ref, loss_ref, delta_ref,
):
    sums = terms_ref[0]
    for n in range(1, PLANE):
        sums = sums + terms_ref[n]
    along = sums[8:16, 0:1]
    loss_ref[...] = sums[8:16, :] / QUERY_COUNT
    norms = ready_ref[16:24, :]
    raw = jnp.concatenate([sums[0:8, 0:64], sums[0:8, 0:64]], axis=1)
    dattn = (raw - ready_ref[0:8, :] * along) / norms / lengths_of(lens_ref)
    dattn_ref[...] = dattn
    lane = lanes(GROUPS)
    ends = [
        jnp.where(lane < 64, dattn, 0.0).astype(BF16),
        jnp.where(lane < 64, 0.0, dattn).astype(BF16),
    ]
    for n, (attn, plane) in enumerate(
        ((spare_ref, place_ref[0]), (other_ref, 1 - place_ref[0]))
    ):
        products = jnp.concatenate(
            [lax.dot_general(part, attn[...], NT, preferred_element_type=F32) for part in ends],
            axis=1,
        )
        member = quarter_member(lens_ref, plane, place_ref[1])
        delta_ref[n * 8 : (n + 1) * 8, :] = rows_of(
            jnp.sum(products * member, axis=0, keepdims=True)
        )
    grad = (sums[0:8, 64:128] - ready_ref[8:16, 0:64] * along) / norms[:, 0:64]
    for z in range(PLANE):
        half = (z % 2) * HALF
        grad_ref[z] = jnp.concatenate([grad, mass_ref[z // 2, :, half : half + HALF]], axis=1)


def inputs_kernel(place_ref, lens_ref, parts_ref, means_ref, grad_inputs_ref, out_ref):
    grad = jnp.concatenate([parts_ref[z, :, 0:64] for z in range(PLANE)], axis=1)
    mine = local_member(lens_ref, place_ref[3])
    members = jnp.concatenate([mine, mine, mine, mine], axis=0).astype(BF16)
    grad_inputs_ref[...] = lax.dot_general(
        members, stacked(grad / lengths_of(lens_ref)[:, 0:1]), TN, preferred_element_type=F32
    ).astype(BF16)
    both = jnp.concatenate([grad, means_ref[...]], axis=1)
    wide = (MODEL + WIDTH) // 2
    both = jnp.concatenate([both[:, :wide], both[:, wide:]], axis=0)
    out_ref[...] = jnp.broadcast_to(both.astype(BF16)[None], (DOCS, 2 * GROUPS, wide))


def value_kernel(lens_ref, parts_ref, w_ref, grad_v_ref):
    grad = jnp.concatenate([parts_ref[z, :, 0:64] for z in range(PLANE)], axis=1)
    grad = grad / lengths_of(lens_ref)[:, 0:1]
    dattn = folded(lax.dot_general(stacked(grad), w_ref[...], NT, preferred_element_type=F32))
    dattn = dattn.astype(BF16).astype(F32)
    dattn = jnp.concatenate([dattn, dattn, dattn, jnp.zeros_like(dattn)], axis=0).astype(BF16)
    for pair in range(HEAD_COUNT // 2):
        cols = slice(pair * 128, (pair + 1) * 128)
        both = []
        for head in (2 * pair, 2 * pair + 1):
            mass = jnp.concatenate(
                [parts_ref[2 * head, :, 64:128], parts_ref[2 * head + 1, :, 64:128]], axis=1
            )
            both.append(
                lax.dot_general(stacked(mass), dattn[:, cols], TN, preferred_element_type=F32)
            )
        grad_v_ref[:, cols] = jnp.where(lanes(ROWS) < 64, both[0], both[1]).astype(BF16)


def weight_kernel(in_ref, out_ref):
    wide = (MODEL + WIDTH) // 2
    both = in_ref[...].astype(F32)
    both = [both[:, n : n + 8].reshape(DOCS * GROUPS, wide) for n in (0, 8)]
    both = jnp.concatenate(both, axis=1).astype(BF16)
    out_ref[...] = lax.dot_general(
        both[:, MODEL:], both[:, :MODEL], TN, preferred_element_type=F32
    )


def row_kernel(
    place_ref, lens_ref, own_ref, all_ref, lse_ref, delta_ref, dattn_ref,
    out_ref, x_ref, q_s, d_s, delta_s, lse_s,
):
    fill(all_ref, x_ref)
    q_s[...] = own_queries(own_ref)
    member = quarter_member(lens_ref, place_ref[0], place_ref[1]).astype(BF16)
    spread = lax.dot_general(
        member, dattn_ref[...].astype(BF16), TN, preferred_element_type=F32
    )
    d_s[...] = jnp.where(lanes(QUARTER) < 64, 0.0, spread).astype(BF16)
    delta_s[...] = turned(delta_ref[0:8, :])
    lse_s[...] = turned(lse_ref[...])

    def block(i, carry):
        rows = pl.ds(pl.multiple_of(i * TALL, TALL), TALL)
        log_total, delta = lse_s[rows, 0:1], delta_s[rows, 0:1]
        total = jnp.zeros((TALL, 128), F32)
        for n in range(KEYS // CHUNK):
            part = x_ref[n * CHUNK : (n + 1) * CHUNK, :]
            scores = lax.dot_general(q_s[rows, :], part, NT, preferred_element_type=F32)
            prob_grad = lax.dot_general(d_s[rows, :], part, NT, preferred_element_type=F32)
            score_grad = (jnp.exp(scores - log_total) * (prob_grad - delta)).astype(BF16)
            total = total + jnp.dot(score_grad, part, preferred_element_type=F32)
        total = total * SCALE
        out_ref[rows, :] = jnp.concatenate([total[:, 0:64]] * 2, axis=1).astype(BF16)
        return carry

    lax.fori_loop(0, QUARTER // TALL, block, 0)


def column_kernel(
    place_ref, lens_ref, own_ref, y_ref, mine_ref, other_ref, lse_ref, dattn_ref, grad_q_ref,
    out_ref, y_s, k_s, v_s, delta_s,
):
    lane = lanes(QUARTER)
    mine = own_ref[:, 0:64, :].reshape(QUARTER, 128)
    zero = jnp.zeros_like(mine)
    k_s[...] = jnp.where(lane < 64, mine, zero)
    v_s[...] = jnp.where(lane < 64, zero, mine)
    dattn = jnp.where(lanes(GROUPS) < 64, 0.0, dattn_ref[...]).astype(BF16)
    for n in range(4):
        rows = slice(n * QUARTER, (n + 1) * QUARTER)
        member = quarter_member(lens_ref, n // 2, n % 2)
        spread = lax.dot_general(member.astype(BF16), dattn, TN, preferred_element_type=F32)
        y_s[rows, :] = jnp.where(lane < 64, y_ref[rows, :], spread.astype(BF16))
        delta = jnp.where(place_ref[1] == n % 2, mine_ref[...], other_ref[...])
        delta = jnp.where(place_ref[0] == n // 2, delta[0:8], delta[8:16])
        for part in range(8):
            at = n * QUARTER + part * 128
            delta_s[:, at : at + 128] = jnp.broadcast_to(delta[part : part + 1, :], (8, 128))

    def block(i, carry):
        rows = pl.ds(pl.multiple_of(i * TALL, TALL), TALL)
        total = jnp.zeros((TALL, 128), F32)
        for n in range(KEYS // CHUNK):
            cols = slice(n * CHUNK, (n + 1) * CHUNK)
            part = y_s[cols, :]
            scores = lax.dot_general(k_s[rows, :], part, NT, preferred_element_type=F32)
            prob_grad = lax.dot_general(v_s[rows, :], part, NT, preferred_element_type=F32)
            score_grad = (
                jnp.exp(scores - lse_ref[0:1, cols]) * (prob_grad - delta_s[0:1, cols])
            ).astype(BF16)
            total = total + jnp.dot(score_grad, part, preferred_element_type=F32)
        both = jnp.where(lanes(TALL) < 64, total.astype(BF16), grad_q_ref[rows, :])
        count = TALL // HALF
        out_ref[pl.ds(i * count, count), :, :] = both.reshape(count, HALF, 128)
        return carry

    lax.fori_loop(0, QUARTER // TALL, block, 0)


SMEM = pl.BlockSpec(memory_space=pltpu.SMEM)
VMEM = pl.BlockSpec(memory_space=pltpu.VMEM)


def call(kernel, outs, scalars, arrays, scratch, estimate, name):
    return pl.pallas_call(
        kernel,
        out_shape=outs,
        in_specs=[SMEM] * len(scalars) + [VMEM] * len(arrays),
        out_specs=jax.tree.map(lambda _: VMEM, outs),
        scratch_shapes=scratch,
        compiler_params=params(56 if name == "pack" else 40 if scratch else 12),
        cost_estimate=estimate,
        name=name,
    )(*scalars, *arrays)


def shape(dims, dtype):
    return jax.ShapeDtypeStruct(dims, dtype)


def body(inputs, q_heads, k_heads, v_heads, w_out, group_lens, query_emb, positive):
    plane = lax.axis_index("yl")
    half = lax.axis_index("zd")
    head = lax.axis_index(HEADS)
    first = lax.axis_index(SEQ) * ROWS
    doc = lax.axis_index(GRP).reshape(1).astype(jnp.int32)
    place = jnp.stack([plane, half, head, first]).astype(jnp.int32)
    lengths = group_lens[0]
    exchange = functools.partial(lax.all_to_all, split_axis=0, concat_axis=0)
    barrier = lax.optimization_barrier
    pairs = QUARTER * KEYS

    packed = call(
        pack_kernel, shape((PLANE, 112, 128), BF16), (place, lengths),
        (q_heads[0], k_heads[0], v_heads[0], inputs[0]), (), cost(0, 1000000), "pack",
    )
    packed, query_emb, positive = barrier((packed, query_emb, positive))
    tagged = jnp.concatenate(
        [query_emb, jnp.pad(positive.astype(BF16)[:, None], ((0, 0), (0, 127)))], axis=1
    )
    own = exchange(packed, ZED)
    queries = gather(tagged, ("yh", "yl", "xa"))
    own, queries = barrier((own, queries))
    keys = share(own[:, 0:96, :], SQUARE)
    queries = gather(queries, ("xb", "co"))
    query_rows = call(
        query_kernel, shape((16, HELD), F32), (), (queries,), (), cost(6 * 2 * 8 * HELD * 1024, 1200000),
        "queries",
    )
    own, keys, queries, query_rows = barrier((own, keys, queries, query_rows))

    spare, lse, means = call(
        forward_kernel,
        (
            shape((SPARE, 128), BF16),
            shape((8, 128), F32),
            shape((2 * GROUPS, 128), F32),
        ),
        (place, lengths), (own, keys),
        [
            pltpu.VMEM((KEYS, 128), BF16),
            pltpu.VMEM((QUARTER, 128), BF16),
            pltpu.VMEM((QUARTER, 128), BF16),
        ],
        cost(pairs * 256 * 4, 3000000, pairs), "forward",
    )
    other_means = swap(means, ("yl",), 1)
    means = call(
        plane_kernel, shape((PLANE, 3 * GROUPS, 128), F32), (), (means, other_means), (),
        cost(0, 200000), "plane",
    )
    spare, means = barrier((spare, means))
    means = exchange(means, ZED)
    other_spare = swap(spare, ("yl",), 1)
    means, other_spare = barrier((means, other_spare))
    pooled_own, doc_means, logits, sums = call(
        pool_kernel,
        (
            shape((GROUPS, MODEL), F32),
            shape((GROUPS, WIDTH), F32),
            shape((GROUPS, HELD), F32),
            shape((DOCS, 8, 128), F32),
        ),
        (doc,), (means, w_out, queries, query_rows), (), cost(2 * 32 * 768 * 1024, 1800000), "pool",
    )
    sums = exchange(sums, GRP)
    ready = call(
        prepare_kernel, shape((24, 128), F32), (place,), (pooled_own, w_out), (),
        cost(2 * 32 * 128 * 1024, 1200000), "prepare",
    )
    sums, ready = barrier((sums, ready))
    terms = call(
        loss_kernel, shape((PLANE, 16, 128), F32), (doc,),
        (sums, logits, pooled_own, queries, query_rows, w_out), (),
        cost(2 * 32 * 768 * 1024, 1800000, 2000), "loss",
    )
    terms, own, keys = barrier((terms, own, keys))
    terms = exchange(terms, ZED)
    mass, lse_rows, columns = call(
        mass_kernel,
        (shape((GROUPS, 8, 128), F32), shape((8, KEYS), F32), shape((KEYS, 128), BF16)),
        (place, lengths), (own, keys, means),
        [pltpu.VMEM((QUARTER, 128), BF16), pltpu.VMEM((128, KEYS), BF16)],
        cost(pairs * 256 * 4, 2500000, pairs), "mass",
    )
    terms, mass, lse_rows = barrier((terms, mass, lse_rows))

    dattn, grad_part, loss, delta = call(
        group_kernel,
        (
            shape((GROUPS, 128), F32),
            shape((PLANE, GROUPS, 128), F32),
            shape((GROUPS, 128), F32),
            shape((2 * GROUPS, 128), F32),
        ),
        (place, lengths), (terms, ready, mass, spare, other_spare), (), cost(0, 100000), "group",
    )
    mean_loss = loss[0, 64]
    grad_parts = exchange(grad_part, ZED)
    other_delta = swap(delta, ("zd",), 1)
    grad_rows = call(
        row_kernel, shape((QUARTER, 128), BF16), (place, lengths), (own, keys, lse, delta, dattn),
        [
            pltpu.VMEM((KEYS, 128), BF16),
            pltpu.VMEM((QUARTER, 128), BF16),
            pltpu.VMEM((QUARTER, 128), BF16),
            pltpu.VMEM((QUARTER, 128), F32),
            pltpu.VMEM((QUARTER, 128), F32),
        ],
        cost(pairs * 256 * 6, 2000000, pairs), "rows",
    )
    grad_inputs, grads = call(
        inputs_kernel,
        (shape((ROWS, MODEL), BF16), shape((DOCS, 2 * GROUPS, (MODEL + WIDTH) // 2), BF16)),
        (place, lengths), (grad_parts, doc_means), (), cost(2 * 32 * 128 * 1024, 1200000), "inputs",
    )
    grad_rows, grads, other_delta = barrier((grad_rows, grads, other_delta))
    all_grads = exchange(grads, GRP)
    packed_grads = call(
        column_kernel, shape((PLANE, HALF, 128), BF16), (place, lengths),
        (own, columns, delta, other_delta, lse_rows, dattn, grad_rows),
        [
            pltpu.VMEM((KEYS, 128), BF16),
            pltpu.VMEM((QUARTER, 128), BF16),
            pltpu.VMEM((QUARTER, 128), BF16),
            pltpu.VMEM((8, KEYS), F32),
        ],
        cost(pairs * 256 * 6, 2500000, pairs), "columns",
    )
    packed_grads, grad_parts = barrier((packed_grads, grad_parts))
    home = exchange(packed_grads, ZED)
    out = shape((ROWS, WIDTH), BF16)
    grad_v = call(
        value_kernel, out, (lengths,), (grad_parts, w_out), (), cost(2 * 32 * 512 * 1024, 1300000),
        "values",
    )
    grad_w_out = call(
        weight_kernel, shape((WIDTH, MODEL), F32), (), (all_grads,), (),
        cost(2 * 384 * 512 * 1024, 3000000), "weights",
    )
    grad_q, grad_k = call(
        unpack_kernel, (out, out), (), (home,), (), cost(0, 500000), "unpack"
    )
    return (mean_loss, grad_inputs[None], grad_q[None], grad_k[None], grad_v[None], grad_w_out)


def solution(mesh):
    fine = Mesh(mesh.devices.reshape((2,) * 9), GRP + SEQ)
    rows = P(GRP, SEQ, None)
    return jax.shard_map(
        body,
        mesh=fine,
        in_specs=(
            rows,
            rows,
            rows,
            rows,
            P(),
            P(GRP, None),
            P(GRP + SEQ, None),
            P(GRP + SEQ),
        ),
        out_specs=(P(), rows, rows, rows, rows, P()),
        check_vma=False,
    )
```

```python
import functools

import jax
import jax.numpy as jnp
from jax import lax
from jax.experimental import pallas as pl
from jax.experimental.pallas import tpu as pltpu
from jax.sharding import Mesh, PartitionSpec as P

HEAD_COUNT = 8
HEAD_DIM = 64
GROUPS = 8
DOCS = 16
MODEL = 1024
WIDTH = 512
ROWS = 128
HALF = 64
QUARTER = 1024
PLANE = 16
SCALE = HEAD_DIM ** (-0.5)

RECIPROCAL_TEMP = 20.0
GRADIENT_FACTOR = 64.0
NORM_EPS = 1e-06
QUERY_COUNT = 8192
EXACT = lax.Precision.HIGHEST

BF16 = jnp.bfloat16
F32 = jnp.float32

GRP = ("yh", "xa", "xb", "co")
SEQ = ("yl", "za", "zb", "zc", "zd")
ZED = ("za", "zb", "zc", "zd")
SQUARE = ("yl", "zd")
HEADS = ("za", "zb", "zc")
NT = (((1,), (1,)), ((), ()))
TN = (((0,), (0,)), ((), ()))

HELD = 512


def params(mebibytes):
    return pltpu.CompilerParams(vmem_limit_bytes=mebibytes << 20)


def cost(flops, moved, exps=0):
    return pl.CostEstimate(flops=int(flops), bytes_accessed=int(moved), transcendentals=int(exps))


def share(value, axes):
    count = 2 ** len(axes)
    return lax.all_to_all(
        jnp.broadcast_to(value[None], (count,) + value.shape), axes, split_axis=0, concat_axis=0
    )


def swap(value, axes, flip):
    count = 2 ** len(axes)
    return lax.ppermute(value, axes, [(i, i ^ flip) for i in range(count)])


def gather(value, axes):
    for axis in axes:
        other = swap(value, (axis,), 1)
        first = lax.axis_index(axis) == 0
        value = jnp.where(
            first,
            jnp.concatenate([value, other], axis=0),
            jnp.concatenate([other, value], axis=0),
        )
    return value


def three(value):
    high = value.astype(BF16)
    rest = value - high.astype(F32)
    middle = rest.astype(BF16)
    low = (rest - middle.astype(F32)).astype(BF16)
    return high, middle, low


def stacked(value):
    parts = [part.astype(F32) for part in three(value)]
    parts.append(jnp.zeros_like(value))
    return jnp.concatenate(parts, axis=0).astype(BF16)


def folded(product):
    return (product[16:24] + product[8:16]) + product[0:8]


def column_of(values):
    row = lax.broadcasted_iota(jnp.int32, (GROUPS, 128), 0)
    out = jnp.full((GROUPS, 128), values[0])
    for n in range(1, GROUPS):
        out = jnp.where(row == n, values[n], out)
    return out


def member_of(position, lens_ref):
    ends = [lens_ref[0]]
    for n in range(1, GROUPS):
        ends.append(ends[-1] + lens_ref[n])
    last = column_of(ends)
    first = last - column_of([lens_ref[n] for n in range(GROUPS)])
    return ((position >= first[:, 0:1]) & (position < last[:, 0:1])).astype(F32)


def lengths_of(lens_ref):
    return column_of([lens_ref[n] for n in range(GROUPS)]).astype(F32)


def quarter_member(lens_ref, plane, half):
    row = lax.broadcasted_iota(jnp.int32, (GROUPS, QUARTER), 1)
    position = plane * (PLANE * ROWS) + (row >> 6) * ROWS + half * HALF + (row & 63)
    return member_of(position, lens_ref)


def local_member(lens_ref, first):
    return member_of(first + lax.broadcasted_iota(jnp.int32, (GROUPS, ROWS), 1), lens_ref)


def halves(packed):
    return jnp.concatenate([packed[:, :, 0:64], packed[:, :, 64:128]], axis=1)


def lanes(rows):
    return lax.broadcasted_iota(jnp.int32, (rows, 128), 1)


def pack_kernel(place_ref, lens_ref, q_ref, k_ref, v_ref, inputs_ref, out_ref):
    mine = local_member(lens_ref, place_ref[3]).astype(BF16)
    sums = jnp.dot(mine, inputs_ref[...], preferred_element_type=F32)
    high, middle, low = [part.astype(F32) for part in three(sums)]
    zero = jnp.zeros((GROUPS, HALF), F32)
    for head in range(HEAD_COUNT):
        cols = slice(head * HEAD_DIM, (head + 1) * HEAD_DIM)
        for half in range(2):
            rows = slice(half * HALF, (half + 1) * HALF)
            place = 2 * head + half
            out_ref[place, 0:64, :] = jnp.concatenate([k_ref[rows, cols], v_ref[rows, cols]], axis=1)
            query = q_ref[rows, cols] * jnp.asarray(SCALE, BF16)
            out_ref[place, 64:96, :] = jnp.concatenate([query[0:32], query[32:64]], axis=1)
            part = slice(place * HALF, (place + 1) * HALF)
            upper = jnp.concatenate([high[:, part], middle[:, part]], axis=1)
            lower = jnp.concatenate([low[:, part], zero], axis=1)
            out_ref[place, 96:112, :] = jnp.concatenate([upper, lower], axis=0).astype(BF16)


def unpack_kernel(in_ref, q_ref, k_ref):
    for pair in range(HEAD_COUNT // 2):
        cols = slice(pair * 128, (pair + 1) * 128)
        for half in range(2):
            rows = slice(half * HALF, (half + 1) * HALF)
            first, second = in_ref[4 * pair + half], in_ref[4 * pair + 2 + half]
            k_ref[rows, cols] = jnp.concatenate([first[:, 0:64], second[:, 0:64]], axis=1)
            q_ref[rows, cols] = jnp.concatenate([first[:, 64:128], second[:, 64:128]], axis=1)


BLOCK = 512
PARTS = BLOCK // 128


KEYS = 4 * QUARTER
SPARE = 512
CHUNK = 512
SHORT = 256
TALL = 1024


def fill(all_ref, x_ref):
    for n in range(4):
        x_ref[n * QUARTER : (n + 1) * QUARTER, :] = all_ref[n, :, 0:64, :].reshape(QUARTER, 128)


def own_queries(own_ref):
    queries = halves(own_ref[:, 64:96, :]).reshape(QUARTER, HEAD_DIM)
    return jnp.concatenate([queries, jnp.zeros_like(queries)], axis=1)


def turned(lines):
    columns = []
    for part in range(8):
        line = jnp.broadcast_to(lines[part : part + 1, :], (128, 128))
        columns.append(jnp.transpose(line))
    return jnp.concatenate(columns, axis=0)


def forward_kernel(
    place_ref, lens_ref, own_ref, all_ref, spare_ref, lse_ref, means_ref, x_ref, y_ref, q_s
):
    fill(all_ref, x_ref)
    q_s[...] = own_queries(own_ref)

    def block(i, carry):
        rows = pl.ds(pl.multiple_of(i * SHORT, SHORT), SHORT)
        scores = lax.dot_general(q_s[rows, :], x_ref[...], NT, preferred_element_type=F32)
        top = jnp.max(scores, axis=1, keepdims=True)
        grown = jnp.exp(scores - top)
        total = jnp.sum(grown, axis=1, keepdims=True)
        mixed = jnp.dot(grown.astype(BF16), x_ref[...], preferred_element_type=F32)
        y_ref[rows, :] = (mixed * (1.0 / total)).astype(BF16)
        log_total = top + jnp.log(total)
        for part in range(SHORT // 128):
            square = jnp.broadcast_to(log_total[part * 128 : (part + 1) * 128], (128, 128))
            lse_ref[pl.ds(i * (SHORT // 128) + part, 1), :] = jnp.transpose(square)[0:1, :]
        return carry

    lax.fori_loop(0, QUARTER // SHORT, block, 0)
    spare_ref[...] = jnp.concatenate(
        [y_ref[0:512, :][:, 64:128], y_ref[512:1024, :][:, 64:128]], axis=1
    )
    member = quarter_member(lens_ref, place_ref[0], place_ref[1]).astype(BF16)
    attn_sums = jnp.dot(member, y_ref[0:QUARTER, :], preferred_element_type=F32)
    sums = jnp.sum(own_ref[:, 96:112, :].astype(F32), axis=0)
    input_sums = (sums[0:8] + pltpu.roll(sums[0:8], 64, 1)) + sums[8:16]
    means = jnp.where(lanes(GROUPS) < 64, input_sums, attn_sums) / lengths_of(lens_ref)
    means_ref[...] = jnp.concatenate([means, lse_ref[...]], axis=0)


def plane_kernel(mine_ref, other_ref, out_ref):
    mine, other = mine_ref[...], other_ref[...]
    both = jnp.concatenate([mine[0:8] + other[0:8], mine[8:16], other[8:16]], axis=0)
    out_ref[...] = jnp.broadcast_to(both[None], (PLANE, 3 * GROUPS, 128))


def pool_kernel(doc_ref, means_ref, w_ref, query_ref, row_ref, own_ref, means_out_ref, logits_ref, out_ref):
    columns = [means_ref[z, 0:8, 0:64] for z in range(PLANE)]
    heads = [
        means_ref[z, 0:8, 64:128] + means_ref[z + 1, 0:8, 64:128] for z in range(0, PLANE, 2)
    ]
    means = jnp.concatenate(heads, axis=1)
    projected = jnp.dot(stacked(means), w_ref[...], preferred_element_type=F32)
    pooled = jnp.concatenate(columns, axis=1) + folded(projected)
    own_ref[...] = pooled
    means_out_ref[...] = means
    unit = pooled / jnp.sqrt(jnp.sum(pooled * pooled, axis=1, keepdims=True) + NORM_EPS)
    logits = folded(
        lax.dot_general(stacked(unit), query_ref[:, :MODEL], NT, preferred_element_type=F32)
    )
    logits = logits * (RECIPROCAL_TEMP / row_ref[0:1, :])
    logits_ref[...] = logits
    group = doc_ref[0] * GROUPS + lax.broadcasted_iota(jnp.int32, logits.shape, 0)
    target = (group == row_ref[8:9, :].astype(jnp.int32)).astype(F32)
    total = jnp.sum(jnp.exp(logits), axis=0, keepdims=True)
    chosen = jnp.sum(target * logits, axis=0, keepdims=True)
    sums = jnp.concatenate(
        [row[:, n : n + 128] for row in (total, chosen) for n in range(0, HELD, 128)], axis=0
    )
    out_ref[...] = jnp.broadcast_to(sums[None], (DOCS, 8, 128))


def prepare_kernel(place_ref, pooled_ref, w_ref, out_ref):
    head = place_ref[2]
    pooled = pooled_ref[...]
    norms = jnp.sqrt(jnp.sum(pooled * pooled, axis=1, keepdims=True) + NORM_EPS)
    unit = pooled / norms
    w_head = w_ref[pl.ds(pl.multiple_of(head * HEAD_DIM, HEAD_DIM), HEAD_DIM), :]
    w_twice = jnp.concatenate([w_head, w_head], axis=0)
    out_ref[0:8, :] = folded(
        lax.dot_general(stacked(unit), w_twice, NT, preferred_element_type=F32)
    )
    z = 2 * head + place_ref[1]
    part = unit[:, 0:64]
    for n in range(1, PLANE):
        part = jnp.where(z == n, unit[:, n * HALF : (n + 1) * HALF], part)
    out_ref[8:16, :] = jnp.concatenate([part, part], axis=1)
    out_ref[16:24, :] = jnp.broadcast_to(norms, (GROUPS, 128))


def query_kernel(query_ref, out_ref):
    query = query_ref[:, :MODEL].astype(F32)
    squares = lax.dot_general(
        jnp.ones((8, MODEL), F32), query * query, NT, precision=EXACT, preferred_element_type=F32
    )
    out_ref[0:8, :] = jnp.sqrt(squares + NORM_EPS)
    out_ref[8:16, :] = lax.dot_general(
        jnp.ones((8, 128), BF16), query_ref[:, MODEL:], NT, preferred_element_type=F32
    )


def loss_kernel(doc_ref, sums_ref, logits_ref, own_ref, query_ref, row_ref, w_ref, out_ref):
    sums = sums_ref[0]
    for n in range(1, DOCS):
        sums = sums + sums_ref[n]
    total = jnp.concatenate([sums[n : n + 1] for n in range(4)], axis=1)
    losses = jnp.log(sums[0:4]) - sums[4:8]
    loss = jnp.sum(jnp.sum(losses, axis=1, keepdims=True), axis=0, keepdims=True)
    query = query_ref[:, :MODEL]
    scale = RECIPROCAL_TEMP / row_ref[0:1, :]
    logits = logits_ref[...]
    group = doc_ref[0] * GROUPS + lax.broadcasted_iota(jnp.int32, logits.shape, 0)
    target = (group == row_ref[8:9, :].astype(jnp.int32)).astype(F32)
    weight = (jnp.exp(logits) / total - target) * (GRADIENT_FACTOR * scale)
    grad = folded(jnp.dot(stacked(weight), query, preferred_element_type=F32))
    own = own_ref[...]
    own_unit = own / jnp.sqrt(jnp.sum(own * own, axis=1, keepdims=True) + NORM_EPS)
    along = jnp.sum(own_unit * grad, axis=1, keepdims=True)
    spread = folded(
        lax.dot_general(stacked(grad), w_ref[...], NT, preferred_element_type=F32)
    )
    extra = jnp.where(lanes(GROUPS) < 64, along, loss)
    for z in range(PLANE):
        head = z // 2
        chunk = jnp.concatenate(
            [
                spread[:, head * HEAD_DIM : (head + 1) * HEAD_DIM],
                grad[:, z * HALF : (z + 1) * HALF],
            ],
            axis=1,
        )
        out_ref[z, 0:8, :] = chunk
        out_ref[z, 8:16, :] = extra


def mass_kernel(
    place_ref, lens_ref, own_ref, all_ref, means_ref, mass_ref, lse_ref, y_ref, k_s, member_s
):
    mine = own_ref[:, 0:64, :].reshape(QUARTER, 128)
    k_s[...] = jnp.where(lanes(QUARTER) < 64, mine, jnp.zeros_like(mine))
    for n in range(4):
        queries = halves(all_ref[n, :, 64:96, :]).reshape(QUARTER, HEAD_DIM)
        y_ref[n * QUARTER : (n + 1) * QUARTER, :] = jnp.concatenate(
            [queries, jnp.zeros_like(queries)], axis=1
        )
        both = means_ref[2 * place_ref[2] + n % 2]
        lse = jnp.where(place_ref[0] == n // 2, both[8:16], both[16:24])
        for part in range(8):
            at = n * QUARTER + part * 128
            lse_ref[:, at : at + 128] = jnp.broadcast_to(lse[part : part + 1, :], (8, 128))
        member = quarter_member(lens_ref, n // 2, n % 2)
        padded = jnp.concatenate([member, jnp.zeros((120, QUARTER), F32)], axis=0)
        member_s[:, n * QUARTER : (n + 1) * QUARTER] = padded.astype(BF16)

    def block(i, carry):
        rows = pl.ds(pl.multiple_of(i * BLOCK, BLOCK), BLOCK)
        sums = jnp.zeros((BLOCK, 128), F32)
        for n in range(4):
            cols = slice(n * QUARTER, (n + 1) * QUARTER)
            scores = lax.dot_general(k_s[rows, :], y_ref[cols, :], NT, preferred_element_type=F32)
            prob = jnp.exp(scores - lse_ref[0:1, cols]).astype(BF16)
            sums = sums + lax.dot_general(
                prob, member_s[:, cols], NT, preferred_element_type=F32
            )
        for part in range(PARTS):
            mass_ref[i * PARTS + part] = jnp.transpose(sums[part * 128 : (part + 1) * 128])[0:8, :]
        return carry

    lax.fori_loop(0, QUARTER // BLOCK, block, 0)


def rows_of(line):
    return jnp.concatenate([line[:, n : n + 128] for n in range(0, QUARTER, 128)], axis=0)


def group_kernel(
    place_ref, lens_ref, terms_ref, ready_ref, mass_ref, spare_ref, other_ref,
    dattn_ref, grad_ref, loss_ref, delta_ref,
):
    sums = terms_ref[0]
    for n in range(1, PLANE):
        sums = sums + terms_ref[n]
    along = sums[8:16, 0:1]
    loss_ref[...] = sums[8:16, :] / QUERY_COUNT
    norms = ready_ref[16:24, :]
    raw = jnp.concatenate([sums[0:8, 0:64], sums[0:8, 0:64]], axis=1)
    dattn = (raw - ready_ref[0:8, :] * along) / norms / lengths_of(lens_ref)
    dattn_ref[...] = dattn
    lane = lanes(GROUPS)
    ends = [
        jnp.where(lane < 64, dattn, 0.0).astype(BF16),
        jnp.where(lane < 64, 0.0, dattn).astype(BF16),
    ]
    for n, (attn, plane) in enumerate(
        ((spare_ref, place_ref[0]), (other_ref, 1 - place_ref[0]))
    ):
        products = jnp.concatenate(
            [lax.dot_general(part, attn[...], NT, preferred_element_type=F32) for part in ends],
            axis=1,
        )
        member = quarter_member(lens_ref, plane, place_ref[1])
        delta_ref[n * 8 : (n + 1) * 8, :] = rows_of(
            jnp.sum(products * member, axis=0, keepdims=True)
        )
    grad = (sums[0:8, 64:128] - ready_ref[8:16, 0:64] * along) / norms[:, 0:64]
    for z in range(PLANE):
        half = (z % 2) * HALF
        grad_ref[z] = jnp.concatenate([grad, mass_ref[z // 2, :, half : half + HALF]], axis=1)


def inputs_kernel(place_ref, lens_ref, parts_ref, means_ref, grad_inputs_ref, out_ref):
    grad = jnp.concatenate([parts_ref[z, :, 0:64] for z in range(PLANE)], axis=1)
    mine = local_member(lens_ref, place_ref[3])
    members = jnp.concatenate([mine, mine, mine, mine], axis=0).astype(BF16)
    grad_inputs_ref[...] = lax.dot_general(
        members, stacked(grad / lengths_of(lens_ref)[:, 0:1]), TN, preferred_element_type=F32
    ).astype(BF16)
    both = jnp.concatenate([grad, means_ref[...]], axis=1)
    wide = (MODEL + WIDTH) // 2
    both = jnp.concatenate([both[:, :wide], both[:, wide:]], axis=0)
    out_ref[...] = jnp.broadcast_to(both.astype(BF16)[None], (DOCS, 2 * GROUPS, wide))


def value_kernel(lens_ref, parts_ref, w_ref, grad_v_ref):
    grad = jnp.concatenate([parts_ref[z, :, 0:64] for z in range(PLANE)], axis=1)
    grad = grad / lengths_of(lens_ref)[:, 0:1]
    dattn = folded(lax.dot_general(stacked(grad), w_ref[...], NT, preferred_element_type=F32))
    dattn = dattn.astype(BF16).astype(F32)
    dattn = jnp.concatenate([dattn, dattn, dattn, jnp.zeros_like(dattn)], axis=0).astype(BF16)
    for pair in range(HEAD_COUNT // 2):
        cols = slice(pair * 128, (pair + 1) * 128)
        both = []
        for head in (2 * pair, 2 * pair + 1):
            mass = jnp.concatenate(
                [parts_ref[2 * head, :, 64:128], parts_ref[2 * head + 1, :, 64:128]], axis=1
            )
            both.append(
                lax.dot_general(stacked(mass), dattn[:, cols], TN, preferred_element_type=F32)
            )
        grad_v_ref[:, cols] = jnp.where(lanes(ROWS) < 64, both[0], both[1]).astype(BF16)


def weight_kernel(in_ref, out_ref):
    wide = (MODEL + WIDTH) // 2
    both = in_ref[...].astype(F32)
    both = [both[:, n : n + 8].reshape(DOCS * GROUPS, wide) for n in (0, 8)]
    both = jnp.concatenate(both, axis=1).astype(BF16)
    out_ref[...] = lax.dot_general(
        both[:, MODEL:], both[:, :MODEL], TN, preferred_element_type=F32
    )


def row_kernel(
    place_ref, lens_ref, own_ref, all_ref, lse_ref, delta_ref, dattn_ref,
    out_ref, x_ref, q_s, d_s, delta_s, lse_s,
):
    fill(all_ref, x_ref)
    q_s[...] = own_queries(own_ref)
    member = quarter_member(lens_ref, place_ref[0], place_ref[1]).astype(BF16)
    spread = lax.dot_general(
        member, dattn_ref[...].astype(BF16), TN, preferred_element_type=F32
    )
    d_s[...] = jnp.where(lanes(QUARTER) < 64, 0.0, spread).astype(BF16)
    delta_s[...] = turned(delta_ref[0:8, :])
    lse_s[...] = turned(lse_ref[...])

    def block(i, carry):
        rows = pl.ds(pl.multiple_of(i * TALL, TALL), TALL)
        log_total, delta = lse_s[rows, 0:1], delta_s[rows, 0:1]
        total = jnp.zeros((TALL, 128), F32)
        for n in range(KEYS // CHUNK):
            part = x_ref[n * CHUNK : (n + 1) * CHUNK, :]
            scores = lax.dot_general(q_s[rows, :], part, NT, preferred_element_type=F32)
            prob_grad = lax.dot_general(d_s[rows, :], part, NT, preferred_element_type=F32)
            score_grad = (jnp.exp(scores - log_total) * (prob_grad - delta)).astype(BF16)
            total = total + jnp.dot(score_grad, part, preferred_element_type=F32)
        total = total * SCALE
        out_ref[rows, :] = jnp.concatenate([total[:, 0:64]] * 2, axis=1).astype(BF16)
        return carry

    lax.fori_loop(0, QUARTER // TALL, block, 0)


def column_kernel(
    place_ref, lens_ref, own_ref, y_ref, mine_ref, other_ref, lse_ref, dattn_ref, grad_q_ref,
    out_ref, y_s, k_s, v_s, delta_s,
):
    lane = lanes(QUARTER)
    mine = own_ref[:, 0:64, :].reshape(QUARTER, 128)
    zero = jnp.zeros_like(mine)
    k_s[...] = jnp.where(lane < 64, mine, zero)
    v_s[...] = jnp.where(lane < 64, zero, mine)
    dattn = jnp.where(lanes(GROUPS) < 64, 0.0, dattn_ref[...]).astype(BF16)
    for n in range(4):
        rows = slice(n * QUARTER, (n + 1) * QUARTER)
        member = quarter_member(lens_ref, n // 2, n % 2)
        spread = lax.dot_general(member.astype(BF16), dattn, TN, preferred_element_type=F32)
        y_s[rows, :] = jnp.where(lane < 64, y_ref[rows, :], spread.astype(BF16))
        delta = jnp.where(place_ref[1] == n % 2, mine_ref[...], other_ref[...])
        delta = jnp.where(place_ref[0] == n // 2, delta[0:8], delta[8:16])
        for part in range(8):
            at = n * QUARTER + part * 128
            delta_s[:, at : at + 128] = jnp.broadcast_to(delta[part : part + 1, :], (8, 128))

    def block(i, carry):
        rows = pl.ds(pl.multiple_of(i * TALL, TALL), TALL)
        total = jnp.zeros((TALL, 128), F32)
        for n in range(KEYS // CHUNK):
            cols = slice(n * CHUNK, (n + 1) * CHUNK)
            part = y_s[cols, :]
            scores = lax.dot_general(k_s[rows, :], part, NT, preferred_element_type=F32)
            prob_grad = lax.dot_general(v_s[rows, :], part, NT, preferred_element_type=F32)
            score_grad = (
                jnp.exp(scores - lse_ref[0:1, cols]) * (prob_grad - delta_s[0:1, cols])
            ).astype(BF16)
            total = total + jnp.dot(score_grad, part, preferred_element_type=F32)
        both = jnp.where(lanes(TALL) < 64, total.astype(BF16), grad_q_ref[rows, :])
        count = TALL // HALF
        out_ref[pl.ds(i * count, count), :, :] = both.reshape(count, HALF, 128)
        return carry

    lax.fori_loop(0, QUARTER // TALL, block, 0)


SMEM = pl.BlockSpec(memory_space=pltpu.SMEM)
VMEM = pl.BlockSpec(memory_space=pltpu.VMEM)


def call(kernel, outs, scalars, arrays, scratch, estimate, name):
    return pl.pallas_call(
        kernel,
        out_shape=outs,
        in_specs=[SMEM] * len(scalars) + [VMEM] * len(arrays),
        out_specs=jax.tree.map(lambda _: VMEM, outs),
        scratch_shapes=scratch,
        compiler_params=params(56 if name == "pack" else 40 if scratch else 12),
        cost_estimate=estimate,
        name=name,
    )(*scalars, *arrays)


def shape(dims, dtype):
    return jax.ShapeDtypeStruct(dims, dtype)


def body(inputs, q_heads, k_heads, v_heads, w_out, group_lens, query_emb, positive):
    plane = lax.axis_index("yl")
    half = lax.axis_index("zd")
    head = lax.axis_index(HEADS)
    first = lax.axis_index(SEQ) * ROWS
    doc = lax.axis_index(GRP).reshape(1).astype(jnp.int32)
    place = jnp.stack([plane, half, head, first]).astype(jnp.int32)
    lengths = group_lens[0]
    exchange = functools.partial(lax.all_to_all, split_axis=0, concat_axis=0)
    barrier = lax.optimization_barrier
    pairs = QUARTER * KEYS

    packed = call(
        pack_kernel, shape((PLANE, 112, 128), BF16), (place, lengths),
        (q_heads[0], k_heads[0], v_heads[0], inputs[0]), (), cost(0, 1000000), "pack",
    )
    packed, query_emb, positive = barrier((packed, query_emb, positive))
    tagged = jnp.concatenate(
        [query_emb, jnp.pad(positive.astype(BF16)[:, None], ((0, 0), (0, 127)))], axis=1
    )
    own = exchange(packed, ZED)
    queries = gather(tagged, ("yh", "yl", "xa"))
    own, queries = barrier((own, queries))
    keys = share(own[:, 0:96, :], SQUARE)
    queries = gather(queries, ("xb", "co"))
    own, keys, queries = barrier((own, keys, queries))

    spare, lse, means = call(
        forward_kernel,
        (
            shape((SPARE, 128), BF16),
            shape((8, 128), F32),
            shape((2 * GROUPS, 128), F32),
        ),
        (place, lengths), (own, keys),
        [
            pltpu.VMEM((KEYS, 128), BF16),
            pltpu.VMEM((QUARTER, 128), BF16),
            pltpu.VMEM((QUARTER, 128), BF16),
        ],
        cost(pairs * 256 * 4, 3000000, pairs), "forward",
    )
    other_means = swap(means, ("yl",), 1)
    means = call(
        plane_kernel, shape((PLANE, 3 * GROUPS, 128), F32), (), (means, other_means), (),
        cost(0, 200000), "plane",
    )
    spare, means, queries = barrier((spare, means, queries))
    means = exchange(means, ZED)
    other_spare = swap(spare, ("yl",), 1)
    query_rows = call(
        query_kernel, shape((16, HELD), F32), (), (queries,), (), cost(6 * 2 * 8 * HELD * 1024, 1200000),
        "queries",
    )
    means, other_spare, query_rows = barrier((means, other_spare, query_rows))
    pooled_own, doc_means, logits, sums = call(
        pool_kernel,
        (
            shape((GROUPS, MODEL), F32),
            shape((GROUPS, WIDTH), F32),
            shape((GROUPS, HELD), F32),
            shape((DOCS, 8, 128), F32),
        ),
        (doc,), (means, w_out, queries, query_rows), (), cost(2 * 32 * 768 * 1024, 1800000), "pool",
    )
    sums = exchange(sums, GRP)
    ready = call(
        prepare_kernel, shape((24, 128), F32), (place,), (pooled_own, w_out), (),
        cost(2 * 32 * 128 * 1024, 1200000), "prepare",
    )
    sums, ready = barrier((sums, ready))
    terms = call(
        loss_kernel, shape((PLANE, 16, 128), F32), (doc,),
        (sums, logits, pooled_own, queries, query_rows, w_out), (),
        cost(2 * 32 * 768 * 1024, 1800000, 2000), "loss",
    )
    terms, own, keys = barrier((terms, own, keys))
    terms = exchange(terms, ZED)
    mass, lse_rows, columns = call(
        mass_kernel,
        (shape((GROUPS, 8, 128), F32), shape((8, KEYS), F32), shape((KEYS, 128), BF16)),
        (place, lengths), (own, keys, means),
        [pltpu.VMEM((QUARTER, 128), BF16), pltpu.VMEM((128, KEYS), BF16)],
        cost(pairs * 256 * 4, 2500000, pairs), "mass",
    )
    terms, mass, lse_rows = barrier((terms, mass, lse_rows))

    dattn, grad_part, loss, delta = call(
        group_kernel,
        (
            shape((GROUPS, 128), F32),
            shape((PLANE, GROUPS, 128), F32),
            shape((GROUPS, 128), F32),
            shape((2 * GROUPS, 128), F32),
        ),
        (place, lengths), (terms, ready, mass, spare, other_spare), (), cost(0, 100000), "group",
    )
    mean_loss = loss[0, 64]
    grad_parts = exchange(grad_part, ZED)
    other_delta = swap(delta, ("zd",), 1)
    grad_rows = call(
        row_kernel, shape((QUARTER, 128), BF16), (place, lengths), (own, keys, lse, delta, dattn),
        [
            pltpu.VMEM((KEYS, 128), BF16),
            pltpu.VMEM((QUARTER, 128), BF16),
            pltpu.VMEM((QUARTER, 128), BF16),
            pltpu.VMEM((QUARTER, 128), F32),
            pltpu.VMEM((QUARTER, 128), F32),
        ],
        cost(pairs * 256 * 6, 2000000, pairs), "rows",
    )
    grad_inputs, grads = call(
        inputs_kernel,
        (shape((ROWS, MODEL), BF16), shape((DOCS, 2 * GROUPS, (MODEL + WIDTH) // 2), BF16)),
        (place, lengths), (grad_parts, doc_means), (), cost(2 * 32 * 128 * 1024, 1200000), "inputs",
    )
    grad_rows, grads, other_delta = barrier((grad_rows, grads, other_delta))
    all_grads = exchange(grads, GRP)
    packed_grads = call(
        column_kernel, shape((PLANE, HALF, 128), BF16), (place, lengths),
        (own, columns, delta, other_delta, lse_rows, dattn, grad_rows),
        [
            pltpu.VMEM((KEYS, 128), BF16),
            pltpu.VMEM((QUARTER, 128), BF16),
            pltpu.VMEM((QUARTER, 128), BF16),
            pltpu.VMEM((8, KEYS), F32),
        ],
        cost(pairs * 256 * 6, 2500000, pairs), "columns",
    )
    packed_grads, grad_parts = barrier((packed_grads, grad_parts))
    home = exchange(packed_grads, ZED)
    out = shape((ROWS, WIDTH), BF16)
    grad_v = call(
        value_kernel, out, (lengths,), (grad_parts, w_out), (), cost(2 * 32 * 512 * 1024, 1300000),
        "values",
    )
    grad_w_out = call(
        weight_kernel, shape((WIDTH, MODEL), F32), (), (all_grads,), (),
        cost(2 * 384 * 512 * 1024, 3000000), "weights",
    )
    grad_q, grad_k = call(
        unpack_kernel, (out, out), (), (home,), (), cost(0, 500000), "unpack"
    )
    return (mean_loss, grad_inputs[None], grad_q[None], grad_k[None], grad_v[None], grad_w_out)


def solution(mesh):
    fine = Mesh(mesh.devices.reshape((2,) * 9), GRP + SEQ)
    rows = P(GRP, SEQ, None)
    return jax.shard_map(
        body,
        mesh=fine,
        in_specs=(
            rows,
            rows,
            rows,
            rows,
            P(),
            P(GRP, None),
            P(GRP + SEQ, None),
            P(GRP + SEQ),
        ),
        out_specs=(P(), rows, rows, rows, rows, P()),
        check_vma=False,
    )
```
